32 devices in a mesh: clip: 8 (over z, x), sp: 4 (over y, core).
Axes of the slice: x: 2, y: 2, z: 4, core: 2. Of those that a mesh axis runs over, the one named last changes fastest.
Arguments:
- features: bfloat16 [32, 4, 28, 28, 1024], P('clip', None, 'sp'), may hold values from -12 to 12
- strides: int32 [32], replicated, may hold values from 1 to 4, as said below
- cotangent: bfloat16 [32, 4, 28, 28, 1024], P('clip', None, 'sp'), may hold values from -6 to 6
- w_reduce: bfloat16 [2, 1024, 256], P(None, ('clip', 'sp')), may hold values from -0.1875 to 0.1875
- w_mix: bfloat16 [2, 256, 256], P(None, ('clip', 'sp')), may hold values from -0.375 to 0.375
- w_expand: bfloat16 [2, 256, 1024], P(None, ('clip', 'sp')), may hold values from -0.375 to 0.375
- w_depth: bfloat16 [2, 27, 256], P(None, None, ('clip', 'sp')), may hold values from -1.25 to 1.25
- gains_mid: bfloat16 [2, 2, 256], P(None, None, ('clip', 'sp')), may hold values from 0.25 to 1.75
- biases_mid: bfloat16 [2, 2, 256], P(None, None, ('clip', 'sp')), may hold values from -2 to 2
- gains_out: bfloat16 [2, 1024], P(None, ('clip', 'sp')), may hold values from 0.25 to 1.75
- biases_out: bfloat16 [2, 1024], P(None, ('clip', 'sp')), may hold values from -2 to 2
Outputs:
- output: bfloat16 [32, 4, 28, 28, 1024], P('clip', None, 'sp')
- input_grad: bfloat16 [32, 4, 28, 28, 1024], P('clip', None, 'sp')
- grad_reduce: float32 [2, 1024, 256], P(None, ('clip', 'sp'))
- grad_mix: float32 [2, 256, 256], P(None, ('clip', 'sp'))
- grad_expand: float32 [2, 256, 1024], P(None, ('clip', 'sp'))
- grad_depth: float32 [2, 27, 256], P(None, None, ('clip', 'sp'))
- grad_gains_mid: float32 [2, 2, 256], P(None, None, ('clip', 'sp'))
- grad_biases_mid: float32 [2, 2, 256], P(None, None, ('clip', 'sp'))
- grad_gains_out: float32 [2, 1024], P(None, ('clip', 'sp'))
- grad_biases_out: float32 [2, 1024], P(None, ('clip', 'sp'))
The draws below stay inside these ranges and needn't reach their ends.
Inputs may be any that keep to these rules, and one draw needn't show every extreme that they name: `strides`: each clip's stride is 1, 2 or 4, and it has 4 // stride valid frames; some clip has stride 1 and some stride 4.
All inputs are finite; a program needn't handle non-finite values.
Results may differ from the reference program's by a relative error of at most 0.02.
Values may be sent and summed in bfloat16 or wider, within the bound.
No kernel may reach another device: no remote copies, remote signals or barrier semaphores. Data moves between devices by JAX's collectives and lax.ppermute only.
A program may use at most 256 MiB of HBM per device.

```python
import jax
import jax.numpy as jnp
from jax import lax

C = 1024
B = 256
FRAMES = 4
COLS = 28
CLIPS = 32
ROWS = 28


def draw_strides(key, part):
    key = jax.random.fold_in(key, 5)
    level_key, order_key = jax.random.split(key)
    levels = jax.random.randint(level_key, (CLIPS,), 0, 3)
    order = jax.random.permutation(order_key, CLIPS)
    levels = levels.at[order[0]].set(0).at[order[1]].set(2)
    return jnp.where(levels == 0, 1, jnp.where(levels == 1, 2, 4)).astype(jnp.int32)


def draw_features(key, part):
    key = jax.random.fold_in(key, 11)
    value_key, clip_key = jax.random.split(key, 2)
    full_shape = (CLIPS, FRAMES, ROWS, COLS, C)
    clip_ramp = jnp.arange(CLIPS, dtype=jnp.float32) / max(CLIPS - 1, 1)
    clip_scale = 0.6 * jnp.exp(clip_ramp * jnp.log(3.0) + jax.random.uniform(clip_key, (CLIPS,), minval=-0.2, maxval=0.2))
    values = jnp.clip(jax.random.normal(value_key, full_shape), -6.0, 6.0)
    values = values * clip_scale[:, None, None, None, None]
    return jnp.clip(values, -12.0, 12.0).astype(jnp.bfloat16)


def steps_of(stream_key, dims, cuts, least, top_value):
    level, own = 1.0, jax.random.fold_in(stream_key, 6)
    for axis_at, blocks in cuts:
        steps = jnp.exp(jax.random.uniform(jax.random.fold_in(own, axis_at), (blocks,), jnp.float32, least / len(cuts), top_value / len(cuts)))
        level = level * jnp.repeat(steps, dims[axis_at] // blocks).reshape([-1 if axis == axis_at else 1 for axis in range(len(dims))])
    return level


def gaussian(own_key, dims, scale, most, cuts=(), kind=jnp.bfloat16):
    drawn = scale * jax.random.normal(own_key, dims, jnp.float32)
    if cuts:
        drawn = drawn * steps_of(own_key, dims, cuts, -0.22, 0.18)
    return jnp.clip(drawn, -most, most).astype(kind)


def setup_inputs(seed: int = 0) -> dict:
    keys = jax.random.split(jax.random.key(seed), 12)
    return {
        "features": draw_features(jax.random.fold_in(keys[11], 71), 0),
        "strides": draw_strides(jax.random.fold_in(keys[11], 71), 0),
        "cotangent": gaussian(keys[2], (CLIPS, FRAMES, ROWS, COLS, C), 1.0, 6.0, ((0, 8), (2, 4))),
        "w_reduce": gaussian(keys[3], (2, C, B), C ** -0.5, 0.1875, ((1, 32),)),
        "w_mix": gaussian(keys[4], (2, B, B), B ** -0.5, 0.375, ((1, 32),)),
        "w_expand": gaussian(keys[5], (2, B, C), B ** -0.5, 0.375, ((1, 32),)),
        "w_depth": gaussian(keys[6], (2, 27, B), 27 ** -0.5, 1.25, ((2, 32),)),
        "gains_mid": jnp.clip(1.0 + 0.15 * jax.random.normal(keys[7], (2, 2, B), jnp.float32), 0.25, 1.75).astype(jnp.bfloat16),
        "biases_mid": gaussian(keys[8], (2, 2, B), 0.3, 2.0, ((2, 32),)),
        "gains_out": jnp.clip(1.0 + 0.15 * jax.random.normal(keys[9], (2, C), jnp.float32), 0.25, 1.75).astype(jnp.bfloat16),
        "biases_out": gaussian(keys[10], (2, C), 0.3, 2.0, ((1, 32),)),
    }


@jax.custom_vjp
def low(v):
    return lax.optimization_barrier(v.astype(jnp.bfloat16)).astype(jnp.float32)

@jax.custom_vjp
def low_back(v):
    return v

def low_keep(v):
    return (low(v), None)

def low_pass(kept, grad):
    return (grad,)

def back_keep(v):
    return (v, None)

def back_low(kept, grad):
    return (low(grad),)
low.defvjp(low_keep, low_pass)
low_back.defvjp(back_keep, back_low)
epsilon = 1e-05
highest = lax.Precision.HIGHEST

def project(left_side, right_side):
    return jnp.einsum('...i,ij->...j', left_side, right_side, precision=highest)

def normalize(source, valid_mask, voxel_count):
    mean_value = lax.optimization_barrier(jnp.sum(source * valid_mask, axis=(0, 1, 2, 3))) / voxel_count
    centered = source - mean_value
    variance = lax.optimization_barrier(jnp.sum(centered * centered * valid_mask, axis=(0, 1, 2, 3))) / voxel_count
    return centered * lax.rsqrt(variance + epsilon)

def depthwise(field, kernel):
    frames, row_count, columns = (field.shape[1], field.shape[2], field.shape[3])
    padded = jnp.pad(field, ((0, 0), (1, 1), (1, 1), (1, 1), (0, 0)))
    result = jnp.zeros_like(field)
    for offset in range(27):
        frame_step, row_step, column_step = (offset // 9, offset // 3 % 3, offset % 3)
        result = result + kernel[offset] * padded[:, frame_step:frame_step + frames, row_step:row_step + row_count, column_step:column_step + columns]
    return result

def bottleneck(block_input, w_reduce, w_mix, w_expand, w_depth, gains_mid, biases_mid, gains_out, biases_out, valid_mask, voxel_count):
    reduced = low_back(project(low(block_input), w_reduce))
    hidden_first = low(valid_mask * jax.nn.silu(gains_mid[0] * normalize(reduced, valid_mask, voxel_count) + biases_mid[0]))
    mixed_field = low_back(low(project(hidden_first, w_mix)))
    spatial = low_back(depthwise(mixed_field, w_depth))
    hidden_second = low(valid_mask * jax.nn.silu(gains_mid[1] * normalize(spatial, valid_mask, voxel_count) + biases_mid[1]))
    expanded = low_back(project(hidden_second, w_expand))
    branch_out = gains_out * normalize(expanded, valid_mask, voxel_count) + biases_out
    return valid_mask * jax.nn.silu(block_input + branch_out)

def reference(features, strides, cotangent, w_reduce, w_mix, w_expand, w_depth, gains_mid, biases_mid, gains_out, biases_out):
    frame_counts = FRAMES // strides
    valid_mask = (lax.broadcasted_iota(jnp.int32, (CLIPS, FRAMES), 1) < frame_counts[:, None]).astype(jnp.float32)[:, :, None, None, None]
    voxel_count = (jnp.sum(frame_counts) * (ROWS * COLS)).astype(jnp.float32)
    weights = tuple((member.astype(jnp.float32) for member in (w_reduce, w_mix, w_expand, w_depth, gains_mid, biases_mid, gains_out, biases_out)))
    saved_block = jax.checkpoint(bottleneck)

    def forward(block_input, *params):
        current = block_input
        for layer in range(2):
            picked = tuple((member[layer] for member in params))
            current = saved_block(current, *picked, valid_mask, voxel_count)
        return current
    output, pullback = jax.vjp(forward, features.astype(jnp.float32), *weights)
    grads = pullback(cotangent.astype(jnp.float32))
    return (output.astype(jnp.bfloat16), grads[0].astype(jnp.bfloat16), grads[1], grads[2], grads[3], grads[4], grads[5], grads[6], grads[7], grads[8])
```

```python
import functools

import jax
import jax.numpy as jnp
from jax import lax
from jax.experimental import pallas as pl
from jax.experimental.pallas import tpu as pltpu
from jax.sharding import Mesh, PartitionSpec as P

epsilon = 1e-05
F32 = jnp.float32
BF16 = jnp.bfloat16
LINE = 32


def dot_nn(left, right):
    return lax.dot_general(left, right, (((1,), (0,)), ((), ())), preferred_element_type=F32)


def dot_nt(left, right):
    return lax.dot_general(left, right, (((1,), (1,)), ((), ())), preferred_element_type=F32)


def dot_tn(left, right):
    return lax.dot_general(left, right, (((0,), (0,)), ((), ())), preferred_element_type=F32)


def dot_split(left, right):
    high = left.astype(BF16)
    rest = (left - high.astype(F32)).astype(BF16)
    return dot_nn(high, right) + dot_nn(rest, right)


def sigmoid(value):
    return 0.5 * jnp.tanh(0.5 * value) + 0.5


def fold(value):
    return jnp.sum(value.reshape(-1, 8, value.shape[-1]), axis=0)


def column_mask(columns):
    return lax.broadcasted_iota(jnp.int32, (LINE, 1), 0) < columns


def full(shape):
    return pl.BlockSpec(shape, lambda *_: (0,) * len(shape))


def smem():
    return pl.BlockSpec(memory_space=pltpu.SMEM)


def call(body, grid, in_specs, out_specs, out_shape, scratch, flops=0, moved=0):
    return pl.pallas_call(
        body,
        grid=grid,
        in_specs=in_specs,
        out_specs=out_specs,
        out_shape=out_shape,
        scratch_shapes=scratch,
        compiler_params=pltpu.CompilerParams(
            dimension_semantics=("arbitrary",) * len(grid), vmem_limit_bytes=58 * 2**20
        ),
    )


def merge_stats(means, squares, counts, total):
    mean = jnp.sum(means * counts, axis=0) / total
    away = means - mean[None]
    spread = jnp.sum(squares + counts * away * away, axis=0) / total
    return mean, lax.rsqrt(spread + epsilon)


def depth_tile(read, weights, frame, frames, flip):
    sums = [None, None, None]
    for a in range(3):
        other = frame + a - 1
        if other < 0 or other >= frames:
            continue
        for b in range(3):
            row = read(other, b).reshape(LINE // 8, 8, -1)
            for e in range(3):
                tap = 9 * a + 3 * b + e
                term = row * weights(26 - tap if flip else tap)[None]
                sums[e] = term if sums[e] is None else sums[e] + term
    first, middle, last = (one.reshape(LINE, -1) for one in sums)
    return pltpu.roll(first, 1, 0) + middle + pltpu.roll(last, LINE - 1, 0)


def first_kernel(dims, scal, nf, x_ref, w_ref, red_ref, up_ref, dn_ref, st_ref, xs, acc):
    frames, rows, columns, group = dims
    clip, part = pl.program_id(0), pl.program_id(1)

    @pl.when((clip == 0) & (part == 0))
    def _():
        xs[...] = jnp.zeros_like(xs)
        acc[...] = jnp.zeros_like(acc)

    for f in range(group):
        live = part * group + f < scal[clip]

        @pl.when(live)
        def _():
            for r in range(rows):
                xs[r, 0:columns, :] = x_ref[0, f, r]
            reduced_tail(dims, f, clip, part, xs, w_ref, red_ref, up_ref, dn_ref, acc)

        @pl.when(jnp.logical_not(live))
        def _():
            red_ref[0, f] = jnp.zeros_like(red_ref[0, f])
            up_ref[0, f] = jnp.zeros_like(up_ref[0, f])
            dn_ref[0, f] = jnp.zeros_like(dn_ref[0, f])

    finish_stats(nf, acc, st_ref)


def reduced_tail(dims, f, clip, part, xs, w_ref, red_ref, up_ref, dn_ref, acc):
    frames, rows, columns, group = dims
    red = dot_nn(xs[...].reshape(rows * LINE, -1), w_ref[...])
    red_ref[0, f] = red.reshape(rows, LINE, -1)
    up_ref[0, f] = red_ref[0, f, 0]
    dn_ref[0, f] = red_ref[0, f, rows - 1]

    if f == 0:

        @pl.when((clip == 0) & (part == 0))
        def _():
            acc[0:1, :] = jnp.sum(red, axis=0, keepdims=True) / (rows * columns)

    collect_stats(rows, columns, lambda r: red_ref[0, f, r], acc)


def collect_stats(rows, columns, read, acc):
    pivot = acc[0:1, :]
    mask = column_mask(columns)

    def one(r, carry):
        plain, square = carry
        away = jnp.where(mask, read(r) - pivot, 0.0)
        return plain + fold(away), square + fold(away * away)

    zero = jnp.zeros((8, acc.shape[1]), F32)
    plain, square = lax.fori_loop(0, rows, one, (zero, zero), unroll=True)
    acc[1:2, :] += jnp.sum(plain, axis=0, keepdims=True)
    acc[2:3, :] += jnp.sum(square, axis=0, keepdims=True)


def finish_stats(nf, acc, st_ref):
    plain, square = acc[1:2, :], acc[2:3, :]
    width = acc.shape[1]
    st_ref[:, 0:width] = acc[0:1, :] + plain * nf[2]
    st_ref[:, width:] = square - plain * plain * nf[2]


def mix_kernel(
    dims, layer, scal, nf, red_ref, up_ref, dn_ref, got_ref, cnt_ref, par_ref, w_ref,
    mix_ref, spa_ref, z_ref, u_ref, h_ref, st_ref, vec_ref, hs, ms, wb, acc,
):
    frames, rows, columns = dims
    clip, clips = pl.program_id(0), pl.num_programs(0)
    width = w_ref.shape[0]
    mask = column_mask(columns)

    @pl.when(clip == 0)
    def _():
        mean, inverse = merge_stats(
            got_ref[:, :, 0:width], got_ref[:, :, width:], cnt_ref[:, :, 0:1], nf[1]
        )
        gain = par_ref[54 + 2 * layer : 55 + 2 * layer, :]
        vec_ref[...] = jnp.zeros_like(vec_ref)
        vec_ref[0:1, :] = inverse
        vec_ref[1:2, :] = -mean * inverse
        vec_ref[2:3, :] = gain
        vec_ref[3:4, :] = par_ref[58 + 2 * layer : 59 + 2 * layer, :]
        vec_ref[4:5, :] = gain * inverse
        acc[...] = jnp.zeros_like(acc)
        hs[...] = jnp.zeros_like(hs)
        for tap in range(27):
            row = par_ref[27 * layer + tap : 27 * layer + tap + 1, :]
            wb[tap] = jnp.broadcast_to(row, (8, width))

    inverse, shift = vec_ref[0:1, :], vec_ref[1:2, :]
    gain, bias = vec_ref[2:3, :], vec_ref[3:4, :]

    def activate(value, keep):
        z = jnp.where(mask, value * inverse + shift, 0.0)
        y = z * gain + bias
        s = sigmoid(y)
        h = jnp.where(keep, y * s, 0.0)
        return z, s, h

    for f in range(frames):
        live = f < scal[clip]

        @pl.when(live)
        def _():
            _, _, h = activate(up_ref[0, f], mask & (scal[clips] > 0))
            hs[f, 0] = h.astype(BF16)
            _, _, h = activate(dn_ref[0, f], mask & (scal[clips + 1] > 0))
            hs[f, rows + 1] = h.astype(BF16)

            def one(r, _):
                z, s, h = activate(red_ref[0, f, r], mask)
                low = h.astype(BF16)
                hs[f, r + 1] = low
                h_ref[0, f, r] = low
                z_ref[0, f, r] = z.astype(BF16)
                u_ref[0, f, r] = jnp.where(mask, s + h * (1.0 - s), 0.0).astype(BF16)
                return 0

            lax.fori_loop(0, rows, one, 0)
            mixed = dot_nn(hs[f].reshape((rows + 2) * LINE, width), w_ref[...]).astype(BF16)
            mix_ref[0, f] = mixed.reshape(rows + 2, LINE, width)
            ms[f] = mixed.astype(F32).reshape(rows + 2, LINE, width)

        @pl.when(jnp.logical_not(live))
        def _():
            h_ref[0, f] = jnp.zeros_like(h_ref[0, f])
            z_ref[0, f] = jnp.zeros_like(z_ref[0, f])
            u_ref[0, f] = jnp.zeros_like(u_ref[0, f])
            mix_ref[0, f] = jnp.zeros_like(mix_ref[0, f])
            ms[f] = jnp.zeros_like(ms[f])

    for f in range(frames):
        live = f < scal[clip]

        @pl.when(live)
        def _():
            for half in range(width // 128):
                lanes = pl.ds(128 * half, 128)

                def one(r, _):
                    tile = depth_tile(
                        lambda t, b: ms[t, r + b, :, lanes],
                        lambda tap: wb[tap, :, lanes],
                        f, frames, False,
                    )
                    spa_ref[0, f, r, :, lanes] = tile
                    return 0

                lax.fori_loop(0, rows, one, 0)

            if f == 0:

                @pl.when(clip == 0)
                def _():
                    total = jnp.zeros((8, width), F32)
                    for r in range(rows):
                        total += fold(jnp.where(mask, spa_ref[0, f, r], 0.0))
                    acc[0:1, :] = jnp.sum(total, axis=0, keepdims=True) / (rows * columns)

            collect_stats(rows, columns, lambda r: spa_ref[0, f, r], acc)

        @pl.when(jnp.logical_not(live))
        def _():
            spa_ref[0, f] = jnp.zeros_like(spa_ref[0, f])

    finish_stats(nf, acc, st_ref)


def hidden_kernel(
    dims, layer, scal, nf, spa_ref, got_ref, cnt_ref, par_ref, w_ref,
    z_ref, u_ref, h_ref, up_ref, dn_ref, st_ref, gram_ref, vec_ref,
):
    frames, rows, columns = dims
    clip = pl.program_id(0)
    width = par_ref.shape[1]
    mask = column_mask(columns)

    @pl.when(clip == 0)
    def _():
        mean, inverse = merge_stats(
            got_ref[:, :, 0:width], got_ref[:, :, width:], cnt_ref[:, :, 0:1], nf[1]
        )
        gain = par_ref[55 + 2 * layer : 56 + 2 * layer, :]
        vec_ref[...] = jnp.zeros_like(vec_ref)
        vec_ref[0:1, :] = inverse
        vec_ref[1:2, :] = -mean * inverse
        vec_ref[2:3, :] = gain
        vec_ref[3:4, :] = par_ref[59 + 2 * layer : 60 + 2 * layer, :]
        vec_ref[4:5, :] = gain * inverse
        gram_ref[...] = jnp.zeros_like(gram_ref)

    inverse, shift = vec_ref[0:1, :], vec_ref[1:2, :]
    gain, bias = vec_ref[2:3, :], vec_ref[3:4, :]

    for f in range(frames):
        live = f < scal[clip]

        @pl.when(live)
        def _():
            def one(r, _):
                z = jnp.where(mask, spa_ref[0, f, r] * inverse + shift, 0.0)
                y = z * gain + bias
                s = sigmoid(y)
                h = y * s
                h_ref[0, f, r] = jnp.where(mask, h, 0.0).astype(BF16)
                z_ref[0, f, r] = z.astype(BF16)
                u_ref[0, f, r] = jnp.where(mask, s + h * (1.0 - s), 0.0).astype(BF16)
                return 0

            lax.fori_loop(0, rows, one, 0)
            low = h_ref[0, f].reshape(rows * LINE, width)
            gram_ref[0:width, :] += dot_tn(low, low)
            ones = jnp.ones((16, rows * LINE), BF16)
            gram_ref[width : width + 8, :] += dot_nn(ones, low)[0:8]

        @pl.when(jnp.logical_not(live))
        def _():
            h_ref[0, f] = jnp.zeros_like(h_ref[0, f])
            z_ref[0, f] = jnp.zeros_like(z_ref[0, f])
            u_ref[0, f] = jnp.zeros_like(u_ref[0, f])

        up_ref[0, f] = z_ref[0, f, 0]
        dn_ref[0, f] = z_ref[0, f, rows - 1]

    @pl.when(clip == pl.num_programs(0) - 1)
    def _():
        total = gram_ref[width : width + 1, :]
        across = jnp.broadcast_to(total, (width, width))
        centered = gram_ref[0:width, :] - across.T * across * nf[2]
        spread = dot_split(centered, w_ref[...]) * w_ref[...].astype(F32)
        st_ref[:, 0:width] = total
        st_ref[:, width:] = jnp.sum(spread, axis=0, keepdims=True)


def wide_norm(nf, got_ref, cnt_ref, rinv_ref, pout_ref, layer, w_ref, vec_ref):
    width = w_ref.shape[0]
    places = got_ref.shape[0]
    hidden_means = got_ref[:, 0, 0:width] * rinv_ref[:, 0:1]
    means = dot_split(hidden_means, w_ref[...])
    counts = cnt_ref[:, 0, 0:1]
    mean = jnp.sum(means * counts, axis=0, keepdims=True) / nf[1]
    away = means - mean
    spread = jnp.sum(got_ref[:, 0, width:] + counts * away * away, axis=0, keepdims=True) / nf[1]
    inverse = lax.rsqrt(spread + epsilon)
    scale = pout_ref[layer : layer + 1, :] * inverse
    vec_ref[...] = jnp.zeros_like(vec_ref)
    vec_ref[0:1, :] = scale
    vec_ref[1:2, :] = pout_ref[2 + layer : 3 + layer, :] - mean * scale
    vec_ref[2:3, :] = inverse
    vec_ref[3:4, :] = mean


def join_kernel(
    dims, scal, nf, x_ref, h_ref, got_ref, cnt_ref, rinv_ref, pout_ref, w3_ref, w1_ref,
    next_ref, du_ref, red_ref, up_ref, dn_ref, st_ref, vec_ref, es, xs, acc,
):
    frames, rows, columns, group = dims
    clip, part = pl.program_id(0), pl.program_id(1)
    wide = w1_ref.shape[0]

    @pl.when((clip == 0) & (part == 0))
    def _():
        wide_norm(nf, got_ref, cnt_ref, rinv_ref, pout_ref, 0, w3_ref, vec_ref)
        xs[...] = jnp.zeros_like(xs)
        acc[...] = jnp.zeros_like(acc)

    for f in range(group):
        live = part * group + f < scal[clip]

        @pl.when(live)
        def _():
            es[...] = dot_nn(h_ref[0, f].reshape(rows * LINE, -1), w3_ref[...]).reshape(es.shape)

            def one(r, _):
                for j in range(wide // 256):
                    lanes = pl.ds(256 * j, 256)
                    y = x_ref[0, f, r, :, lanes].astype(F32) + (
                        es[r, 0:columns, lanes] * vec_ref[0:1, lanes] + vec_ref[1:2, lanes]
                    )
                    s = sigmoid(y)
                    o = y * s
                    xs[r, 0:columns, lanes] = o.astype(BF16)
                    du_ref[0, f, r, :, lanes] = (s + o * (1.0 - s)).astype(BF16)
                return 0

            lax.fori_loop(0, rows, one, 0)
            next_ref[0, f] = xs[...]
            reduced_tail(dims, f, clip, part, xs, w1_ref, red_ref, up_ref, dn_ref, acc)

        @pl.when(jnp.logical_not(live))
        def _():
            next_ref[0, f] = jnp.zeros_like(next_ref[0, f])
            du_ref[0, f] = jnp.zeros_like(du_ref[0, f])
            red_ref[0, f] = jnp.zeros_like(red_ref[0, f])
            up_ref[0, f] = jnp.zeros_like(up_ref[0, f])
            dn_ref[0, f] = jnp.zeros_like(dn_ref[0, f])

    finish_stats(nf, acc, st_ref)


def wide_tail(f, rows, h_ref, gs, w3s, low_ref, t_ref, ones_rows):
    low = h_ref[0, f].reshape(rows * LINE, -1)
    grad = gs[...].reshape(rows * LINE, -1)
    width = low.shape[1]
    t_ref[0:width, :] += dot_tn(low, grad)
    t_ref[width : width + 8, :] += dot_nn(ones_rows, grad)[0:8]
    low_ref[0, f] = dot_nt(grad, w3s[...]).reshape(rows, LINE, width)


def wide_sums(w3_ref, t_ref, vec_ref, sum_ref):
    width, wide = w3_ref.shape
    plain = t_ref[width : width + 1, :]
    along = jnp.sum(w3_ref[...].astype(F32) * t_ref[0:width, :], axis=0, keepdims=True)
    sum_ref[:, 0:wide] = plain
    sum_ref[:, wide:] = (along - vec_ref[3:4, :] * plain) * vec_ref[2:3, :]


def out_kernel(
    dims, scal, nf, x_ref, h_ref, cot_ref, got_ref, cnt_ref, rinv_ref, pout_ref, w3_ref,
    out_ref, gs_ref, low_ref, t_ref, sum_ref, vec_ref, es, gs, w3s,
):
    frames, rows, columns, group = dims
    clip, part = pl.program_id(0), pl.program_id(1)
    width, wide = w3_ref.shape

    @pl.when((clip == 0) & (part == 0))
    def _():
        wide_norm(nf, got_ref, cnt_ref, rinv_ref, pout_ref, 1, w3_ref, vec_ref)
        gs[...] = jnp.zeros_like(gs)
        t_ref[...] = jnp.zeros_like(t_ref)
        w3s[...] = (w3_ref[...].astype(F32) * vec_ref[0:1, :]).astype(BF16)

    for f in range(group):
        live = part * group + f < scal[clip]

        @pl.when(live)
        def _():
            es[...] = dot_nn(h_ref[0, f].reshape(rows * LINE, -1), w3_ref[...]).reshape(es.shape)

            def one(r, _):
                for j in range(wide // 256):
                    lanes = pl.ds(256 * j, 256)
                    y = x_ref[0, f, r, 0:columns, lanes].astype(F32) + (
                        es[r, 0:columns, lanes] * vec_ref[0:1, lanes] + vec_ref[1:2, lanes]
                    )
                    s = sigmoid(y)
                    o = y * s
                    out_ref[0, f, r, :, lanes] = o.astype(BF16)
                    grad = cot_ref[0, f, r, :, lanes].astype(F32) * (s + o * (1.0 - s))
                    grad = grad.astype(BF16)
                    gs[r, 0:columns, lanes] = grad
                    gs_ref[0, f, r, :, lanes] = grad
                return 0

            lax.fori_loop(0, rows, one, 0)
            wide_tail(f, rows, h_ref, gs, w3s, low_ref, t_ref, jnp.ones((16, rows * LINE), BF16))

        @pl.when(jnp.logical_not(live))
        def _():
            out_ref[0, f] = jnp.zeros_like(out_ref[0, f])
            gs_ref[0, f] = jnp.zeros_like(gs_ref[0, f])
            low_ref[0, f] = jnp.zeros_like(low_ref[0, f])

    @pl.when((clip == pl.num_programs(0) - 1) & (part == pl.num_programs(1) - 1))
    def _():
        wide_sums(w3_ref, t_ref, vec_ref, sum_ref)


def expand_back_kernel(
    dims, scal, nf, low_ref, h_ref, z_ref, u_ref, got_ref, vec_ref, t_ref, gram_ref, w3_ref,
    go_ref, up_ref, dn_ref, sum_ref, ge_ref, tot_ref, ks, crow, hk, acc,
):
    frames, rows, columns = dims
    clip = pl.program_id(0)
    width, wide = w3_ref.shape

    @pl.when(clip == 0)
    def _():
        totals = jnp.sum(got_ref[...].astype(F32), axis=0)
        tot_ref[...] = totals
        plain, along = totals[:, 0:wide] * nf[3], totals[:, wide:] * nf[3]
        scale, inverse, mean = vec_ref[0:1, :], vec_ref[2:3, :], vec_ref[3:4, :]
        w3 = w3_ref[...]
        rise = scale * inverse * along
        flat = scale * plain - rise * mean
        ks[...] = dot_nt((w3.astype(F32) * rise).astype(BF16), w3).astype(BF16)
        flat_high = flat.astype(BF16)
        flat_rest = (flat - flat_high.astype(F32)).astype(BF16)
        spread = lambda one: jnp.broadcast_to(one, (16, wide))
        crow[...] = (dot_nt(spread(flat_high), w3) + dot_nt(spread(flat_rest), w3))[0:8]
        total = gram_ref[width : width + 1, :]
        column = jnp.broadcast_to(total, (128, width)).T[:, 0:1]
        cross = dot_split(gram_ref[0:width, :], w3)
        ge = t_ref[0:width, :] * scale - column * flat - cross * rise
        ge_ref[...] = ge.astype(BF16)
        acc[...] = jnp.zeros_like(acc)

    row = crow[0:1, :]
    for f in range(frames):
        live = f < scal[clip]

        @pl.when(live)
        def _():
            hk[...] = dot_nn(h_ref[0, f].reshape(rows * LINE, width), ks[...]).reshape(hk.shape)

            def one(r, carry):
                plain, along = carry
                grad = low_ref[0, f, r] - row - hk[r]
                grad = grad * u_ref[0, f, r].astype(F32)
                go_ref[0, f, r] = grad.astype(BF16)
                z = z_ref[0, f, r].astype(F32)
                return plain + fold(grad), along + fold(grad * z)

            zero = jnp.zeros((8, width), F32)
            plain, along = lax.fori_loop(0, rows, one, (zero, zero))
            acc[0:8, :] += plain
            acc[8:16, :] += along

        @pl.when(jnp.logical_not(live))
        def _():
            go_ref[0, f] = jnp.zeros_like(go_ref[0, f])

        up_ref[0, f] = go_ref[0, f, 0]
        dn_ref[0, f] = go_ref[0, f, rows - 1]

    sum_ref[:, 0:width] = jnp.sum(acc[0:8, :], axis=0, keepdims=True)
    sum_ref[:, width:] = jnp.sum(acc[8:16, :], axis=0, keepdims=True)


def norm_rows(nf, got_ref, vec_ref, tot_ref, rows3):
    width = vec_ref.shape[1]
    totals = jnp.sum(got_ref[...], axis=0)
    tot_ref[...] = totals
    rows3[0:1, :] = vec_ref[4:5, :]
    rows3[1:2, :] = totals[:, 0:width] * nf[3]
    rows3[2:3, :] = totals[:, width:] * nf[3]


def depth_back_kernel(
    dims, layer, scal, nf, go_ref, gup_ref, gdn_ref, z_ref, zup_ref, zdn_ref, got_ref, vec_ref,
    mix_ref, h_ref, z1_ref, u1_ref, par_ref, w_ref,
    go1_ref, sum_ref, gmix_ref, gdep_ref, tot_ref, gp, ms, gm, gh, wb, rows3, gd, acc,
):
    frames, rows, columns = dims
    clip, clips = pl.program_id(0), pl.num_programs(0)
    width = w_ref.shape[0]
    mask = column_mask(columns)

    @pl.when(clip == 0)
    def _():
        norm_rows(nf, got_ref, vec_ref, tot_ref, rows3)
        gmix_ref[...] = jnp.zeros_like(gmix_ref)
        gd[...] = jnp.zeros_like(gd)
        acc[...] = jnp.zeros_like(acc)
        for tap in range(27):
            row = par_ref[27 * layer + tap : 27 * layer + tap + 1, :]
            wb[tap] = jnp.broadcast_to(row, (8, width))

    gain, flat, rise = rows3[0:1, :], rows3[1:2, :], rows3[2:3, :]

    def normed(go, z, keep):
        value = gain * (go.astype(F32) - flat - z.astype(F32) * rise)
        return jnp.where(keep, value, 0.0).astype(BF16).astype(F32)

    for f in range(frames):
        live = f < scal[clip]

        @pl.when(live)
        def _():
            gp[f, 0] = normed(gup_ref[0, f], zup_ref[0, f], mask & (scal[clips] > 0))
            gp[f, rows + 1] = normed(gdn_ref[0, f], zdn_ref[0, f], mask & (scal[clips + 1] > 0))

            def one(r, _):
                gp[f, r + 1] = normed(go_ref[0, f, r], z_ref[0, f, r], mask)
                return 0

            lax.fori_loop(0, rows, one, 0)

            def two(r, _):
                ms[f, r] = mix_ref[0, f, r].astype(F32)
                return 0

            lax.fori_loop(0, rows + 2, two, 0)

        @pl.when(jnp.logical_not(live))
        def _():
            gp[f] = jnp.zeros_like(gp[f])
            ms[f] = jnp.zeros_like(ms[f])

    for f in range(frames):
        live = f < scal[clip]

        @pl.when(live)
        def _():
            for half in range(width // 128):
                lanes = pl.ds(128 * half, 128)

                def one(r, _):
                    tile = depth_tile(
                        lambda t, b: gp[t, r + b, :, lanes],
                        lambda tap: wb[tap, :, lanes],
                        f, frames, True,
                    )
                    gm[f, r, :, lanes] = jnp.where(mask, tile, 0.0).astype(BF16)
                    return 0

                lax.fori_loop(0, rows, one, 0)

                taps = [
                    9 * a + 3 * b + e
                    for a in range(3)
                    if 0 <= f + a - 1 < frames
                    for b in range(3)
                    for e in range(3)
                ]

                def two(r, carry):
                    own = gp[f, r + 1, :, lanes]
                    moved = [
                        pltpu.roll(own, LINE - 1, 0).reshape(-1, 8, 128),
                        own.reshape(-1, 8, 128),
                        pltpu.roll(own, 1, 0).reshape(-1, 8, 128),
                    ]
                    result = []
                    rows_read = {}
                    for tap, kept in zip(taps, carry):
                        a, b, e = tap // 9, tap // 3 % 3, tap % 3
                        if (a, b) not in rows_read:
                            rows_read[a, b] = ms[f + a - 1, r + b, :, lanes].reshape(-1, 8, 128)
                        result.append(kept + jnp.sum(moved[e] * rows_read[a, b], axis=0))
                    return tuple(result)

                start = tuple(gd[tap, :, lanes] for tap in taps)
                for tap, kept in zip(taps, lax.fori_loop(0, rows, two, start)):
                    gd[tap, :, lanes] = kept

            grad = gm[f].reshape(rows * LINE, width)
            gmix_ref[...] += dot_tn(h_ref[0, f].reshape(rows * LINE, width), grad)
            gh[...] = dot_nt(grad, w_ref[...]).reshape(gh.shape)

            def three(r, carry):
                plain, along = carry
                value = gh[r] * u1_ref[0, f, r].astype(F32)
                go1_ref[0, f, r] = value.astype(BF16)
                return plain + fold(value), along + fold(value * z1_ref[0, f, r].astype(F32))

            zero = jnp.zeros((8, width), F32)
            plain, along = lax.fori_loop(0, rows, three, (zero, zero))
            acc[0:8, :] += plain
            acc[8:16, :] += along

        @pl.when(jnp.logical_not(live))
        def _():
            go1_ref[0, f] = jnp.zeros_like(go1_ref[0, f])

    sum_ref[:, 0:width] = jnp.sum(acc[0:8, :], axis=0, keepdims=True)
    sum_ref[:, width:] = jnp.sum(acc[8:16, :], axis=0, keepdims=True)

    @pl.when(clip == pl.num_programs(0) - 1)
    def _():
        gdep_ref[...] = jnp.zeros_like(gdep_ref)
        for tap in range(27):
            gdep_ref[tap : tap + 1, :] = jnp.sum(gd[tap], axis=0, keepdims=True)


def reduced_grad(rows, columns, f, go_ref, z_ref, rows3, gr):
    gain, flat, rise = rows3[0:1, :], rows3[1:2, :], rows3[2:3, :]
    mask = column_mask(columns)

    def one(r, _):
        value = go_ref[0, f, r].astype(F32) - flat - z_ref[0, f, r].astype(F32) * rise
        gr[r] = jnp.where(mask, gain * value, 0.0).astype(BF16)
        return 0

    lax.fori_loop(0, rows, one, 0)


def cross_kernel(
    dims, scal, nf, go_ref, z_ref, got_ref, vec1_ref, x_ref, gs_ref, du_ref, h_ref,
    vec3_ref, w1_ref, w3_ref,
    gs0_ref, low_ref, t_ref, sum_ref, gred_ref, tot_ref, gr, ds, gs, w3s, rows3, gacc,
):
    frames, rows, columns, group = dims
    clip, part = pl.program_id(0), pl.program_id(1)
    width, wide = w3_ref.shape

    @pl.when((clip == 0) & (part == 0))
    def _():
        norm_rows(nf, got_ref, vec1_ref, tot_ref, rows3)
        gs[...] = jnp.zeros_like(gs)
        t_ref[...] = jnp.zeros_like(t_ref)
        gacc[...] = jnp.zeros_like(gacc)
        w3s[...] = (w3_ref[...].astype(F32) * vec3_ref[0:1, :]).astype(BF16)

    for f in range(group):
        live = part * group + f < scal[clip]

        @pl.when(live)
        def _():
            reduced_grad(rows, columns, f, go_ref, z_ref, rows3, gr)
            grad = gr[...].reshape(rows * LINE, width)
            gacc[...] += dot_tn(grad, x_ref[0, f].reshape(rows * LINE, wide))
            ds[...] = dot_nt(grad, w1_ref[...]).reshape(ds.shape)

            def one(r, _):
                for j in range(wide // 256):
                    lanes = pl.ds(256 * j, 256)
                    value = gs_ref[0, f, r, :, lanes].astype(F32) + ds[r, 0:columns, lanes]
                    value = (value * du_ref[0, f, r, :, lanes].astype(F32)).astype(BF16)
                    gs[r, 0:columns, lanes] = value
                    gs0_ref[0, f, r, :, lanes] = value
                return 0

            lax.fori_loop(0, rows, one, 0)
            wide_tail(f, rows, h_ref, gs, w3s, low_ref, t_ref, jnp.ones((16, rows * LINE), BF16))

        @pl.when(jnp.logical_not(live))
        def _():
            gs0_ref[0, f] = jnp.zeros_like(gs0_ref[0, f])
            low_ref[0, f] = jnp.zeros_like(low_ref[0, f])

    @pl.when((clip == pl.num_programs(0) - 1) & (part == pl.num_programs(1) - 1))
    def _():
        wide_sums(w3_ref, t_ref, vec3_ref, sum_ref)
        gred_ref[...] = gacc[...].T.astype(BF16)


def last_kernel(
    dims, scal, nf, go_ref, z_ref, got_ref, vec1_ref, x_ref, gs_ref, w1_ref,
    out_ref, gred_ref, tot_ref, gr, ds, xs, rows3, gacc,
):
    frames, rows, columns, group = dims
    clip, part = pl.program_id(0), pl.program_id(1)
    wide, width = w1_ref.shape

    @pl.when((clip == 0) & (part == 0))
    def _():
        norm_rows(nf, got_ref, vec1_ref, tot_ref, rows3)
        xs[...] = jnp.zeros_like(xs)
        gacc[...] = jnp.zeros_like(gacc)

    for f in range(group):
        live = part * group + f < scal[clip]

        @pl.when(live)
        def _():
            reduced_grad(rows, columns, f, go_ref, z_ref, rows3, gr)
            for r in range(rows):
                xs[r, 0:columns, :] = x_ref[0, f, r]
            grad = gr[...].reshape(rows * LINE, width)
            gacc[...] += dot_tn(grad, xs[...].reshape(rows * LINE, wide))
            ds[...] = dot_nt(grad, w1_ref[...]).reshape(ds.shape)

            def one(r, _):
                for j in range(wide // 256):
                    lanes = pl.ds(256 * j, 256)
                    value = gs_ref[0, f, r, :, lanes].astype(F32) + ds[r, 0:columns, lanes]
                    out_ref[0, f, r, :, lanes] = value.astype(BF16)
                return 0

            lax.fori_loop(0, rows, one, 0)

        @pl.when(jnp.logical_not(live))
        def _():
            out_ref[0, f] = jnp.zeros_like(out_ref[0, f])

    @pl.when((clip == pl.num_programs(0) - 1) & (part == pl.num_programs(1) - 1))
    def _():
        gred_ref[...] = gacc[...].T.astype(BF16)


ALL = ("clip", "outer", "inner")
CHIPS = ("clip", "outer")
SP = ("outer", "inner")


def share(row):
    peers = lax.axis_size(ALL)
    return lax.all_to_all(jnp.broadcast_to(row[None], (peers,) + row.shape), ALL, 0, 0)


def neighbours(from_top, from_bottom):
    peers = lax.axis_size(SP)
    down = [(i, i + 1) for i in range(peers - 1)]
    above = lax.ppermute(from_bottom, SP, down)
    below = lax.ppermute(from_top, SP, [(j, i) for i, j in down])
    return above, below


def swap(value):
    peers = lax.axis_size("inner")
    return lax.ppermute(value, "inner", [(i, (i + 1) % peers) for i in range(peers)])


def on_device(
    features, strides, cotangent, w_reduce, w_mix, w_expand, w_depth,
    gains_mid, biases_mid, gains_out, biases_out,
):
    clips, frames, rows, columns, wide = features.shape
    width = w_mix.shape[2]
    peers, chips = lax.axis_size(ALL), lax.axis_size(CHIPS)
    inner = lax.axis_size("inner")
    sp_size = lax.axis_size(SP)
    part, place = lax.axis_index("inner"), lax.axis_index(ALL)
    sp_at = lax.axis_index(SP)

    counts = frames // strides
    by_group = jnp.sum(counts.reshape(-1, clips), axis=1) * (rows * columns)
    by_device = jnp.repeat(by_group, sp_size).astype(F32)
    local = lax.dynamic_slice_in_dim(counts, lax.axis_index("clip") * clips, clips)
    edges = jnp.stack([sp_at > 0, sp_at < sp_size - 1]).astype(jnp.int32)
    scal = jnp.concatenate([local.astype(jnp.int32), edges])
    own = jnp.sum(local).astype(F32) * (rows * columns)
    total = jnp.sum(by_device)
    nf = jnp.stack([own, total, 1.0 / own, 1.0 / total])
    cnt = jnp.broadcast_to(by_device[:, None, None], (peers, 1, 128))
    rinv = jnp.broadcast_to(1.0 / by_device[:, None], (peers, 128))

    r1, r2 = w_reduce.shape[1], w_mix.shape[1]
    r4 = w_depth.shape[2]
    r5 = gains_out.shape[1] // r4
    small = jnp.concatenate(
        [
            w_depth.transpose(2, 0, 1).reshape(r4, -1),
            gains_mid.transpose(2, 0, 1).reshape(r4, -1),
            biases_mid.transpose(2, 0, 1).reshape(r4, -1),
            jnp.zeros((r4, 2), BF16),
            gains_out.reshape(2, r4, r5).transpose(1, 0, 2).reshape(r4, -1),
            biases_out.reshape(2, r4, r5).transpose(1, 0, 2).reshape(r4, -1),
        ],
        axis=1,
    )
    small = jnp.pad(small, ((0, 0), (0, width - small.shape[1])))
    wide_rows = w_expand.reshape(2, r2, wide // width, width).transpose(0, 2, 1, 3)
    packed = jnp.concatenate(
        [
            w_reduce.reshape(-1, width),
            w_mix.reshape(-1, width),
            wide_rows.reshape(-1, width),
            small,
        ],
        axis=0,
    )
    pad = -packed.shape[0] % 16
    packed = jnp.pad(packed, ((0, pad), (0, 0)))
    near = lax.all_to_all(jnp.broadcast_to(packed[None], (chips,) + packed.shape), CHIPS, 0, 0)
    held = [near]
    for _ in range(inner - 1):
        held.append(swap(held[-1]))
    everything = jnp.stack(
        [lax.select_n(lax.rem(part - c + inner, inner), *held) for c in range(inner)], axis=1
    )
    everything = everything.reshape((peers,) + packed.shape)

    w1, w2, w3 = [], [], []
    base = 0
    for layer in range(2):
        w1.append(everything[:, base + layer * r1 : base + (layer + 1) * r1].reshape(-1, width))
    base += 2 * r1
    for layer in range(2):
        w2.append(everything[:, base + layer * r2 : base + (layer + 1) * r2].reshape(-1, width))
    base += 2 * r2
    blocks = wide // width
    for layer in range(2):
        start = base + layer * r2 * blocks
        one = everything[:, start : start + r2 * blocks].reshape(peers, blocks, r2, width)
        w3.append(one.transpose(0, 2, 1, 3).reshape(peers * r2, wide))
    base += 2 * r2 * blocks
    small = everything[:, base : base + r4]
    par = small[:, :, 0:64].reshape(-1, 64).T.astype(F32)
    out_rows = small[:, :, 64 : 64 + 4 * r5].reshape(peers, r4, 4, r5)
    pout = out_rows.transpose(2, 0, 1, 3).reshape(4, wide).astype(F32)

    pad_field = (clips, frames, rows, LINE, width)
    narrow = lambda kind: jax.ShapeDtypeStruct(pad_field, kind)
    edge = lambda kind: jax.ShapeDtypeStruct((clips, frames, LINE, width), kind)
    flat = lambda *shape: jax.ShapeDtypeStruct(shape, F32)
    group = 2 if frames % 2 == 0 else 1
    dims3 = (frames, rows, columns)
    dims4 = (frames, rows, columns, group)
    grid2 = (clips, frames // group)

    def by_clip(*shape):
        return pl.BlockSpec((1,) + shape, lambda c: (c,) + (0,) * len(shape))

    def by_part(*shape):
        return pl.BlockSpec((1, group) + shape, lambda c, p: (c, p) + (0,) * len(shape))

    line = by_part(rows, LINE, width)
    edge_part = by_part(LINE, width)
    clip_field = by_clip(frames, rows, LINE, width)
    clip_tall = by_clip(frames, rows + 2, LINE, width)
    clip_edge = by_clip(frames, LINE, width)
    raw = by_part(rows, columns, wide)
    kept = by_part(rows, LINE, wide)
    raw_shape = jax.ShapeDtypeStruct((clips, frames, rows, columns, wide), BF16)
    kept_shape = jax.ShapeDtypeStruct((clips, frames, rows, LINE, wide), BF16)

    reduced, up, dn, stats = call(
        functools.partial(first_kernel, dims4), grid2,
        [smem(), smem(), raw, full((wide, width))],
        [line, edge_part, edge_part, full((1, 2 * width))],
        [narrow(F32), edge(F32), edge(F32), flat(1, 2 * width)],
        [pltpu.VMEM((rows, LINE, wide), BF16), pltpu.VMEM((8, width), F32)],
    )(scal, nf, features, w1[0])

    stored = []
    for layer in range(2):
        above, below = neighbours(up, dn)
        got = share(stats)
        mixed, spatial, z1, u1, h1, stats, vec1 = call(
            functools.partial(mix_kernel, dims3, layer), (clips,),
            [smem(), smem(), clip_field, clip_edge, clip_edge, full((peers, 1, 2 * width)),
             full((peers, 1, 128)), full((64, width)), full((width, width))],
            [clip_tall, clip_field, clip_field, clip_field, clip_field,
             full((1, 2 * width)), full((8, width))],
            [jax.ShapeDtypeStruct((clips, frames, rows + 2, LINE, width), BF16), narrow(F32),
             narrow(BF16), narrow(BF16), narrow(BF16), flat(1, 2 * width), flat(8, width)],
            [pltpu.VMEM((frames, rows + 2, LINE, width), BF16),
             pltpu.VMEM((frames, rows + 2, LINE, width), F32),
             pltpu.VMEM((27, 8, width), F32), pltpu.VMEM((8, width), F32)],
        )(scal, nf, reduced, above, below, got, cnt, par, w2[layer])
        got = share(stats)
        z2, u2, h2, zup, zdn, stats, gram, vec2 = call(
            functools.partial(hidden_kernel, dims3, layer), (clips,),
            [smem(), smem(), clip_field, full((peers, 1, 2 * width)), full((peers, 1, 128)),
             full((64, width)), full((width, wide))],
            [clip_field, clip_field, clip_field, clip_edge, clip_edge,
             full((1, width + wide)), full((width + 8, width)), full((8, width))],
            [narrow(BF16), narrow(BF16), narrow(BF16), edge(BF16), edge(BF16),
             flat(1, width + wide), flat(width + 8, width), flat(8, width)],
            [],
        )(scal, nf, spatial, got, cnt, par, w3[layer])
        z_halo = neighbours(zup, zdn)
        got = share(stats)
        norm_specs = [full((peers, 1, width + wide)), full((peers, 1, 128)), full((peers, 128)),
                      full((4, wide)), full((width, wide))]
        norm_args = (got, cnt, rinv, pout, w3[layer])
        if layer == 0:
            carried, slope, reduced, up, dn, stats, vec3 = call(
                functools.partial(join_kernel, dims4), grid2,
                [smem(), smem(), raw, line] + norm_specs + [full((wide, width))],
                [kept, raw, line, edge_part, edge_part, full((1, 2 * width)), full((8, wide))],
                [kept_shape, raw_shape, narrow(F32), edge(F32), edge(F32),
                 flat(1, 2 * width), flat(8, wide)],
                [pltpu.VMEM((rows, LINE, wide), F32), pltpu.VMEM((rows, LINE, wide), BF16),
                 pltpu.VMEM((8, width), F32)],
            )(scal, nf, features, h2, *norm_args, w1[1])
        else:
            output, gs, low, t, sums, vec3 = call(
                functools.partial(out_kernel, dims4), grid2,
                [smem(), smem(), kept, line, raw] + norm_specs,
                [raw, raw, line, full((width + 8, wide)), full((1, 2 * wide)), full((8, wide))],
                [raw_shape, raw_shape, narrow(F32), flat(width + 8, wide), flat(1, 2 * wide),
                 flat(8, wide)],
                [pltpu.VMEM((rows, LINE, wide), F32), pltpu.VMEM((rows, LINE, wide), BF16),
                 pltpu.VMEM((width, wide), BF16)],
            )(scal, nf, carried, h2, cotangent, *norm_args)
        stored.append((z1, u1, h1, vec1, mixed, z2, u2, h2, vec2, z_halo, gram, vec3))

    results = [None, None]
    for layer in (1, 0):
        z1, u1, h1, vec1, mixed, z2, u2, h2, vec2, z_halo, gram, vec3 = stored[layer]
        got = share(sums.astype(BF16))
        go2, gup, gdn, sums, g_expand, tot3 = call(
            functools.partial(expand_back_kernel, dims3), (clips,),
            [smem(), smem(), clip_field, clip_field, clip_field, clip_field,
             full((peers, 1, 2 * wide)), full((8, wide)), full((width + 8, wide)),
             full((width + 8, width)), full((width, wide))],
            [clip_field, clip_edge, clip_edge, full((1, 2 * width)), full((width, wide)),
             full((1, 2 * wide))],
            [narrow(BF16), edge(BF16), edge(BF16), flat(1, 2 * width),
             jax.ShapeDtypeStruct((width, wide), BF16), flat(1, 2 * wide)],
            [pltpu.VMEM((width, width), BF16), pltpu.VMEM((8, width), F32),
             pltpu.VMEM((rows, LINE, width), F32), pltpu.VMEM((16, width), F32)],
        )(scal, nf, low, h2, z2, u2, got, vec3, t, gram, w3[layer])
        above, below = neighbours(gup, gdn)
        got = share(sums)
        go1, sums, g_mix, g_depth, tot2 = call(
            functools.partial(depth_back_kernel, dims3, layer), (clips,),
            [smem(), smem(), clip_field, clip_edge, clip_edge, clip_field, clip_edge, clip_edge,
             full((peers, 1, 2 * width)), full((8, width)), clip_tall, clip_field, clip_field,
             clip_field, full((64, width)), full((width, width))],
            [clip_field, full((1, 2 * width)), full((width, width)), full((LINE, width)),
             full((1, 2 * width))],
            [narrow(BF16), flat(1, 2 * width), flat(width, width), flat(LINE, width),
             flat(1, 2 * width)],
            [pltpu.VMEM((frames, rows + 2, LINE, width), F32),
             pltpu.VMEM((frames, rows + 2, LINE, width), F32),
             pltpu.VMEM((frames, rows, LINE, width), BF16),
             pltpu.VMEM((rows, LINE, width), F32),
             pltpu.VMEM((27, 8, width), F32), pltpu.VMEM((8, width), F32),
             pltpu.VMEM((27, 8, width), F32), pltpu.VMEM((16, width), F32)],
        )(scal, nf, go2, above, below, z2, z_halo[0], z_halo[1], got, vec2, mixed, h1, z1, u1,
          par, w2[layer])
        got = share(sums)
        if layer == 1:
            _, _, _, _, _, _, _, h2_0, _, _, _, vec3_0 = stored[0]
            gs, low, t, sums, g_reduce, tot1 = call(
                functools.partial(cross_kernel, dims4), grid2,
                [smem(), smem(), line, line, full((peers, 1, 2 * width)), full((8, width)),
                 kept, raw, raw, line, full((8, wide)), full((wide, width)),
                 full((width, wide))],
                [raw, line, full((width + 8, wide)), full((1, 2 * wide)), full((wide, width)),
                 full((1, 2 * width))],
                [raw_shape, narrow(F32), flat(width + 8, wide), flat(1, 2 * wide),
                 jax.ShapeDtypeStruct((wide, width), BF16), flat(1, 2 * width)],
                [pltpu.VMEM((rows, LINE, width), BF16), pltpu.VMEM((rows, LINE, wide), F32),
                 pltpu.VMEM((rows, LINE, wide), BF16), pltpu.VMEM((width, wide), BF16),
                 pltpu.VMEM((8, width), F32), pltpu.VMEM((width, wide), F32)],
            )(scal, nf, go1, z1, got, vec1, carried, gs, slope, h2_0, vec3_0, w1[1],
              w3[0])
        else:
            input_grad, g_reduce, tot1 = call(
                functools.partial(last_kernel, dims4), grid2,
                [smem(), smem(), line, line, full((peers, 1, 2 * width)), full((8, width)),
                 raw, raw, full((wide, width))],
                [raw, full((wide, width)), full((1, 2 * width))],
                [raw_shape, jax.ShapeDtypeStruct((wide, width), BF16), flat(1, 2 * width)],
                [pltpu.VMEM((rows, LINE, width), BF16), pltpu.VMEM((rows, LINE, wide), F32),
                 pltpu.VMEM((rows, LINE, wide), BF16), pltpu.VMEM((8, width), F32),
                 pltpu.VMEM((width, wide), F32)],
            )(scal, nf, go1, z1, got, vec1, features, gs, w1[0])
        results[layer] = (g_reduce, g_mix, g_expand, g_depth, tot1, tot2, tot3)

    pieces = []
    for layer in range(2):
        g_reduce, g_mix, g_expand, g_depth = results[layer][0:4]
        pieces.append(g_reduce.reshape(peers, -1, width))
        pieces.append(g_mix.astype(BF16).reshape(peers, -1, width))
        one = g_expand.reshape(peers, r2, blocks, width).transpose(0, 2, 1, 3)
        pieces.append(one.reshape(peers, r2 * blocks, width))
        one = g_depth.astype(BF16).T.reshape(peers, r4, LINE)
        pieces.append(jnp.pad(one, ((0, 0), (0, 0), (0, width - LINE))))
    packed = jnp.concatenate(pieces, axis=1).reshape(chips, inner, -1, width)
    sent = lax.dynamic_index_in_dim(packed, lax.rem(part + 1, inner), 1, keepdims=False)
    mine = lax.dynamic_index_in_dim(packed, part, 1, keepdims=False).astype(F32)
    mine = mine + swap(sent).astype(F32)
    got = lax.all_to_all(mine.astype(BF16), CHIPS, 0, 0)
    got = jnp.sum(got.astype(F32), axis=0)
    grads = [[], [], [], []]
    at = 0
    for layer in range(2):
        grads[0].append(got[at : at + r1])
        at += r1
        grads[1].append(got[at : at + r2])
        at += r2
        one = got[at : at + r2 * blocks].reshape(blocks, r2, width)
        grads[2].append(one.transpose(1, 0, 2).reshape(r2, wide))
        at += r2 * blocks
        grads[3].append(got[at : at + r4, 0:27].T)
        at += r4

    def cut(row, size):
        return lax.dynamic_slice_in_dim(row, place * size, size, axis=1)

    mid_sums = jnp.concatenate(
        [
            jnp.concatenate([results[layer][4], results[layer][5]], axis=0).reshape(2, 2, width)
            for layer in range(2)
        ],
        axis=0,
    )
    mid = lax.dynamic_slice_in_dim(mid_sums, place * r4, r4, axis=2)
    out_sums = jnp.concatenate([results[layer][6].reshape(1, 2, wide) for layer in range(2)])
    r6 = gains_out.shape[1]
    outs = lax.dynamic_slice_in_dim(out_sums, place * r6, r6, axis=2)
    return (
        output,
        input_grad,
        jnp.stack(grads[0]),
        jnp.stack(grads[1]),
        jnp.stack(grads[2]),
        jnp.stack(grads[3]),
        mid[:, 1].reshape(2, 2, r4),
        mid[:, 0].reshape(2, 2, r4),
        outs[:, 1],
        outs[:, 0],
    )


def solution(mesh):
    clip_size, sp_size = mesh.shape["clip"], mesh.shape["sp"]
    inner = 2 if sp_size % 2 == 0 else 1
    split = Mesh(mesh.devices.reshape(clip_size, sp_size // inner, inner), ALL)
    return jax.shard_map(
        on_device,
        mesh=split,
        in_specs=(
            P("clip", None, SP, None, None),
            P(),
            P("clip", None, SP, None, None),
            P(None, ALL, None),
            P(None, ALL, None),
            P(None, ALL, None),
            P(None, None, ALL),
            P(None, None, ALL),
            P(None, None, ALL),
            P(None, ALL),
            P(None, ALL),
        ),
        out_specs=(
            P("clip", None, SP, None, None),
            P("clip", None, SP, None, None),
            P(None, ALL, None),
            P(None, ALL, None),
            P(None, ALL, None),
            P(None, None, ALL),
            P(None, None, ALL),
            P(None, None, ALL),
            P(None, ALL),
            P(None, ALL),
        ),
        check_vma=False,
    )
```

```python
import functools

import jax
import jax.numpy as jnp
from jax import lax
from jax.experimental import pallas as pl
from jax.experimental.pallas import tpu as pltpu
from jax.sharding import Mesh, PartitionSpec as P

epsilon = 1e-05
F32 = jnp.float32
BF16 = jnp.bfloat16
LANE = 128
STEP = 16
COST = 3.0e6
PER = {"mix": 1, "hidden": 4, "expand": 2, "depth": 1, "grads": 2}


def dot_nn(left, right):
    return lax.dot_general(left, right, (((1,), (0,)), ((), ())), preferred_element_type=F32)


def dot_nt(left, right):
    return lax.dot_general(left, right, (((1,), (1,)), ((), ())), preferred_element_type=F32)


def dot_tn(left, right):
    return lax.dot_general(left, right, (((0,), (0,)), ((), ())), preferred_element_type=F32)


def split(value):
    high = value.astype(BF16)
    return high, (value - high.astype(F32)).astype(BF16)


def dot_split(left, right):
    high, rest = split(left)
    return dot_nn(high, right) + dot_nn(rest, right)


def fold(value):
    return jnp.sum(value.reshape(-1, 8, value.shape[-1]), axis=0)


def row_sum(value):
    return jnp.sum(value, axis=0, keepdims=True)


def live_rows(count, frames, rows, width):
    at = lax.rem(lax.broadcasted_iota(jnp.int32, (rows, width), 0), frames)
    return jnp.where(at < count, 1.0, 0.0)


def live_cap(count, frames, rows, width):
    return jnp.where(live_rows(count, frames, rows, width) > 0.5, 3e38, -60.0)


def full(shape):
    return pl.BlockSpec(shape, lambda *_: (0,) * len(shape))


def smem():
    return pl.BlockSpec(memory_space=pltpu.SMEM)


def call(body, steps, in_specs, out_specs, out_shape, scratch, micros, room=58):
    return pl.pallas_call(
        body,
        grid=(steps,),
        in_specs=in_specs,
        out_specs=out_specs,
        out_shape=out_shape,
        scratch_shapes=scratch,
        cost_estimate=pl.CostEstimate(
            flops=0, transcendentals=0, bytes_accessed=int(micros * COST)
        ),
        compiler_params=pltpu.CompilerParams(
            dimension_semantics=("arbitrary",), vmem_limit_bytes=room * 2**20
        ),
    )


def each(count, body, unroll=1):
    def step(i, carry):
        body(pl.multiple_of(i * STEP, STEP))
        return carry

    lax.fori_loop(0, count // STEP, step, 0, unroll=unroll)


def clip_loop(dims, per, body):
    frames, rows, line = dims
    size = rows * line
    step = pl.program_id(0)

    def one(k, carry):
        def view(ref, extra=0):
            length = size + extra * line
            return ref.at[pl.ds(pl.multiple_of(k * length, STEP), length), :]

        body(step * per + k, k, view)
        return carry

    lax.fori_loop(0, per, one, 0)


def merge_stats(means, squares, counts, total):
    mean = jnp.sum(means * counts, axis=0) / total
    away = means - mean[None]
    spread = jnp.sum(squares + counts * away * away, axis=0) / total
    return mean, lax.rsqrt(spread + epsilon)


def narrow_norm(nf, got_ref, cnt_ref, gain, bias, vec_ref):
    width = vec_ref.shape[1]
    mean, inverse = merge_stats(
        got_ref[:, :, 0:width], got_ref[:, :, width:], cnt_ref[:, :, 0:1], nf[1]
    )
    scale = gain * inverse
    vec_ref[...] = jnp.zeros_like(vec_ref)
    vec_ref[0:1, :] = inverse
    vec_ref[1:2, :] = -mean * inverse
    vec_ref[2:3, :] = 0.5 * scale
    vec_ref[3:4, :] = 0.5 * (bias - mean * scale)
    vec_ref[4:5, :] = scale


def silu_half(half):
    both = jnp.tanh(half) + 1.0
    return half * both, both


def slope_of(value, both):
    return 0.5 * slope_twice(value, both)


def slope_twice(value, both):
    return both + value * (2.0 - both)


def line_stats(nf, scal, dims, read, lines, first_line, is_first, acc, st_ref):
    frames, rows, line = dims
    width = acc.shape[1]

    @pl.when(is_first)
    def _():
        mask = live_rows(scal[0], frames, STEP, width)
        total = jnp.zeros((8, width), F32)
        for i in range(line // STEP):
            total = total + fold(read(0, i * STEP) * mask)
        acc[...] = jnp.zeros_like(acc)
        alive = (scal[0] * (line // frames)).astype(F32)
        acc[0:1, :] = row_sum(total) / alive

    pivot = acc[0:1, :]

    def one(at, carry):
        plain, square = carry
        mask = live_rows(scal[(first_line + at) // rows], frames, STEP, width)
        for i in range(line // STEP):
            away = (read(at, i * STEP) - pivot) * mask
            plain = plain + fold(away)
            square = square + fold(away * away)
        return plain, square

    zero = jnp.zeros((8, width), F32)
    plain, square = lax.fori_loop(0, lines, one, (zero, zero))
    acc[8:16, :] += plain
    acc[16:24, :] += square


def edge_places(scal, clips, line, rows):
    last = line * (rows + 1)
    near = jnp.where(scal[clips + 2] == 0, last, 0)
    return pl.multiple_of(near, STEP), pl.multiple_of(last - near, STEP)


def finish_stats(nf, acc, st_ref):
    plain, square = row_sum(acc[8:16, :]), row_sum(acc[16:24, :])
    width = acc.shape[1]
    peers = st_ref.shape[0]
    st_ref[:, :, 0:width] = jnp.broadcast_to(acc[0:1, :] + plain * nf[2], (peers, 1, width))
    spread = square - plain * plain * nf[2]
    st_ref[:, :, width:] = jnp.broadcast_to(spread, (peers, 1, width))


def share_sums(acc, sum_ref):
    width = acc.shape[1]
    peers = sum_ref.shape[0]
    for k in range(2):
        one = row_sum(acc[8 * k : 8 * k + 8, :])
        sum_ref[:, :, width * k : width * (k + 1)] = jnp.broadcast_to(one, (peers, 1, width))


def depth_weights(par_ref, layer, wd, flip):
    one = lax.broadcasted_iota(jnp.int32, (LANE, LANE), 0)
    two = lax.broadcasted_iota(jnp.int32, (LANE, LANE), 1)
    eye = jnp.where(one == two, 1.0, 0.0)
    for half in range(wd.shape[0]):
        for i in range(9):
            for e in (0, 2):
                tap = 3 * i + e
                at = 27 * layer + (26 - tap if flip else tap)
                row = par_ref[at : at + 1, LANE * half : LANE * (half + 1)]
                k = LANE * (e // 2)
                wd[half, LANE * i : LANE * (i + 1), k : k + LANE] = (eye * row).astype(BF16)


def frame_moves(frames, value):
    here = lax.rem(lax.broadcasted_iota(jnp.int32, value.shape, 0), frames)
    onward = jnp.where(here > 0, pltpu.roll(value, 1, 0), 0.0)
    back = jnp.where(here < frames - 1, pltpu.roll(value, value.shape[0] - 1, 0), 0.0)
    return onward, back


def frame_shifts(dims, value, tv, at):
    onward, back = frame_moves(dims[0], value)
    part = pl.ds(at, value.shape[0])
    tv[0, part, :] = onward.astype(BF16)
    tv[1, part, :] = value.astype(BF16)
    tv[2, part, :] = back.astype(BF16)


def column_moves(dims, value):
    frames, rows, line = dims
    at = lax.broadcasted_iota(jnp.int32, value.shape, 0)
    onward = jnp.where(at >= frames, pltpu.roll(value, frames, 0), 0.0)
    back = jnp.where(at < line - frames, pltpu.roll(value, line - frames, 0), 0.0)
    return onward, back


def depth_sum(dims, layer, flip, par_ref, ms, tv, wd, ds, temp, store):
    frames, rows, line = dims
    halves = wd.shape[0]
    piece = line // 2 if line % (2 * 8) == 0 else line
    for half in range(halves):
        lanes = slice(LANE * half, LANE * (half + 1))
        views = [tv[a, line * b : line * (b + rows), lanes] for a in range(3) for b in range(3)]
        ds[half] = dot_nn(jnp.concatenate(views, axis=1), wd[half])
        taps = []
        for i in range(9):
            tap = 3 * i + 1
            at = 27 * layer + (26 - tap if flip else tap)
            taps.append(par_ref[at : at + 1, lanes])
        for start in range(0, rows * line, piece):
            seen = [ms[start + line * b : start + line * b + piece, lanes] for b in range(3)]
            sums = []
            for a in range(3):
                one = seen[0] * taps[3 * a]
                one = one + seen[1] * taps[3 * a + 1]
                sums.append(one + seen[2] * taps[3 * a + 2])
            onward, _ = frame_moves(frames, sums[0])
            _, back = frame_moves(frames, sums[2])
            temp[start : start + piece, lanes] = onward + sums[1] + back
    for half in range(halves):
        lanes = slice(LANE * half, LANE * (half + 1))
        for r in range(rows):
            part = slice(line * r, line * (r + 1))
            onward, _ = column_moves(dims, ds[half, part, 0:LANE])
            _, back = column_moves(dims, ds[half, part, LANE : 2 * LANE])
            store(r, lanes, onward + temp[part, lanes] + back)


def pack_kernel(wr_ref, wm_ref, wd_ref, gm_ref, bm_ref, go_ref, bo_ref, out_ref):
    r1, width = wr_ref.shape[1:]
    r2 = wm_ref.shape[1]
    r4, taps = wd_ref.shape[1:]
    r6 = go_ref.shape[1]
    zeros = lambda rows, size: jnp.zeros((rows, size), F32)
    part = [wd_ref[k].astype(F32) for k in range(2)]
    pad = zeros(r4, 32 - taps)
    taps_rows = jnp.concatenate([part[0], pad, part[1], pad, zeros(r4, width - 64)], axis=1)
    mids = [gm_ref[k].astype(F32) for k in range(2)] + [bm_ref[k].astype(F32) for k in range(2)]
    mids = jnp.concatenate(mids, axis=0)
    outs = jnp.concatenate([go_ref[...].astype(F32), bo_ref[...].astype(F32)], axis=0)
    mids = jnp.concatenate([mids, zeros(8, 32 - r4)], axis=1)
    outs = jnp.concatenate([outs, zeros(4, r6)], axis=0)
    others = jnp.concatenate([mids, outs, zeros(8, width - 32 - r6)], axis=1)
    rest = out_ref.shape[1] - r1 - r2 - r4 - 8
    rows = [wr_ref[0].astype(F32), wm_ref[0].astype(F32), taps_rows, others, zeros(rest, width)]
    block = jnp.concatenate(rows, axis=0).astype(BF16)
    for k in range(out_ref.shape[0]):
        out_ref[k] = block


def first_kernel(dims, lines, scal, nf, x_ref, w_ref, red_ref, up_ref, dn_ref, st_ref, acc):
    step = pl.program_id(0)
    red_ref[...] = dot_nn(x_ref[...], w_ref[...].reshape(-1, w_ref.shape[2]))
    reduced_tail(dims, lines, step, scal, nf, red_ref, up_ref, dn_ref, st_ref, acc)


def reduced_tail(dims, lines, step, scal, nf, red_ref, up_ref, dn_ref, st_ref, acc):
    frames, rows, line = dims
    read = lambda at, i: red_ref[pl.ds(pl.multiple_of(line * at, STEP) + i, STEP), :]
    line_stats(nf, scal, dims, read, lines, step * lines, step == 0, acc, st_ref)
    for k in range(lines // rows):
        clip, at = step * (lines // rows) + k, k * rows * line
        even = scal[scal.shape[0] - 1] == 0
        last = line * (rows - 1)
        near = jnp.where(even, last, 0)
        up_ref[clip] = red_ref[pl.ds(pl.multiple_of(at + near, STEP), line), :]
        dn_ref[clip] = red_ref[pl.ds(pl.multiple_of(at + last - near, STEP), line), :]

    @pl.when(step == pl.num_programs(0) - 1)
    def _():
        finish_stats(nf, acc, st_ref)


def mix_kernel(
    dims, layer, per, scal, nf, red_ref, up_ref, dn_ref, got_ref, cnt_ref, par_ref, w_ref,
    mix_ref, spa_ref, z_ref, u_ref, h_ref, st_ref, vec_ref, hs, ms, tv, wd, ds, acc,
):
    step, last = pl.program_id(0), pl.num_programs(0) - 1
    width = w_ref.shape[0]

    @pl.when(step == 0)
    def _():
        at = 2 * layer
        narrow_norm(
            nf, got_ref, cnt_ref, par_ref[54 + at : 55 + at, :], par_ref[58 + at : 59 + at, :],
            vec_ref,
        )
        depth_weights(par_ref, layer, wd, False)

    def body(clip, k, view):
        mix_clip(
            dims, layer, scal, nf, view(red_ref), up_ref.at[k], dn_ref.at[k], par_ref, w_ref,
            view(mix_ref, 2), view(spa_ref), view(z_ref), view(u_ref), view(h_ref), st_ref,
            vec_ref, hs, ms, tv, wd, ds, acc, clip, per * (last + 1),
        )

    clip_loop(dims, per, body)

    @pl.when(step == last)
    def _():
        finish_stats(nf, acc, st_ref)


def mix_clip(
    dims, layer, scal, nf, red_ref, up_ref, dn_ref, par_ref, w_ref, mix_ref, spa_ref, z_ref,
    u_ref, h_ref, st_ref, vec_ref, hs, ms, tv, wd, ds, acc, clip, clips,
):
    frames, rows, line = dims
    width = w_ref.shape[0]
    mask = live_rows(scal[clip], frames, STEP, width)
    near = mask * scal[clips].astype(F32)
    far = mask * scal[clips + 1].astype(F32)
    near_at, far_at = edge_places(scal, clips, line, rows)

    def edge(i):
        h, _ = silu_half(up_ref[pl.ds(i, STEP), :] * vec_ref[2:3, :] + vec_ref[3:4, :])
        hs[pl.ds(near_at + i, STEP), :] = (h * near).astype(BF16)
        h, _ = silu_half(dn_ref[pl.ds(i, STEP), :] * vec_ref[2:3, :] + vec_ref[3:4, :])
        hs[pl.ds(far_at + i, STEP), :] = (h * far).astype(BF16)

    each(line, edge, 7)

    def own(i):
        value = red_ref[pl.ds(i, STEP), :]
        h, both = silu_half(value * vec_ref[2:3, :] + vec_ref[3:4, :])
        low = (h * mask).astype(BF16)
        hs[pl.ds(i + line, STEP), :] = low
        h_ref[pl.ds(i, STEP), :] = low
        u_ref[pl.ds(i, STEP), :] = (slope_of(h, both) * mask).astype(BF16)
        z_ref[pl.ds(i, STEP), :] = (value * vec_ref[0:1, :] + vec_ref[1:2, :]).astype(BF16)

    each(line * rows, own, 7)
    ms[...] = dot_nn(hs[...], w_ref[...])

    def shifts(r, carry):
        at = pl.multiple_of(r * line, STEP)
        for half in range(width // LANE):
            lanes = slice(LANE * half, LANE * (half + 1))
            part = pl.ds(at, line)
            value = ms[part, lanes].astype(BF16).astype(F32)
            ms[part, lanes] = value
            frame_shifts(dims, value, tv.at[:, :, lanes], at)
        return carry

    lax.fori_loop(0, rows + 2, shifts, 0)
    mix_ref[...] = tv[1]

    def store(r, lanes, value):
        spa_ref[line * r : line * (r + 1), lanes] = value

    depth_sum(dims, layer, False, par_ref, ms, tv, wd, ds, spa_ref, store)
    read = lambda at, i: spa_ref[pl.ds(pl.multiple_of(line * at, STEP) + i, STEP), :]
    line_stats(nf, scal, dims, read, rows, clip * rows, clip == 0, acc, st_ref)

def hidden_rows(i, mask, spa_ref, h_ref, u_ref, z_ref, vec_ref, acc):
    part = pl.ds(i, STEP)
    value = spa_ref[part, :]
    h, both = silu_half(value * vec_ref[2:3, :] + vec_ref[3:4, :])
    low = (h * mask).astype(BF16)
    h_ref[part, :] = low
    u_ref[part, :] = (slope_of(h, both) * mask).astype(BF16)
    z_ref[part, :] = (value * vec_ref[0:1, :] + vec_ref[1:2, :]).astype(BF16)
    acc[...] += fold(low.astype(F32))


def hidden_kernel(
    dims, layer, per, scal, nf, spa_ref, got_ref, cnt_ref, par_ref, w_ref,
    z_ref, u_ref, h_ref, st_ref, gram_ref, vec_ref, acc,
):
    frames, rows, line = dims
    step = pl.program_id(0)
    width = par_ref.shape[1]

    @pl.when(step == 0)
    def _():
        at = 2 * layer
        narrow_norm(
            nf, got_ref, cnt_ref, par_ref[55 + at : 56 + at, :], par_ref[59 + at : 60 + at, :],
            vec_ref,
        )
        gram_ref[...] = jnp.zeros_like(gram_ref)
        acc[...] = jnp.zeros_like(acc)

    def body(clip, k, view):
        mask = live_rows(scal[clip], frames, STEP, width)
        spa, h_out, u_out, z_out = view(spa_ref), view(h_ref), view(u_ref), view(z_ref)

        def own(i):
            hidden_rows(i, mask, spa, h_out, u_out, z_out, vec_ref, acc)

        each(line * rows, own, 7)

    clip_loop(dims, per, body)
    gram_ref[0:width, :] += dot_tn(h_ref[...], h_ref[...])

    @pl.when(step == pl.num_programs(0) - 1)
    def _():
        total = row_sum(acc[...])
        gram_ref[width : width + 8, :] = jnp.broadcast_to(total, (8, width))
        across = jnp.broadcast_to(total, (width, width))
        centered = gram_ref[0:width, :] - across.T * across * nf[2]
        spread = row_sum(dot_split(centered, w_ref[...]) * w_ref[...].astype(F32))
        peers = st_ref.shape[0]
        st_ref[:, :, 0:width] = jnp.broadcast_to(total, (peers, 1, width))
        st_ref[:, :, width:] = jnp.broadcast_to(spread, (peers, 1, spread.shape[1]))


def wide_norm(nf, got_ref, cnt_ref, rinv_ref, pout_ref, layer, w_ref, vec_ref):
    width = w_ref.shape[0]
    hidden_means = got_ref[:, 0, 0:width] * rinv_ref[:, 0:1]
    means = dot_split(hidden_means, w_ref[...])
    counts = cnt_ref[:, 0, 0:1]
    mean = row_sum(means * counts) / nf[1]
    away = means - mean
    spread = row_sum(got_ref[:, 0, width:] + counts * away * away) / nf[1]
    inverse = lax.rsqrt(spread + epsilon)
    scale = pout_ref[layer : layer + 1, :] * inverse
    vec_ref[...] = jnp.zeros_like(vec_ref)
    vec_ref[0:1, :] = scale
    vec_ref[1:2, :] = 0.5 * (pout_ref[2 + layer : 3 + layer, :] - mean * scale)
    vec_ref[2:3, :] = inverse
    vec_ref[3:4, :] = mean
    vec_ref[4:5, :] = 0.5 * scale


def each_line(dims, lines, step, scal, width, body, make=live_cap):
    frames, rows, line = dims

    def run(carry):
        for at in range(lines):
            mask = make(scal[(step * lines + at) // rows], frames, STEP, width)
            for i in range(at * line, (at + 1) * line, STEP):
                carry = body(slice(i, i + STEP), mask, carry)
        return carry

    return run


def join_kernel(
    dims, lines, scal, nf, x_ref, h_ref, got_ref, cnt_ref, rinv_ref, pout_ref, w3_ref, w1_ref,
    next_ref, du_ref, red_ref, up_ref, dn_ref, st_ref, vec_ref, es, acc,
):
    step = pl.program_id(0)
    wide, width = w1_ref.shape
    block = 256

    @pl.when(step == 0)
    def _():
        wide_norm(nf, got_ref, cnt_ref, rinv_ref, pout_ref, 0, w3_ref, vec_ref)

    for j in range(wide // block):
        lanes = slice(block * j, block * (j + 1))
        es[j % 2] = dot_nn(h_ref[...], w3_ref[:, lanes])
        scale, shift = vec_ref[4:5, lanes], vec_ref[1:2, lanes]

        def own(part, cap, carry):
            half = x_ref[part, lanes].astype(F32) * 0.5 + (es[j % 2, part, :] * scale + shift)
            o, both = silu_half(jnp.minimum(half, cap))
            next_ref[part, lanes] = (0.5 * o).astype(BF16)
            du_ref[part, lanes] = slope_twice(o, both).astype(BF16)
            return carry

        each_line(dims, lines, step, scal, block, own)(0)
    red_ref[...] = 2.0 * dot_nn(next_ref[...], w1_ref[...])
    reduced_tail(dims, lines, step, scal, nf, red_ref, up_ref, dn_ref, st_ref, acc)


def wide_tail(hT, gs_ref, w3s, low_ref, t_ref):
    t_ref[...] += dot_nn(hT, gs_ref[...])
    low_ref[...] = dot_nt(gs_ref[...], w3s[...])


def wide_sums(w3_ref, t_ref, sacc, vec_ref, sum_ref, unit):
    wide = w3_ref.shape[1]
    t_ref[...] = unit * t_ref[...]
    plain = unit * row_sum(sacc[...])
    along = row_sum(w3_ref[...].astype(F32) * t_ref[...])
    along = (along - vec_ref[3:4, :] * plain) * vec_ref[2:3, :]
    pieces = [
        one[:, LANE * k : LANE * (k + 1)] for one in (plain, along) for k in range(wide // LANE)
    ]
    sum_ref[...] = jnp.broadcast_to(jnp.concatenate(pieces, axis=0)[None], sum_ref.shape).astype(
        BF16
    )


def out_kernel(
    dims, lines, scal, nf, x_ref, h_ref, cot_ref, got_ref, cnt_ref, rinv_ref, pout_ref, w3_ref,
    out_ref, gs_ref, low_ref, t_ref, sum_ref, vec_ref, es, w3s, sacc,
):
    step = pl.program_id(0)
    width, wide = w3_ref.shape
    frames = dims[0]
    block = 256
    unit = 0.5

    @pl.when(step == 0)
    def _():
        wide_norm(nf, got_ref, cnt_ref, rinv_ref, pout_ref, 1, w3_ref, vec_ref)
        t_ref[...] = jnp.zeros_like(t_ref)
        sacc[...] = jnp.zeros_like(sacc)
        w3s[...] = (w3_ref[...].astype(F32) * (unit * vec_ref[0:1, :])).astype(BF16)

    hT = h_ref[...].T
    for j in range(wide // block):
        lanes = slice(block * j, block * (j + 1))
        es[j % 2] = dot_nn(h_ref[...], w3_ref[:, lanes])
        scale, shift = vec_ref[4:5, lanes], vec_ref[1:2, lanes]

        def own(part, cap, total):
            half = x_ref[part, lanes].astype(F32) + (es[j % 2, part, :] * scale + shift)
            o, both = silu_half(jnp.minimum(half, cap))
            spot = slice(part.start // frames, part.stop // frames)
            out_ref[spot, :, lanes] = o.astype(BF16).reshape(-1, frames, block)
            grad = cot_ref[spot, :, lanes].reshape(-1, block).astype(F32)
            grad = grad * slope_twice(o, both)
            gs_ref[part, lanes] = grad.astype(BF16)
            return total + fold(grad)

        total = each_line(dims, lines, step, scal, block, own)(jnp.zeros((8, block), F32))
        sacc[:, lanes] += total
    wide_tail(hT, gs_ref, w3s, low_ref, t_ref)

    @pl.when(step == pl.num_programs(0) - 1)
    def _():
        wide_sums(w3_ref, t_ref, sacc, vec_ref, sum_ref, unit)


def expand_back_kernel(
    dims, per, scal, nf, low_ref, h_ref, z_ref, u_ref, got_ref, vec_ref, t_ref, gram_ref, w3_ref,
    go_ref, up_ref, dn_ref, sum_ref, ge_ref, tot_ref, ks, crow, hk, acc,
):
    frames, rows, line = dims
    step = pl.program_id(0)
    width, wide = w3_ref.shape

    @pl.when(step == 0)
    def _():
        totals = jnp.sum(got_ref[...].astype(F32), axis=0)
        count = wide // LANE
        plain = jnp.concatenate([totals[k : k + 1, :] for k in range(count)], axis=1)
        along = jnp.concatenate([totals[k : k + 1, :] for k in range(count, 2 * count)], axis=1)
        tot_ref[:, 0:wide] = plain
        tot_ref[:, wide:] = along
        plain, along = plain * nf[3], along * nf[3]
        scale, inverse, mean = vec_ref[0:1, :], vec_ref[2:3, :], vec_ref[3:4, :]
        w3 = w3_ref[...]
        rise = scale * inverse * along
        flat = scale * plain - rise * mean
        ks[...] = dot_nt((w3.astype(F32) * rise).astype(BF16), w3).astype(BF16)
        spread = [jnp.broadcast_to(one, (16, wide)) for one in split(flat)]
        crow[...] = (dot_nt(spread[0], w3) + dot_nt(spread[1], w3))[0:8]
        column = jnp.broadcast_to(gram_ref[width : width + 1, :], (LANE, width)).T[:, 0:1]
        cross = dot_split(gram_ref[0:width, :], w3)
        ge_ref[...] = (t_ref[...] * scale - column * flat - cross * rise).astype(BF16)
        acc[...] = jnp.zeros_like(acc)

    hk[...] = dot_nn(h_ref[...], ks[...])

    def own(i):
        part = pl.ds(i, STEP)
        grad = (low_ref[part, :] - crow[0:1, :] - hk[part, :]) * u_ref[part, :].astype(F32)
        go_ref[part, :] = grad.astype(BF16)
        acc[0:8, :] += fold(grad)
        acc[8:16, :] += fold(grad * z_ref[part, :].astype(F32))

    each(line * rows * per, own, 7)
    for k in range(per):
        expand_edges(dims, scal, k * rows * line, go_ref, z_ref, up_ref.at[k], dn_ref.at[k])

    @pl.when(step == pl.num_programs(0) - 1)
    def _():
        share_sums(acc, sum_ref)


def expand_edges(dims, scal, base, go_ref, z_ref, up_ref, dn_ref):
    frames, rows, line = dims
    even = scal[scal.shape[0] - 1] == 0
    last = line * (rows - 1)
    first = jnp.where(even, last, 0)
    near = pl.multiple_of(base + first, STEP)
    far = pl.multiple_of(base + last - first, STEP)
    up_ref[0] = go_ref[pl.ds(near, line), :]
    up_ref[1] = z_ref[pl.ds(near, line), :]
    dn_ref[0] = go_ref[pl.ds(far, line), :]
    dn_ref[1] = z_ref[pl.ds(far, line), :]


def norm_rows(nf, got_ref, vec_ref, tot_ref, rows3):
    width = vec_ref.shape[1]
    totals = jnp.sum(got_ref[...], axis=0)
    tot_ref[...] = totals
    rows3[0:1, :] = vec_ref[4:5, :]
    rows3[1:2, :] = vec_ref[4:5, :] * totals[:, 0:width] * nf[3]
    rows3[2:3, :] = vec_ref[4:5, :] * totals[:, width:] * nf[3]


def norm_back(rows3, go, z, mask):
    value = rows3[0:1, :] * go.astype(F32) - rows3[1:2, :] - rows3[2:3, :] * z.astype(F32)
    return value * mask


def depth_back_kernel(
    dims, layer, per, scal, nf, go_ref, above_ref, below_ref, z_ref, got_ref, vec_ref,
    z1_ref, u1_ref, par_ref, w_ref,
    go1_ref, sum_ref, gm_ref, gp_ref, tot_ref, ms, tv, wd, ds, gh, rows3, acc,
):
    step, last = pl.program_id(0), pl.num_programs(0) - 1
    width = w_ref.shape[0]

    @pl.when(step == 0)
    def _():
        norm_rows(nf, got_ref, vec_ref, tot_ref, rows3)
        depth_weights(par_ref, layer, wd, True)
        acc[...] = jnp.zeros_like(acc)

    def body(clip, k, view):
        depth_back_clip(
            dims, layer, scal, view(go_ref), above_ref.at[k], below_ref.at[k], view(z_ref),
            view(z1_ref), view(u1_ref), par_ref, w_ref, view(go1_ref), view(gm_ref), view(gp_ref),
            ms, tv, wd, ds, gh, rows3, acc, clip, per * (last + 1),
        )

    clip_loop(dims, per, body)

    @pl.when(step == last)
    def _():
        share_sums(acc, sum_ref)


def depth_back_clip(
    dims, layer, scal, go_ref, above_ref, below_ref, z_ref, z1_ref, u1_ref, par_ref, w_ref,
    go1_ref, gm_ref, gp_ref, ms, tv, wd, ds, gh, rows3, acc, clip, clips,
):
    frames, rows, line = dims
    width = w_ref.shape[0]
    mask = live_rows(scal[clip], frames, STEP, width)
    near = mask * scal[clips].astype(F32)
    far = mask * scal[clips + 1].astype(F32)
    near_at, far_at = edge_places(scal, clips, line, rows)

    def edge(i):
        part = pl.ds(i, STEP)
        ms[pl.ds(near_at + i, STEP), :] = norm_back(
            rows3, above_ref[0, part, :], above_ref[1, part, :], near
        )
        ms[pl.ds(far_at + i, STEP), :] = norm_back(
            rows3, below_ref[0, part, :], below_ref[1, part, :], far
        )

    each(line, edge, 7)

    def own(i):
        part = pl.ds(i, STEP)
        ms[pl.ds(i + line, STEP), :] = norm_back(rows3, go_ref[part, :], z_ref[part, :], mask)

    each(line * rows, own, 7)

    def shifts(r, carry):
        at = pl.multiple_of(r * line, STEP)
        for half in range(width // LANE):
            lanes = slice(LANE * half, LANE * (half + 1))
            part = pl.ds(at, line)
            value = ms[part, lanes].astype(BF16).astype(F32)
            ms[part, lanes] = value
            frame_shifts(dims, value, tv.at[:, :, lanes], at)
        return carry

    lax.fori_loop(0, rows + 2, shifts, 0)
    gp_ref[...] = tv[1, line : line * (rows + 1), :]

    def store(r, lanes, value):
        gm_ref[line * r : line * (r + 1), lanes] = value.astype(BF16)

    depth_sum(dims, layer, True, par_ref, ms, tv, wd, ds, gh, store)
    gh[...] = dot_nt(gm_ref[...], w_ref[...])

    def first(i):
        part = pl.ds(i, STEP)
        value = gh[part, :] * u1_ref[part, :].astype(F32)
        go1_ref[part, :] = value.astype(BF16)
        acc[0:8, :] += fold(value)
        acc[8:16, :] += fold(value * z1_ref[part, :].astype(F32))

    each(line * rows, first, 7)

def kernel_grads(
    dims, per, mix_ref, gp_ref, gm_ref, h_ref, gmix_ref, gdep_ref, tv, mv, gacc, vacc,
):
    step = pl.program_id(0)
    width = h_ref.shape[1]
    halves = width // LANE

    @pl.when(step == 0)
    def _():
        gmix_ref[...] = jnp.zeros_like(gmix_ref)
        gacc[...] = jnp.zeros_like(gacc)
        vacc[...] = jnp.zeros_like(vacc)

    gmix_ref[...] += dot_tn(h_ref[...], gm_ref[...])

    def body(clip, k, view):
        kernel_clip(dims, halves, view(mix_ref, 2), view(gp_ref), tv, mv, gacc, vacc)

    clip_loop(dims, per, body)

    @pl.when(step == pl.num_programs(0) - 1)
    def _():
        one = lax.broadcasted_iota(jnp.int32, (LANE, LANE), 0)
        two = lax.broadcasted_iota(jnp.int32, (LANE, LANE), 1)
        gdep_ref[...] = jnp.zeros_like(gdep_ref)
        for half in range(halves):
            lanes = slice(LANE * half, LANE * (half + 1))
            for i in range(9):
                gdep_ref[3 * i + 1 : 3 * i + 2, lanes] = row_sum(vacc[i, :, lanes])
                for e in (0, 2):
                    k = LANE * (e // 2)
                    part = gacc[half, k : k + LANE, LANE * i : LANE * (i + 1)]
                    gdep_ref[3 * i + e : 3 * i + e + 1, lanes] = row_sum(
                        jnp.where(one == two, part, 0.0)
                    )


def kernel_clip(dims, halves, mix_ref, gp_ref, tv, mv, gacc, vacc):
    frames, rows, line = dims

    def shifts(r, carry):
        at = pl.multiple_of(r * line, STEP)
        for half in range(halves):
            lanes = slice(LANE * half, LANE * (half + 1))
            value = mix_ref[pl.ds(at, line), lanes].astype(F32)
            frame_shifts(dims, value, tv.at[:, :, lanes], at)
        return carry

    lax.fori_loop(0, rows + 2, shifts, 0)

    def moves(r, carry):
        at = pl.multiple_of(r * line, STEP)
        for half in range(halves):
            lanes = slice(LANE * half, LANE * (half + 1))
            value = gp_ref[pl.ds(at, line), lanes].astype(F32)
            onward, back = column_moves(dims, value)
            mv[half, pl.ds(at, line), 0:LANE] = back.astype(BF16)
            mv[half, pl.ds(at, line), LANE : 2 * LANE] = onward.astype(BF16)
        return carry

    lax.fori_loop(0, rows, moves, 0)
    for half in range(halves):
        lanes = slice(LANE * half, LANE * (half + 1))
        views = [tv[a, line * b : line * (b + rows), lanes] for a in range(3) for b in range(3)]
        gacc[half] += dot_tn(mv[half], jnp.concatenate(views, axis=1))
        sums = [vacc[i, :, lanes] for i in range(9)]
        for start in range(0, rows * line, line):
            own = gp_ref[start : start + line, lanes].astype(F32)
            onward, back = frame_moves(frames, own)
            for b in range(3):
                seen = mix_ref[start + line * b : start + line * b + line, lanes].astype(F32)
                for a, moved in enumerate((back, own, onward)):
                    sums[3 * a + b] = sums[3 * a + b] + fold(moved * seen)
        for i in range(9):
            vacc[i, :, lanes] = sums[i]


def reduced_grad(dims, lines, step, scal, go_ref, z_ref, rows3, gr_ref):
    def own(part, mask, carry):
        gr_ref[part, :] = norm_back(rows3, go_ref[part, :], z_ref[part, :], mask).astype(BF16)
        return carry

    each_line(dims, lines, step, scal, rows3.shape[1], own, live_rows)(0)


def cross_kernel(
    dims, lines, scal, nf, go_ref, z_ref, got_ref, vec1_ref, gs_ref, du_ref, h_ref,
    vec3_ref, w1_ref, w3_ref,
    gs0_ref, low_ref, t_ref, sum_ref, gr_ref, tot_ref, ds, w1s, w3s, rows3, sacc,
):
    step = pl.program_id(0)
    width, wide = w3_ref.shape
    block = 256
    unit = 0.25

    @pl.when(step == 0)
    def _():
        norm_rows(nf, got_ref, vec1_ref, tot_ref, rows3)
        t_ref[...] = jnp.zeros_like(t_ref)
        sacc[...] = jnp.zeros_like(sacc)
        w3s[...] = (w3_ref[...].astype(F32) * (unit * vec3_ref[0:1, :])).astype(BF16)
        w1s[...] = (w1_ref[...].astype(F32) * 2.0).astype(BF16)

    reduced_grad(dims, lines, step, scal, go_ref, z_ref, rows3, gr_ref)
    hT = h_ref[...].T
    for j in range(wide // block):
        lanes = slice(block * j, block * (j + 1))
        ds[j % 2] = dot_nt(gr_ref[...], w1s[lanes, :])

        def own(part, mask, total):
            value = gs_ref[part, lanes].astype(F32) + ds[j % 2, part, :]
            value = value * du_ref[part, lanes].astype(F32)
            gs0_ref[part, lanes] = value.astype(BF16)
            return total + fold(value)

        total = each_line(dims, lines, step, scal, block, own)(jnp.zeros((8, block), F32))
        sacc[:, lanes] += total
    wide_tail(hT, gs0_ref, w3s, low_ref, t_ref)

    @pl.when(step == pl.num_programs(0) - 1)
    def _():
        wide_sums(w3_ref, t_ref, sacc, vec3_ref, sum_ref, unit)


def reduce_grad_kernel(unit, x_ref, gr_ref, out_ref, gacc):
    step = pl.program_id(0)

    @pl.when(step == 0)
    def _():
        gacc[...] = jnp.zeros_like(gacc)

    gacc[...] += dot_tn(gr_ref[...], x_ref[...])

    @pl.when(step == pl.num_programs(0) - 1)
    def _():
        out_ref[...] = (unit * gacc[...].T).astype(BF16)


def last_grad_kernel(
    dims, lines, scal, nf, go_ref, z_ref, got_ref, vec1_ref, x_ref,
    gr_ref, mine_ref, sent_ref, tot_ref, rows3, gacc,
):
    step = pl.program_id(0)

    @pl.when(step == 0)
    def _():
        norm_rows(nf, got_ref, vec1_ref, tot_ref, rows3)
        gacc[...] = jnp.zeros_like(gacc)

    reduced_grad(dims, lines, step, scal, go_ref, z_ref, rows3, gr_ref)
    gacc[...] += dot_tn(gr_ref[...], x_ref[...])

    @pl.when(step == pl.num_programs(0) - 1)
    def _():
        chips, size, width = mine_ref.shape
        both = gacc[...].T.reshape(chips, -1, size, width)
        even = scal[scal.shape[0] - 1] == 0
        other = both.shape[1] - 1
        mine_ref[...] = jnp.where(even, both[:, 0], both[:, other]).astype(BF16)
        sent_ref[...] = jnp.where(even, both[:, other], both[:, 0]).astype(BF16)


def input_kernel(gr_ref, gs_ref, w1_ref, out_ref):
    w1 = w1_ref[...].reshape(-1, w1_ref.shape[2])
    value = dot_nt(gr_ref[...], w1) + 0.25 * gs_ref[...].astype(F32)
    out_ref[...] = value.astype(BF16).reshape(out_ref.shape)


ALL = ("clip", "outer", "inner")
CHIPS = ("clip", "outer")
SP = ("outer", "inner")


def share(rows):
    return lax.all_to_all(rows, ALL, 0, 0)


def gather(value):
    return share(jnp.broadcast_to(value[None], (lax.axis_size(ALL),) + value.shape))


def neighbours(near, far):
    peers = lax.axis_size(SP)
    first = [(i, i + 1) for i in range(0, peers - 1, 2)]
    second = [(i, i + 1) for i in range(1, peers - 1, 2)]
    near = lax.ppermute(near, SP, first + [(j, i) for i, j in first])
    far = lax.ppermute(far, SP, second + [(j, i) for i, j in second])
    return near, far


def swap(value):
    peers = lax.axis_size("inner")
    return lax.ppermute(value, "inner", [(i, (i + 1) % peers) for i in range(peers)])


def after(value, other):
    return lax.optimization_barrier((value, other))[0]


def on_device(
    features, strides, cotangent, w_reduce, w_mix, w_expand, w_depth,
    gains_mid, biases_mid, gains_out, biases_out,
):
    clips, frames, rows, columns, wide = features.shape
    width = w_mix.shape[2]
    peers, chips = lax.axis_size(ALL), lax.axis_size(CHIPS)
    inner = lax.axis_size("inner")
    sp_size = lax.axis_size(SP)
    part, place = lax.axis_index("inner"), lax.axis_index(ALL)
    sp_at = lax.axis_index(SP)
    line = columns * frames
    per_clip = rows * line
    voxels = clips * per_clip
    r1, r2 = w_reduce.shape[1], w_mix.shape[1]
    r4 = w_depth.shape[2]
    r5 = gains_out.shape[1] // r4
    blocks = wide // width

    def from_chips(packed):
        packed = jnp.pad(packed, ((0, -packed.shape[0] % 16), (0, 0)))
        return lax.all_to_all(
            jnp.broadcast_to(packed[None], (chips,) + packed.shape), CHIPS, 0, 0
        )

    def from_cores(near):
        held = [near]
        for _ in range(inner - 1):
            held.append(swap(held[-1]))
        turns = [lax.rem(part - c + inner, inner) for c in range(inner)]
        whole = jnp.stack([lax.select_n(turn, *held) for turn in turns], axis=1)
        return whole.reshape((peers,) + near.shape[1:])

    def wide_weight(rows_of_all):
        one = rows_of_all.reshape(peers, blocks, r2, width).transpose(0, 2, 1, 3)
        return one.reshape(peers * r2, wide)

    height = r1 + r2 + r4 + 8
    height += -height % 16
    whole = lambda value: full(value.shape)
    raw = (w_reduce, w_mix, w_depth.transpose(0, 2, 1), gains_mid, biases_mid, gains_out,
           biases_out)
    packed = call(
        pack_kernel, 1, [whole(one) for one in raw], full((chips, height, width)),
        jax.ShapeDtypeStruct((chips, height, width), BF16), [], 1,
    )(*raw)
    near = lax.all_to_all(packed, CHIPS, 0, 0)
    x = features.transpose(0, 2, 3, 1, 4).reshape(voxels, wide)
    near, x = lax.optimization_barrier((near, x))
    early = from_cores(near)
    w2 = [early[:, r1 : r1 + r2].reshape(-1, width)]
    at = r1 + r2
    taps = early[:, at : at + r4, 0:64].reshape(-1, 64).T
    taps = [taps[32 * k : 32 * k + 27] for k in range(2)]
    others = early[:, at + r4 : at + r4 + 8]
    mids = others[:, :, 0:r4].transpose(1, 0, 2).reshape(8, width)
    par = jnp.concatenate([*taps, mids, jnp.zeros((2, width), BF16)], axis=0).astype(F32)
    pout = others[:, 0:4, 32 : 32 + r4 * r5].transpose(1, 0, 2).reshape(4, wide).astype(F32)

    counts = frames // strides
    by_group = jnp.sum(counts.reshape(-1, clips), axis=1) * (rows * columns)
    by_device = jnp.repeat(by_group, sp_size).astype(F32)
    local = lax.dynamic_slice_in_dim(counts, lax.axis_index("clip") * clips, clips)
    odd = lax.rem(sp_at, 2)
    has_near = (odd == 1) | (sp_at < sp_size - 1)
    has_far = jnp.where(odd == 1, sp_at < sp_size - 1, sp_at > 0)
    edges = jnp.stack([has_near.astype(jnp.int32), has_far.astype(jnp.int32), odd])
    scal = jnp.concatenate([local.astype(jnp.int32), edges])
    own = jnp.sum(local).astype(F32) * (rows * columns)
    total = jnp.sum(by_device)
    nf = jnp.stack([own, total, 1.0 / own, 1.0 / total])
    cnt = jnp.broadcast_to(by_device[:, None, None], (peers, 1, LANE))
    rinv = jnp.broadcast_to(1.0 / by_device[:, None], (peers, LANE))

    struct = jax.ShapeDtypeStruct
    dims = (frames, rows, line)
    lines = rows
    steps = clips * rows // lines
    tall = (rows + 2) * line
    by_step = lambda size: pl.BlockSpec((lines * line, size), lambda s: (s, 0))
    thin, broad = by_step(width), by_step(wide)

    def by_clip(name):
        per = PER[name] if clips % PER[name] == 0 else 1
        field = pl.BlockSpec((per * per_clip, width), lambda c: (c, 0))
        tall_field = pl.BlockSpec((per * tall, width), lambda c: (c, 0))
        edge_one = pl.BlockSpec((per, line, width), lambda c: (c, 0, 0))
        edge_two = pl.BlockSpec((per, 2, line, width), lambda c: (c, 0, 0, 0))
        return per, field, tall_field, edge_one, edge_two

    native = pl.BlockSpec((lines * line // frames, frames, wide), lambda s: (s, 0, 0))
    native_shape = struct((voxels // frames, frames, wide), BF16)
    narrow = lambda kind: struct((voxels, width), kind)
    wide_shape = struct((voxels, wide), BF16)
    edge = struct((clips, line, width), F32)
    pair = struct((clips, 2, line, width), BF16)
    flat = lambda *shape: struct(shape, F32)
    two = (peers, 1, 2 * width)
    three = (peers, 1, width + wide)
    many = (peers, 2 * wide // LANE, LANE)
    vec, vec_wide = (8, width), (8, wide)

    reduced, up, dn, stats = call(
        functools.partial(first_kernel, dims, lines), steps,
        [smem(), smem(), broad, full((peers, r1, width))],
        [thin, full(edge.shape), full(edge.shape), full(two)],
        [narrow(F32), edge, edge, flat(*two)],
        [pltpu.VMEM((24, width), F32)], 6,
    )(scal, nf, x, early)

    depth_scratch = [
        pltpu.VMEM((tall, width), F32), pltpu.VMEM((3, tall, width), BF16),
        pltpu.VMEM((width // LANE, 9 * LANE, 2 * LANE), BF16),
        pltpu.VMEM((width // LANE, per_clip, 2 * LANE), F32),
    ]
    above, below = neighbours(up, dn)
    got = share(stats)
    wide_rows = w_expand.reshape(2, r2, blocks, width).transpose(0, 2, 1, 3)
    wide_rows = wide_rows.reshape(2, r2 * blocks, width)

    near = from_chips(
        after(jnp.concatenate([wide_rows[0], w_reduce[1]], axis=0), (got, above, below))
    )
    w1, w3 = [early], []
    stored = []
    for layer in range(2):
        if layer == 1:
            above, below = neighbours(up, dn)
            got = share(stats)
            late = from_cores(after(near, stats))
            w3.append(wide_weight(late[:, : r2 * blocks]))
            w2.append(late[:, r2 * blocks : r2 * blocks + r2].reshape(-1, width))
        per, field, tall_field, edge_one, edge_two = by_clip("mix")
        mixed, spatial, z1, u1, h1, stats, vec1 = call(
            functools.partial(mix_kernel, dims, layer, per), clips // per,
            [smem(), smem(), field, edge_one, edge_one, full(two),
             full((peers, 1, LANE)), full((64, width)), full((width, width))],
            [tall_field, field, field, field, field, full(two), full(vec)],
            [struct((clips * tall, width), BF16), narrow(F32), narrow(BF16), narrow(BF16),
             narrow(BF16), flat(*two), flat(*vec)],
            [pltpu.VMEM((tall, width), BF16), *depth_scratch, pltpu.VMEM((24, width), F32)], 10,
        )(scal, nf, reduced, above, below, got, cnt, par, w2[layer])
        got = share(stats)
        if layer == 0:
            late = from_cores(after(near, stats))
            w3.append(wide_weight(late[:, : r2 * blocks]))
            w1.append(late[:, r2 * blocks :].reshape(-1, width))
        per, field, tall_field, edge_one, edge_two = by_clip("hidden")
        z2, u2, h2, stats, gram, vec2 = call(
            functools.partial(hidden_kernel, dims, layer, per), clips // per,
            [smem(), smem(), field, full(two), full((peers, 1, LANE)),
             full((64, width)), full((width, wide))],
            [field, field, field, full(three), full((width + 8, width)), full(vec)],
            [narrow(BF16), narrow(BF16), narrow(BF16), flat(*three), flat(width + 8, width),
             flat(*vec)],
            [pltpu.VMEM((8, width), F32)], 5,
        )(scal, nf, spatial, got, cnt, par, w3[layer])
        got = share(stats)
        if layer == 0:
            near = from_chips(after(jnp.concatenate([wide_rows[1], w_mix[1]], axis=0), got))
        norm_specs = [full(three), full((peers, 1, LANE)), full((peers, LANE)),
                      full((4, wide)), full((width, wide))]
        norm_args = (got, cnt, rinv, pout, w3[layer])
        if layer == 0:
            carried, slope, reduced, up, dn, stats, vec3 = call(
                functools.partial(join_kernel, dims, lines), steps,
                [smem(), smem(), broad, thin] + norm_specs + [full((wide, width))],
                [broad, broad, thin, full(edge.shape), full(edge.shape), full(two),
                 full(vec_wide)],
                [wide_shape, wide_shape, narrow(F32), edge, edge, flat(*two), flat(*vec_wide)],
                [pltpu.VMEM((2, lines * line, 256), F32), pltpu.VMEM((24, width), F32)], 12,
            )(scal, nf, x, h2, *norm_args, w1[1])
        else:
            cot = cotangent.transpose(0, 2, 3, 1, 4).reshape(voxels // frames, frames, wide)
            output, gs, low, t, sums, vec3 = call(
                functools.partial(out_kernel, dims, lines), steps,
                [smem(), smem(), broad, thin, native] + norm_specs,
                [native, broad, thin, full((width, wide)), full(many), full(vec_wide)],
                [native_shape, wide_shape, narrow(F32), flat(width, wide), struct(many, BF16),
                 flat(*vec_wide)],
                [pltpu.VMEM((2, lines * line, 256), F32), pltpu.VMEM((width, wide), BF16),
                 pltpu.VMEM((8, wide), F32)], 15,
            )(scal, nf, carried, h2, cot, *norm_args)
        stored.append((z1, u1, h1, vec1, mixed, z2, u2, h2, vec2, gram, vec3))

    def voxel_form(value):
        return value.reshape(clips, rows, columns, frames, wide).transpose(0, 3, 1, 2, 4)

    def by_owner(g_mix, g_depth):
        g_depth = g_depth.astype(BF16).T.reshape(peers, r4, 32)
        g_depth = jnp.pad(g_depth, ((0, 0), (0, 0), (0, width - 32)))
        return [g_mix.astype(BF16).reshape(peers, -1, width), g_depth]

    def expand_by_owner(g_expand):
        one = g_expand.reshape(peers, r2, blocks, width).transpose(0, 2, 1, 3)
        return one.reshape(peers, r2 * blocks, width)

    def sum_cores(pieces):
        packed = jnp.concatenate(pieces, axis=1).reshape(chips, inner, -1, width)
        mine = lax.dynamic_index_in_dim(packed, part, 1, keepdims=False)
        for k in range(1, inner):
            to = lax.rem(part + k, inner)
            sent = lax.dynamic_index_in_dim(packed, to, 1, keepdims=False)
            mine = mine + lax.ppermute(
                sent, "inner", [(i, (i + k) % inner) for i in range(inner)]
            )
        return mine

    results = [None, None]
    for layer in (1, 0):
        z1, u1, h1, vec1, mixed, z2, u2, h2, vec2, gram, vec3 = stored[layer]
        if layer == 0:
            sums = after(sums, first)
        got = share(sums)
        if layer == 0:
            got = after(got, g_reduce)
        per, field, tall_field, edge_one, edge_two = by_clip("expand")
        go2, up, dn, sums, g_expand, tot3 = call(
            functools.partial(expand_back_kernel, dims, per), clips // per,
            [smem(), smem(), field, field, field, field, full(many), full(vec_wide),
             full((width, wide)), full((width + 8, width)), full((width, wide))],
            [field, edge_two, edge_two, full(two), full((width, wide)), full((1, 2 * wide))],
            [narrow(BF16), pair, pair, flat(*two), struct((width, wide), BF16),
             flat(1, 2 * wide)],
            [pltpu.VMEM((width, width), BF16), pltpu.VMEM(vec, F32),
             pltpu.VMEM((per * per_clip, width), F32), pltpu.VMEM((16, width), F32)], 6,
        )(scal, nf, low, h2, z2, u2, got, vec3, t, gram, w3[layer])
        above, below = neighbours(up, dn)
        got = share(sums)
        if layer == 1:
            g_expand_1 = g_expand
        else:
            pieces = [after(g_reduce, sums).reshape(peers, -1, width), expand_by_owner(g_expand)]
            second = lax.all_to_all(sum_cores(pieces), CHIPS, 0, 0)
        per, field, tall_field, edge_one, edge_two = by_clip("depth")
        go1, sums, gm, gp, tot2 = call(
            functools.partial(depth_back_kernel, dims, layer, per), clips // per,
            [smem(), smem(), field, edge_two, edge_two, field, full(two), full(vec), field,
             field, full((64, width)), full((width, width))],
            [field, full(two), field, field, full((1, 2 * width))],
            [narrow(BF16), flat(*two), narrow(BF16), narrow(BF16), flat(1, 2 * width)],
            [*depth_scratch, pltpu.VMEM((per_clip, width), F32), pltpu.VMEM(vec, F32),
             pltpu.VMEM((16, width), F32)], 12,
        )(scal, nf, go2, above, below, z2, got, vec2, z1, u1, par, w2[layer])
        if layer == 0:
            sums = after(sums, second)
        got = share(sums)
        per, field, tall_field, edge_one, edge_two = by_clip("grads")
        g_mix, g_depth = call(
            functools.partial(kernel_grads, dims, per), clips // per,
            [tall_field, field, field, field],
            [full((width, width)), full((32, width))],
            [flat(width, width), flat(32, width)],
            [pltpu.VMEM((3, tall, width), BF16),
             pltpu.VMEM((width // LANE, per_clip, 2 * LANE), BF16),
             pltpu.VMEM((width // LANE, 2 * LANE, 9 * LANE), F32),
             pltpu.VMEM((9, 8, width), F32)], 12,
        )(mixed, gp, gm, h1)
        if layer == 1:
            got, g_mix, g_depth = lax.optimization_barrier((got, g_mix, g_depth))
            pieces = [*by_owner(g_mix, g_depth), expand_by_owner(g_expand_1)]
            first = lax.all_to_all(sum_cores(pieces), CHIPS, 0, 0)
        else:
            rest = sum_cores(by_owner(g_mix, g_depth))
            got = after(got, rest)
        if layer == 1:
            h2_0, vec3_0 = stored[0][7], stored[0][10]
            gs, low, t, sums, gr, tot1 = call(
                functools.partial(cross_kernel, dims, lines), steps,
                [smem(), smem(), thin, thin, full(two), full(vec), broad, broad, thin,
                 full(vec_wide), full((wide, width)), full((width, wide))],
                [broad, thin, full((width, wide)), full(many), thin, full((1, 2 * width))],
                [wide_shape, narrow(F32), flat(width, wide), struct(many, BF16), narrow(BF16),
                 flat(1, 2 * width)],
                [pltpu.VMEM((2, lines * line, 256), F32), pltpu.VMEM((wide, width), BF16),
                 pltpu.VMEM((width, wide), BF16), pltpu.VMEM(vec, F32),
                 pltpu.VMEM((8, wide), F32)], 15,
            )(scal, nf, go1, z1, got, vec1, gs, slope, h2_0, vec3_0, w1[1], w3[0])
            g_reduce = call(
                functools.partial(reduce_grad_kernel, 2.0), steps,
                [broad, thin], full((wide, width)), struct((wide, width), BF16),
                [pltpu.VMEM((width, wide), F32)], 5,
            )(carried, gr)
        else:
            gr, mine, sent, tot1 = call(
                functools.partial(last_grad_kernel, dims, lines), steps,
                [smem(), smem(), thin, thin, full(two), full(vec), broad],
                [thin, full((chips, r1, width)), full((chips, r1, width)), full((1, 2 * width))],
                [narrow(BF16), struct((chips, r1, width), BF16), struct((chips, r1, width), BF16),
                 flat(1, 2 * width)],
                [pltpu.VMEM(vec, F32), pltpu.VMEM((width, wide), F32)], 6,
            )(scal, nf, go1, z1, got, vec1, x)
            input_grad = call(
                input_kernel, steps, [thin, broad, full((peers, r1, width))], native,
                native_shape, [], 6,
            )(gr, gs, early)
        results[layer] = (tot1, tot2, tot3)

    last = jnp.concatenate([mine + swap(sent), rest], axis=1)
    last = jnp.sum(lax.all_to_all(last, CHIPS, 0, 0).astype(F32), axis=0)
    first = jnp.sum(first.astype(F32), axis=0)
    second = jnp.sum(second.astype(F32), axis=0)
    to_wide = lambda one: one.reshape(blocks, r2, width).transpose(1, 0, 2).reshape(r2, wide)
    grad_reduce = jnp.stack([last[0:r1], second[0:r1]])
    grad_mix = jnp.stack([last[r1 : r1 + r2], first[0:r2]])
    depths = (last[r1 + r2 :], first[r2 : r2 + r4])
    grad_depth = jnp.stack([one[:, 0:27].T for one in depths])
    grad_expand = jnp.stack([to_wide(second[r1:]), to_wide(first[r2 + r4 :])])

    mid_sums = jnp.concatenate(
        [
            jnp.concatenate([results[layer][0], results[layer][1]], axis=0).reshape(2, 2, width)
            for layer in range(2)
        ],
        axis=0,
    )
    mid = lax.dynamic_slice_in_dim(mid_sums, place * r4, r4, axis=2)
    out_sums = jnp.concatenate([results[layer][2].reshape(1, 2, wide) for layer in range(2)])
    r6 = gains_out.shape[1]
    outs = lax.dynamic_slice_in_dim(out_sums, place * r6, r6, axis=2)

    return (
        voxel_form(output),
        voxel_form(input_grad),
        grad_reduce,
        grad_mix,
        grad_expand,
        grad_depth,
        mid[:, 1].reshape(2, 2, r4),
        mid[:, 0].reshape(2, 2, r4),
        outs[:, 1],
        outs[:, 0],
    )


def solution(mesh):
    clip_size, sp_size = mesh.shape["clip"], mesh.shape["sp"]
    inner = 2 if sp_size % 2 == 0 else 1
    divided = Mesh(mesh.devices.reshape(clip_size, sp_size // inner, inner), ALL)
    activations = P("clip", None, SP, None, None)
    middle, last, vectors = P(None, ALL, None), P(None, None, ALL), P(None, ALL)
    return jax.shard_map(
        on_device,
        mesh=divided,
        in_specs=(
            activations, P(), activations, middle, middle, middle, last, last, last, vectors,
            vectors,
        ),
        out_specs=(
            activations, activations, middle, middle, middle, last, last, last, vectors, vectors,
        ),
        check_vma=False,
    )
```

```python
import functools

import jax
import jax.numpy as jnp
from jax import lax
from jax.experimental import pallas as pl
from jax.experimental.pallas import tpu as pltpu
from jax.sharding import Mesh, PartitionSpec as P

epsilon = 1e-05
F32 = jnp.float32
BF16 = jnp.bfloat16
LANE = 128
STEP = 16
COST = 3.0e6
PER = {"mix": 1, "hidden": 4, "expand": 2, "depth": 1, "grads": 1}


def dot_nn(left, right):
    return lax.dot_general(left, right, (((1,), (0,)), ((), ())), preferred_element_type=F32)


def dot_nt(left, right):
    return lax.dot_general(left, right, (((1,), (1,)), ((), ())), preferred_element_type=F32)


def dot_tn(left, right):
    return lax.dot_general(left, right, (((0,), (0,)), ((), ())), preferred_element_type=F32)


def split(value):
    high = value.astype(BF16)
    return high, (value - high.astype(F32)).astype(BF16)


def dot_split(left, right):
    high, rest = split(left)
    return dot_nn(high, right) + dot_nn(rest, right)


def fold(value):
    return jnp.sum(value.reshape(-1, 8, value.shape[-1]), axis=0)


def row_sum(value):
    return jnp.sum(value, axis=0, keepdims=True)


def live_rows(count, frames, rows, width):
    at = lax.rem(lax.broadcasted_iota(jnp.int32, (rows, width), 0), frames)
    return jnp.where(at < count, 1.0, 0.0)


def live_cap(count, frames, rows, width):
    return jnp.where(live_rows(count, frames, rows, width) > 0.5, 3e38, -60.0)


def full(shape):
    return pl.BlockSpec(shape, lambda *_: (0,) * len(shape))


def smem():
    return pl.BlockSpec(memory_space=pltpu.SMEM)


def call(body, steps, in_specs, out_specs, out_shape, scratch, micros, room=58):
    return pl.pallas_call(
        body,
        grid=(steps,),
        in_specs=in_specs,
        out_specs=out_specs,
        out_shape=out_shape,
        scratch_shapes=scratch,
        cost_estimate=pl.CostEstimate(
            flops=0, transcendentals=0, bytes_accessed=int(micros * COST)
        ),
        compiler_params=pltpu.CompilerParams(
            dimension_semantics=("arbitrary",), vmem_limit_bytes=room * 2**20
        ),
    )


def each(count, body, unroll=1):
    def step(i, carry):
        body(pl.multiple_of(i * STEP, STEP))
        return carry

    lax.fori_loop(0, count // STEP, step, 0, unroll=unroll)


def clip_loop(dims, per, body):
    frames, rows, line = dims
    size = rows * line
    step = pl.program_id(0)

    def one(k, carry):
        def view(ref, extra=0):
            length = size + extra * line
            return ref.at[pl.ds(pl.multiple_of(k * length, STEP), length), :]

        body(step * per + k, k, view)
        return carry

    lax.fori_loop(0, per, one, 0)


def merge_stats(means, squares, counts, total):
    mean = jnp.sum(means * counts, axis=0) / total
    away = means - mean[None]
    spread = jnp.sum(squares + counts * away * away, axis=0) / total
    return mean, lax.rsqrt(spread + epsilon)


def narrow_norm(nf, got_ref, cnt_ref, gain, bias, vec_ref):
    width = vec_ref.shape[1]
    mean, inverse = merge_stats(
        got_ref[:, :, 0:width], got_ref[:, :, width:], cnt_ref[:, :, 0:1], nf[1]
    )
    scale = gain * inverse
    vec_ref[...] = jnp.zeros_like(vec_ref)
    vec_ref[0:1, :] = inverse
    vec_ref[1:2, :] = -mean * inverse
    vec_ref[2:3, :] = 0.5 * scale
    vec_ref[3:4, :] = 0.5 * (bias - mean * scale)
    vec_ref[4:5, :] = scale


def silu_half(half):
    both = jnp.tanh(half) + 1.0
    return half * both, both


def slope_of(value, both):
    return 0.5 * slope_twice(value, both)


def slope_twice(value, both):
    return both + value * (2.0 - both)


def line_stats(nf, scal, dims, read, lines, first_line, is_first, acc, st_ref):
    frames, rows, line = dims
    width = acc.shape[1]

    @pl.when(is_first)
    def _():
        mask = live_rows(scal[0], frames, STEP, width)
        total = jnp.zeros((8, width), F32)
        for i in range(line // STEP):
            total = total + fold(read(0, i * STEP) * mask)
        acc[...] = jnp.zeros_like(acc)
        alive = (scal[0] * (line // frames)).astype(F32)
        acc[0:1, :] = row_sum(total) / alive

    pivot = acc[0:1, :]

    def one(at, carry):
        plain, square = carry
        mask = live_rows(scal[(first_line + at) // rows], frames, STEP, width)
        for i in range(line // STEP):
            away = (read(at, i * STEP) - pivot) * mask
            plain = plain + fold(away)
            square = square + fold(away * away)
        return plain, square

    zero = jnp.zeros((8, width), F32)
    plain, square = lax.fori_loop(0, lines, one, (zero, zero), unroll=True)
    acc[8:16, :] += plain
    acc[16:24, :] += square


def edge_places(scal, clips, line, rows):
    last = line * (rows + 1)
    near = jnp.where(scal[scal.shape[0] - 1] == 0, last, 0)
    return pl.multiple_of(near, STEP), pl.multiple_of(last - near, STEP)


def hand_over(scal, value, mine_ref, sent_ref):
    even = scal[scal.shape[0] - 1] == 0
    other = value.shape[1] - 1
    mine_ref[...] = jnp.where(even, value[:, 0], value[:, other]).astype(BF16)
    sent_ref[...] = jnp.where(even, value[:, other], value[:, 0]).astype(BF16)


def finish_stats(nf, acc, st_ref):
    plain, square = row_sum(acc[8:16, :]), row_sum(acc[16:24, :])
    width = acc.shape[1]
    peers = st_ref.shape[0]
    st_ref[:, :, 0:width] = jnp.broadcast_to(acc[0:1, :] + plain * nf[2], (peers, 1, width))
    spread = square - plain * plain * nf[2]
    st_ref[:, :, width:] = jnp.broadcast_to(spread, (peers, 1, width))


def share_sums(acc, sum_ref):
    width = acc.shape[1]
    peers = sum_ref.shape[0]
    for k in range(2):
        one = row_sum(acc[8 * k : 8 * k + 8, :])
        sum_ref[:, :, width * k : width * (k + 1)] = jnp.broadcast_to(one, (peers, 1, width))


def depth_weights(par_ref, layer, wd, flip):
    one = lax.broadcasted_iota(jnp.int32, (LANE, LANE), 0)
    two = lax.broadcasted_iota(jnp.int32, (LANE, LANE), 1)
    eye = jnp.where(one == two, 1.0, 0.0)
    for half in range(wd.shape[0]):
        for i in range(9):
            for e in (0, 2):
                tap = 3 * i + e
                at = 27 * layer + (26 - tap if flip else tap)
                row = par_ref[at : at + 1, LANE * half : LANE * (half + 1)]
                k = LANE * (e // 2)
                wd[half, LANE * i : LANE * (i + 1), k : k + LANE] = (eye * row).astype(BF16)


def frame_moves(frames, value):
    here = lax.rem(lax.broadcasted_iota(jnp.int32, value.shape, 0), frames)
    onward = jnp.where(here > 0, pltpu.roll(value, 1, 0), 0.0)
    back = jnp.where(here < frames - 1, pltpu.roll(value, value.shape[0] - 1, 0), 0.0)
    return onward, back


def frame_shifts(dims, value, tv, at):
    onward, back = frame_moves(dims[0], value)
    part = pl.ds(at, value.shape[0])
    tv[0, part, :] = onward.astype(BF16)
    tv[1, part, :] = value.astype(BF16)
    tv[2, part, :] = back.astype(BF16)


def column_moves(dims, value):
    frames, rows, line = dims
    at = lax.broadcasted_iota(jnp.int32, value.shape, 0)
    onward = jnp.where(at >= frames, pltpu.roll(value, frames, 0), 0.0)
    back = jnp.where(at < line - frames, pltpu.roll(value, line - frames, 0), 0.0)
    return onward, back


def depth_sum(dims, layer, flip, par_ref, ms, tv, wd, ds, temp, store):
    frames, rows, line = dims
    halves = wd.shape[0]
    piece = line // 2 if line % (2 * 8) == 0 else line
    for half in range(halves):
        lanes = slice(LANE * half, LANE * (half + 1))
        views = [tv[a, line * b : line * (b + rows), lanes] for a in range(3) for b in range(3)]
        ds[half] = dot_nn(jnp.concatenate(views, axis=1), wd[half])
        taps = []
        for i in range(9):
            tap = 3 * i + 1
            at = 27 * layer + (26 - tap if flip else tap)
            taps.append(par_ref[at : at + 1, lanes])
        for start in range(0, rows * line, piece):
            seen = [ms[start + line * b : start + line * b + piece, lanes] for b in range(3)]
            sums = []
            for a in range(3):
                one = seen[0] * taps[3 * a]
                one = one + seen[1] * taps[3 * a + 1]
                sums.append(one + seen[2] * taps[3 * a + 2])
            onward, _ = frame_moves(frames, sums[0])
            _, back = frame_moves(frames, sums[2])
            temp[start : start + piece, lanes] = onward + sums[1] + back
    for half in range(halves):
        lanes = slice(LANE * half, LANE * (half + 1))
        for r in range(rows):
            part = slice(line * r, line * (r + 1))
            onward, _ = column_moves(dims, ds[half, part, 0:LANE])
            _, back = column_moves(dims, ds[half, part, LANE : 2 * LANE])
            store(r, lanes, onward + temp[part, lanes] + back)


def pack_kernel(wr_ref, wm_ref, wd_ref, gm_ref, bm_ref, go_ref, bo_ref, out_ref):
    r1, width = wr_ref.shape[1:]
    r2 = wm_ref.shape[1]
    r4, taps = wd_ref.shape[1:]
    r6 = go_ref.shape[1]
    zeros = lambda rows, size: jnp.zeros((rows, size), F32)
    part = [wd_ref[k].astype(F32) for k in range(2)]
    if r4 < 8:
        part = [jnp.concatenate([one, zeros(8 - r4, taps)], axis=0) for one in part]
    pad = zeros(8, 32 - taps)
    mids = [gm_ref[k].astype(F32) for k in range(2)] + [bm_ref[k].astype(F32) for k in range(2)]
    mids = jnp.concatenate(mids, axis=0)
    outs = jnp.concatenate([go_ref[...].astype(F32), bo_ref[...].astype(F32)], axis=0)
    mids = jnp.concatenate([mids, zeros(8, 32 - r4)], axis=1)
    outs = jnp.concatenate([outs, zeros(4, r6)], axis=0)
    small = [part[0], pad, part[1], pad, mids, outs]
    small.append(zeros(8, width - 96 - r6))
    rest = out_ref.shape[1] - r1 - r2 - 8
    rows = [wr_ref[0].astype(F32), wm_ref[0].astype(F32), jnp.concatenate(small, axis=1)]
    if rest:
        rows.append(zeros(rest, width))
    block = jnp.concatenate(rows, axis=0).astype(BF16)
    for k in range(out_ref.shape[0]):
        out_ref[k] = block


def first_kernel(dims, lines, scal, nf, x_ref, w_ref, red_ref, up_ref, dn_ref, st_ref, acc, lines_kept):
    step = pl.program_id(0)
    x = x_ref[...].reshape(-1, x_ref.shape[2])
    red_ref[...] = dot_nn(x, w_ref[...].reshape(-1, w_ref.shape[2]))
    reduced_tail(dims, lines, step, scal, nf, red_ref, up_ref, dn_ref, st_ref, acc, lines_kept)


def reduced_tail(dims, lines, step, scal, nf, red_ref, up_ref, dn_ref, st_ref, acc, lines_kept):
    frames, rows, line = dims
    read = lambda at, i: red_ref[pl.ds(pl.multiple_of(line * at, STEP) + i, STEP), :]
    line_stats(nf, scal, dims, read, lines, step * lines, step == 0, acc, st_ref)
    for k in range(lines // rows):
        clip, at = step * (lines // rows) + k, k * rows * line
        even = scal[scal.shape[0] - 1] == 0
        last = line * (rows - 1)
        near = jnp.where(even, last, 0)
        for way, start in enumerate((near, last - near)):
            part = pl.ds(pl.multiple_of(at + start, STEP), line)
            lines_kept[way, clip] = red_ref[part, :]

    @pl.when(step == pl.num_programs(0) - 1)
    def _():
        finish_stats(nf, acc, st_ref)
        mean = acc[0:1, :] + row_sum(acc[8:16, :]) * nf[2]
        for at in range(up_ref.shape[0]):
            up_ref[at] = (lines_kept[0, at] - mean).astype(BF16)
            dn_ref[at] = (lines_kept[1, at] - mean).astype(BF16)


def mix_kernel(
    dims, layer, per, scal, nf, red_ref, up_ref, dn_ref, got_ref, cnt_ref, par_ref, w_ref,
    mix_ref, spa_ref, z_ref, u_ref, h_ref, st_ref, vec_ref, hs, ms, tv, wd, ds, acc,
):
    step, last = pl.program_id(0), pl.num_programs(0) - 1
    width = w_ref.shape[0]

    @pl.when(step == 0)
    def _():
        at = 2 * layer
        narrow_norm(
            nf, got_ref, cnt_ref, par_ref[54 + at : 55 + at, :], par_ref[58 + at : 59 + at, :],
            vec_ref,
        )
        for k in range(2):
            mean = got_ref[scal[scal.shape[0] - 3 + k], :, 0:width]
            vec_ref[5 + k : 6 + k, :] = vec_ref[3:4, :] + vec_ref[2:3, :] * mean
        depth_weights(par_ref, layer, wd, False)

    def body(clip, k, view):
        mix_clip(
            dims, layer, scal, nf, view(red_ref), up_ref.at[k], dn_ref.at[k], par_ref, w_ref,
            view(mix_ref, 2), view(spa_ref), view(z_ref), view(u_ref), view(h_ref), st_ref,
            vec_ref, hs, ms, tv, wd, ds, acc, clip, per * (last + 1),
        )

    clip_loop(dims, per, body)

    @pl.when(step == last)
    def _():
        finish_stats(nf, acc, st_ref)


def mix_clip(
    dims, layer, scal, nf, red_ref, up_ref, dn_ref, par_ref, w_ref, mix_ref, spa_ref, z_ref,
    u_ref, h_ref, st_ref, vec_ref, hs, ms, tv, wd, ds, acc, clip, clips,
):
    frames, rows, line = dims
    width = w_ref.shape[0]
    mask = live_rows(scal[clip], frames, STEP, width)
    near = mask * scal[clips].astype(F32)
    far = mask * scal[clips + 1].astype(F32)
    near_at, far_at = edge_places(scal, clips, line, rows)

    def edge(i):
        h, _ = silu_half(up_ref[pl.ds(i, STEP), :].astype(F32) * vec_ref[2:3, :] + vec_ref[5:6, :])
        hs[pl.ds(near_at + i, STEP), :] = (h * near).astype(BF16)
        h, _ = silu_half(dn_ref[pl.ds(i, STEP), :].astype(F32) * vec_ref[2:3, :] + vec_ref[6:7, :])
        hs[pl.ds(far_at + i, STEP), :] = (h * far).astype(BF16)

    each(line, edge, 7)

    def own(i):
        value = red_ref[pl.ds(i, STEP), :]
        h, both = silu_half(value * vec_ref[2:3, :] + vec_ref[3:4, :])
        low = (h * mask).astype(BF16)
        hs[pl.ds(i + line, STEP), :] = low
        h_ref[pl.ds(i, STEP), :] = low
        u_ref[pl.ds(i, STEP), :] = (slope_of(h, both) * mask).astype(BF16)
        z_ref[pl.ds(i, STEP), :] = (value * vec_ref[0:1, :] + vec_ref[1:2, :]).astype(BF16)

    each(line * rows, own, 49)
    ms[...] = dot_nn(hs[...], w_ref[...])

    def shifts(r, carry):
        at = pl.multiple_of(r * line, STEP)
        for half in range(width // LANE):
            lanes = slice(LANE * half, LANE * (half + 1))
            part = pl.ds(at, line)
            value = ms[part, lanes].astype(BF16).astype(F32)
            ms[part, lanes] = value
            frame_shifts(dims, value, tv.at[:, :, lanes], at)
        return carry

    lax.fori_loop(0, rows + 2, shifts, 0, unroll=True)
    mix_ref[...] = tv[1]

    def store(r, lanes, value):
        spa_ref[line * r : line * (r + 1), lanes] = value

    depth_sum(dims, layer, False, par_ref, ms, tv, wd, ds, spa_ref, store)
    read = lambda at, i: spa_ref[pl.ds(pl.multiple_of(line * at, STEP) + i, STEP), :]
    line_stats(nf, scal, dims, read, rows, clip * rows, clip == 0, acc, st_ref)

def hidden_rows(i, mask, spa_ref, h_ref, u_ref, z_ref, vec_ref, acc):
    part = pl.ds(i, STEP)
    value = spa_ref[part, :]
    h, both = silu_half(value * vec_ref[2:3, :] + vec_ref[3:4, :])
    low = (h * mask).astype(BF16)
    h_ref[part, :] = low
    u_ref[part, :] = (slope_of(h, both) * mask).astype(BF16)
    z_ref[part, :] = (value * vec_ref[0:1, :] + vec_ref[1:2, :]).astype(BF16)
    acc[...] += fold(low.astype(F32))


def hidden_kernel(
    dims, layer, per, scal, nf, spa_ref, got_ref, cnt_ref, par_ref, w_ref,
    z_ref, u_ref, h_ref, st_ref, gram_ref, vec_ref, acc,
):
    frames, rows, line = dims
    step = pl.program_id(0)
    width = par_ref.shape[1]

    @pl.when(step == 0)
    def _():
        at = 2 * layer
        narrow_norm(
            nf, got_ref, cnt_ref, par_ref[55 + at : 56 + at, :], par_ref[59 + at : 60 + at, :],
            vec_ref,
        )
        gram_ref[...] = jnp.zeros_like(gram_ref)
        acc[...] = jnp.zeros_like(acc)

    def body(clip, k, view):
        mask = live_rows(scal[clip], frames, STEP, width)
        spa, h_out, u_out, z_out = view(spa_ref), view(h_ref), view(u_ref), view(z_ref)

        def own(i):
            hidden_rows(i, mask, spa, h_out, u_out, z_out, vec_ref, acc)

        each(line * rows, own, 49)

    clip_loop(dims, per, body)
    gram_ref[0:width, :] += dot_tn(h_ref[...], h_ref[...])

    @pl.when(step == pl.num_programs(0) - 1)
    def _():
        total = row_sum(acc[...])
        gram_ref[width : width + 8, :] = jnp.broadcast_to(total, (8, width))
        across = jnp.broadcast_to(total, (width, width))
        centered = gram_ref[0:width, :] - across.T * across * nf[2]
        spread = row_sum(dot_split(centered, w_ref[...]) * w_ref[...].astype(F32))
        peers = st_ref.shape[0]
        st_ref[:, :, 0:width] = jnp.broadcast_to(total, (peers, 1, width))
        st_ref[:, :, width:] = jnp.broadcast_to(spread, (peers, 1, spread.shape[1]))


def wide_norm(nf, got_ref, cnt_ref, rinv_ref, pout_ref, layer, w_ref, vec_ref):
    width = w_ref.shape[0]
    hidden_means = got_ref[:, 0, 0:width] * rinv_ref[:, 0:1]
    means = dot_split(hidden_means, w_ref[...])
    counts = cnt_ref[:, 0, 0:1]
    mean = row_sum(means * counts) / nf[1]
    away = means - mean
    spread = row_sum(got_ref[:, 0, width:] + counts * away * away) / nf[1]
    inverse = lax.rsqrt(spread + epsilon)
    scale = pout_ref[layer : layer + 1, :] * inverse
    vec_ref[...] = jnp.zeros_like(vec_ref)
    vec_ref[0:1, :] = scale
    vec_ref[1:2, :] = 0.5 * (pout_ref[2 + layer : 3 + layer, :] - mean * scale)
    vec_ref[2:3, :] = inverse
    vec_ref[3:4, :] = mean
    vec_ref[4:5, :] = 0.5 * scale


def each_line(dims, lines, step, scal, width, body, make=live_cap):
    frames, rows, line = dims

    def run(carry):
        for at in range(lines):
            mask = make(scal[(step * lines + at) // rows], frames, STEP, width)
            for i in range(at * line, (at + 1) * line, STEP):
                carry = body(slice(i, i + STEP), mask, carry)
        return carry

    return run


def join_kernel(
    dims, lines, scal, nf, x_ref, h_ref, got_ref, cnt_ref, rinv_ref, pout_ref, w3_ref, w1_ref,
    next_ref, du_ref, red_ref, up_ref, dn_ref, st_ref, vec_ref, es, acc, lines_kept,
):
    step = pl.program_id(0)
    wide, width = w1_ref.shape
    frames = dims[0]
    block = 256

    @pl.when(step == 0)
    def _():
        wide_norm(nf, got_ref, cnt_ref, rinv_ref, pout_ref, 0, w3_ref, vec_ref)

    for j in range(wide // block):
        lanes = slice(block * j, block * (j + 1))
        es[j % 2] = dot_nn(h_ref[...], w3_ref[:, lanes])
        scale, shift = vec_ref[4:5, lanes], vec_ref[1:2, lanes]

        def own(part, cap, carry):
            spot = slice(part.start // frames, part.stop // frames)
            x = x_ref[spot, :, lanes].reshape(-1, block).astype(F32)
            half = x * 0.5 + (es[j % 2, part, :] * scale + shift)
            o, both = silu_half(jnp.minimum(half, cap))
            next_ref[part, lanes] = (0.5 * o).astype(BF16)
            du_ref[part, lanes] = slope_twice(o, both).astype(BF16)
            return carry

        each_line(dims, lines, step, scal, block, own)(0)
    red_ref[...] = 2.0 * dot_nn(next_ref[...], w1_ref[...])
    reduced_tail(dims, lines, step, scal, nf, red_ref, up_ref, dn_ref, st_ref, acc, lines_kept)


def wide_tail(hT, gs_ref, w3s, low_ref, t_ref):
    t_ref[...] += dot_nn(hT, gs_ref[...])
    low_ref[...] = dot_nt(gs_ref[...], w3s[...])


def wide_sums(w3_ref, t_ref, sacc, vec_ref, sum_ref, unit):
    wide = w3_ref.shape[1]
    t_ref[...] = unit * t_ref[...]
    plain = unit * row_sum(sacc[...])
    along = row_sum(w3_ref[...].astype(F32) * t_ref[...])
    along = (along - vec_ref[3:4, :] * plain) * vec_ref[2:3, :]
    pieces = [
        one[:, LANE * k : LANE * (k + 1)] for one in (plain, along) for k in range(wide // LANE)
    ]
    sum_ref[...] = jnp.broadcast_to(jnp.concatenate(pieces, axis=0)[None], sum_ref.shape).astype(
        BF16
    )


def out_kernel(
    dims, lines, scal, nf, x_ref, h_ref, cot_ref, got_ref, cnt_ref, rinv_ref, pout_ref, w3_ref,
    out_ref, gs_ref, low_ref, t_ref, sum_ref, vec_ref, es, w3s, sacc,
):
    step = pl.program_id(0)
    width, wide = w3_ref.shape
    frames = dims[0]
    block = 256
    unit = 0.5

    @pl.when(step == 0)
    def _():
        wide_norm(nf, got_ref, cnt_ref, rinv_ref, pout_ref, 1, w3_ref, vec_ref)
        t_ref[...] = jnp.zeros_like(t_ref)
        sacc[...] = jnp.zeros_like(sacc)
        w3s[...] = (w3_ref[...].astype(F32) * (unit * vec_ref[0:1, :])).astype(BF16)

    hT = h_ref[...].T
    for j in range(wide // block):
        lanes = slice(block * j, block * (j + 1))
        es[j % 2] = dot_nn(h_ref[...], w3_ref[:, lanes])
        scale, shift = vec_ref[4:5, lanes], vec_ref[1:2, lanes]

        def own(part, cap, total):
            half = x_ref[part, lanes].astype(F32) + (es[j % 2, part, :] * scale + shift)
            o, both = silu_half(jnp.minimum(half, cap))
            spot = slice(part.start // frames, part.stop // frames)
            out_ref[spot, :, lanes] = o.astype(BF16).reshape(-1, frames, block)
            grad = cot_ref[spot, :, lanes].reshape(-1, block).astype(F32)
            grad = grad * slope_twice(o, both)
            gs_ref[part, lanes] = grad.astype(BF16)
            return total + fold(grad)

        total = each_line(dims, lines, step, scal, block, own)(jnp.zeros((8, block), F32))
        sacc[:, lanes] += total
    wide_tail(hT, gs_ref, w3s, low_ref, t_ref)

    @pl.when(step == pl.num_programs(0) - 1)
    def _():
        wide_sums(w3_ref, t_ref, sacc, vec_ref, sum_ref, unit)


def expand_back_kernel(
    dims, per, scal, nf, low_ref, h_ref, z_ref, u_ref, got_ref, vec_ref, w3_ref,
    go_ref, up_ref, dn_ref, sum_ref, tot_ref, ks, crow, hk, acc,
):
    frames, rows, line = dims
    step = pl.program_id(0)
    width, wide = w3_ref.shape

    @pl.when(step == 0)
    def _():
        totals = jnp.sum(got_ref[...].astype(F32), axis=0)
        count = wide // LANE
        plain = jnp.concatenate([totals[k : k + 1, :] for k in range(count)], axis=1)
        along = jnp.concatenate([totals[k : k + 1, :] for k in range(count, 2 * count)], axis=1)
        tot_ref[:, 0:wide] = plain
        tot_ref[:, wide:] = along
        w3 = w3_ref[...]
        rise, flat = wide_rows_of(nf, plain, along, vec_ref)
        ks[...] = dot_nt((w3.astype(F32) * rise).astype(BF16), w3).astype(BF16)
        spread = [jnp.broadcast_to(one, (16, wide)) for one in split(flat)]
        crow[...] = (dot_nt(spread[0], w3) + dot_nt(spread[1], w3))[0:8]
        acc[...] = jnp.zeros_like(acc)

    hk[...] = dot_nn(h_ref[...], ks[...])

    def own(i):
        part = pl.ds(i, STEP)
        grad = (low_ref[part, :] - crow[0:1, :] - hk[part, :]) * u_ref[part, :].astype(F32)
        go_ref[part, :] = grad.astype(BF16)
        acc[0:8, :] += fold(grad)
        acc[8:16, :] += fold(grad * z_ref[part, :].astype(F32))

    each(line * rows * per, own, 49)
    for k in range(per):
        expand_edges(dims, scal, k * rows * line, go_ref, z_ref, up_ref.at[k], dn_ref.at[k])

    @pl.when(step == pl.num_programs(0) - 1)
    def _():
        share_sums(acc, sum_ref)


def wide_rows_of(nf, plain, along, vec_ref):
    scale, inverse, mean = vec_ref[0:1, :], vec_ref[2:3, :], vec_ref[3:4, :]
    rise = scale * inverse * along * nf[3]
    return rise, scale * plain * nf[3] - rise * mean


def expand_grad_kernel(
    scal, nf, tot_ref, vec_ref, t_ref, gram_ref, w3_ref, mine_ref, sent_ref
):
    width, wide = w3_ref.shape
    rise, flat = wide_rows_of(nf, tot_ref[:, 0:wide], tot_ref[:, wide:], vec_ref)
    column = jnp.broadcast_to(gram_ref[width : width + 1, :], (LANE, width)).T[:, 0:1]
    cross = dot_split(gram_ref[0:width, :], w3_ref[...])
    ge = t_ref[...] * vec_ref[0:1, :] - column * flat - cross * rise
    chips, size = mine_ref.shape[0:2]
    parts = [ge[:, width * k : width * (k + 1)] for k in range(wide // width)]
    parts = [one.reshape(chips, -1, size * width // wide, width) for one in parts]
    hand_over(scal, jnp.concatenate(parts, axis=2), mine_ref, sent_ref)


def expand_edges(dims, scal, base, go_ref, z_ref, up_ref, dn_ref):
    frames, rows, line = dims
    even = scal[scal.shape[0] - 1] == 0
    last = line * (rows - 1)
    first = jnp.where(even, last, 0)
    near = pl.multiple_of(base + first, STEP)
    far = pl.multiple_of(base + last - first, STEP)
    up_ref[0] = go_ref[pl.ds(near, line), :]
    up_ref[1] = z_ref[pl.ds(near, line), :]
    dn_ref[0] = go_ref[pl.ds(far, line), :]
    dn_ref[1] = z_ref[pl.ds(far, line), :]


def norm_rows(nf, got_ref, vec_ref, tot_ref, rows3):
    width = vec_ref.shape[1]
    totals = jnp.sum(got_ref[...], axis=0)
    tot_ref[...] = totals
    rows3[0:1, :] = vec_ref[4:5, :]
    rows3[1:2, :] = vec_ref[4:5, :] * totals[:, 0:width] * nf[3]
    rows3[2:3, :] = vec_ref[4:5, :] * totals[:, width:] * nf[3]


def norm_back(rows3, go, z, mask):
    value = rows3[0:1, :] * go.astype(F32) - rows3[1:2, :] - rows3[2:3, :] * z.astype(F32)
    return value * mask


def depth_back_kernel(
    dims, layer, per, scal, nf, go_ref, above_ref, below_ref, z_ref, got_ref, vec_ref,
    z1_ref, u1_ref, par_ref, w_ref,
    go1_ref, sum_ref, gm_ref, gp_ref, tot_ref, ms, tv, wd, ds, gh, rows3, acc,
):
    step, last = pl.program_id(0), pl.num_programs(0) - 1
    width = w_ref.shape[0]

    @pl.when(step == 0)
    def _():
        norm_rows(nf, got_ref, vec_ref, tot_ref, rows3)
        depth_weights(par_ref, layer, wd, True)
        acc[...] = jnp.zeros_like(acc)

    def body(clip, k, view):
        depth_back_clip(
            dims, layer, scal, view(go_ref), above_ref.at[k], below_ref.at[k], view(z_ref),
            view(z1_ref), view(u1_ref), par_ref, w_ref, view(go1_ref), view(gm_ref), view(gp_ref),
            ms, tv, wd, ds, gh, rows3, acc, clip, per * (last + 1),
        )

    clip_loop(dims, per, body)

    @pl.when(step == last)
    def _():
        share_sums(acc, sum_ref)


def depth_back_clip(
    dims, layer, scal, go_ref, above_ref, below_ref, z_ref, z1_ref, u1_ref, par_ref, w_ref,
    go1_ref, gm_ref, gp_ref, ms, tv, wd, ds, gh, rows3, acc, clip, clips,
):
    frames, rows, line = dims
    width = w_ref.shape[0]
    mask = live_rows(scal[clip], frames, STEP, width)
    near = mask * scal[clips].astype(F32)
    far = mask * scal[clips + 1].astype(F32)
    near_at, far_at = edge_places(scal, clips, line, rows)

    def edge(i):
        part = pl.ds(i, STEP)
        ms[pl.ds(near_at + i, STEP), :] = norm_back(
            rows3, above_ref[0, part, :], above_ref[1, part, :], near
        )
        ms[pl.ds(far_at + i, STEP), :] = norm_back(
            rows3, below_ref[0, part, :], below_ref[1, part, :], far
        )

    each(line, edge, 7)

    def own(i):
        part = pl.ds(i, STEP)
        ms[pl.ds(i + line, STEP), :] = norm_back(rows3, go_ref[part, :], z_ref[part, :], mask)

    each(line * rows, own, 49)

    def shifts(r, carry):
        at = pl.multiple_of(r * line, STEP)
        for half in range(width // LANE):
            lanes = slice(LANE * half, LANE * (half + 1))
            part = pl.ds(at, line)
            value = ms[part, lanes].astype(BF16).astype(F32)
            ms[part, lanes] = value
            frame_shifts(dims, value, tv.at[:, :, lanes], at)
        return carry

    lax.fori_loop(0, rows + 2, shifts, 0, unroll=True)
    gp_ref[...] = tv[1, line : line * (rows + 1), :]

    def store(r, lanes, value):
        gm_ref[line * r : line * (r + 1), lanes] = value.astype(BF16)

    depth_sum(dims, layer, True, par_ref, ms, tv, wd, ds, gh, store)
    gh[...] = dot_nt(gm_ref[...], w_ref[...])

    def first(i):
        part = pl.ds(i, STEP)
        value = gh[part, :] * u1_ref[part, :].astype(F32)
        go1_ref[part, :] = value.astype(BF16)
        acc[0:8, :] += fold(value)
        acc[8:16, :] += fold(value * z1_ref[part, :].astype(F32))

    each(line * rows, first, 49)

def kernel_grads(
    dims, per, scal, mix_ref, gp_ref, gm_ref, h_ref,
    mine_ref, sent_ref, gmix_ref, gdep_ref, tv, mv, gacc, vacc,
):
    step = pl.program_id(0)
    width = h_ref.shape[1]
    halves = width // LANE

    @pl.when(step == 0)
    def _():
        gmix_ref[...] = jnp.zeros_like(gmix_ref)
        gacc[...] = jnp.zeros_like(gacc)
        vacc[...] = jnp.zeros_like(vacc)

    gmix_ref[...] += dot_tn(h_ref[...], gm_ref[...])

    def body(clip, k, view):
        kernel_clip(dims, halves, view(mix_ref, 2), view(gp_ref), tv, mv, gacc, vacc)

    clip_loop(dims, per, body)

    @pl.when(step == pl.num_programs(0) - 1)
    def _():
        one = lax.broadcasted_iota(jnp.int32, (LANE, LANE), 0)
        two = lax.broadcasted_iota(jnp.int32, (LANE, LANE), 1)
        gdep_ref[...] = jnp.zeros_like(gdep_ref)
        for half in range(halves):
            lanes = slice(LANE * half, LANE * (half + 1))
            for i in range(9):
                gdep_ref[3 * i + 1 : 3 * i + 2, lanes] = row_sum(vacc[i, :, lanes])
                for e in (0, 2):
                    k = LANE * (e // 2)
                    part = gacc[half, k : k + LANE, LANE * i : LANE * (i + 1)]
                    gdep_ref[3 * i + e : 3 * i + e + 1, lanes] = row_sum(
                        jnp.where(one == two, part, 0.0)
                    )
        chips, size = mine_ref.shape[0:2]
        taps = jnp.concatenate([gdep_ref[...].T, jnp.zeros((width, width - LANE), F32)], axis=1)
        parts = [gmix_ref[...], taps]
        parts = [one.reshape(chips, -1, size // 2, width) for one in parts]
        hand_over(scal, jnp.concatenate(parts, axis=2), mine_ref, sent_ref)


def kernel_clip(dims, halves, mix_ref, gp_ref, tv, mv, gacc, vacc):
    frames, rows, line = dims

    def shifts(r, carry):
        at = pl.multiple_of(r * line, STEP)
        for half in range(halves):
            lanes = slice(LANE * half, LANE * (half + 1))
            value = mix_ref[pl.ds(at, line), lanes].astype(F32)
            frame_shifts(dims, value, tv.at[:, :, lanes], at)
        return carry

    lax.fori_loop(0, rows + 2, shifts, 0, unroll=True)

    def moves(r, carry):
        at = pl.multiple_of(r * line, STEP)
        for half in range(halves):
            lanes = slice(LANE * half, LANE * (half + 1))
            value = gp_ref[pl.ds(at, line), lanes].astype(F32)
            onward, back = column_moves(dims, value)
            mv[half, pl.ds(at, line), 0:LANE] = back.astype(BF16)
            mv[half, pl.ds(at, line), LANE : 2 * LANE] = onward.astype(BF16)
        return carry

    lax.fori_loop(0, rows, moves, 0, unroll=True)
    for half in range(halves):
        lanes = slice(LANE * half, LANE * (half + 1))
        views = [tv[a, line * b : line * (b + rows), lanes] for a in range(3) for b in range(3)]
        gacc[half] += dot_tn(mv[half], jnp.concatenate(views, axis=1))
        sums = [vacc[i, :, lanes] for i in range(9)]
        for start in range(0, rows * line, line):
            own = gp_ref[start : start + line, lanes].astype(F32)
            onward, back = frame_moves(frames, own)
            for b in range(3):
                seen = mix_ref[start + line * b : start + line * b + line, lanes].astype(F32)
                for a, moved in enumerate((back, own, onward)):
                    sums[3 * a + b] = sums[3 * a + b] + fold(moved * seen)
        for i in range(9):
            vacc[i, :, lanes] = sums[i]


def reduced_grad(dims, lines, step, scal, go_ref, z_ref, rows3, gr_ref):
    def own(part, mask, carry):
        gr_ref[part, :] = norm_back(rows3, go_ref[part, :], z_ref[part, :], mask).astype(BF16)
        return carry

    each_line(dims, lines, step, scal, rows3.shape[1], own, live_rows)(0)


def cross_kernel(
    dims, lines, scal, nf, go_ref, z_ref, got_ref, vec1_ref, gs_ref, du_ref, h_ref,
    vec3_ref, w1_ref, w3_ref,
    gs0_ref, low_ref, t_ref, sum_ref, gr_ref, tot_ref, ds, w1s, w3s, rows3, sacc,
):
    step = pl.program_id(0)
    width, wide = w3_ref.shape
    block = 256
    unit = 0.25

    @pl.when(step == 0)
    def _():
        norm_rows(nf, got_ref, vec1_ref, tot_ref, rows3)
        t_ref[...] = jnp.zeros_like(t_ref)
        sacc[...] = jnp.zeros_like(sacc)
        w3s[...] = (w3_ref[...].astype(F32) * (unit * vec3_ref[0:1, :])).astype(BF16)
        w1s[...] = (w1_ref[...].astype(F32) * 2.0).astype(BF16)

    reduced_grad(dims, lines, step, scal, go_ref, z_ref, rows3, gr_ref)
    hT = h_ref[...].T
    for j in range(wide // block):
        lanes = slice(block * j, block * (j + 1))
        ds[j % 2] = dot_nt(gr_ref[...], w1s[lanes, :])

        def own(part, mask, total):
            value = gs_ref[part, lanes].astype(F32) + ds[j % 2, part, :]
            value = value * du_ref[part, lanes].astype(F32)
            gs0_ref[part, lanes] = value.astype(BF16)
            return total + fold(value)

        total = each_line(dims, lines, step, scal, block, own)(jnp.zeros((8, block), F32))
        sacc[:, lanes] += total
    wide_tail(hT, gs0_ref, w3s, low_ref, t_ref)

    @pl.when(step == pl.num_programs(0) - 1)
    def _():
        wide_sums(w3_ref, t_ref, sacc, vec3_ref, sum_ref, unit)


def reduce_grad_kernel(unit, scal, x_ref, gr_ref, mine_ref, sent_ref, gacc):
    step = pl.program_id(0)

    @pl.when(step == 0)
    def _():
        gacc[...] = jnp.zeros_like(gacc)

    gacc[...] += dot_tn(gr_ref[...], x_ref[...])

    @pl.when(step == pl.num_programs(0) - 1)
    def _():
        chips, size, width = mine_ref.shape
        value = (unit * gacc[...].T).reshape(chips, -1, size, width)
        hand_over(scal, value, mine_ref, sent_ref)


def last_grad_kernel(
    dims, lines, scal, nf, go_ref, z_ref, got_ref, vec1_ref, x_ref,
    gr_ref, mine_ref, sent_ref, tot_ref, rows3, gacc,
):
    step = pl.program_id(0)

    @pl.when(step == 0)
    def _():
        norm_rows(nf, got_ref, vec1_ref, tot_ref, rows3)
        gacc[...] = jnp.zeros_like(gacc)

    reduced_grad(dims, lines, step, scal, go_ref, z_ref, rows3, gr_ref)
    gacc[...] += dot_tn(gr_ref[...], x_ref[...].reshape(-1, x_ref.shape[2]))

    @pl.when(step == pl.num_programs(0) - 1)
    def _():
        chips, size, width = mine_ref.shape
        hand_over(scal, gacc[...].T.reshape(chips, -1, size, width), mine_ref, sent_ref)


def input_kernel(gr_ref, gs_ref, w1_ref, out_ref):
    w1 = w1_ref[...].reshape(-1, w1_ref.shape[2])
    value = dot_nt(gr_ref[...], w1) + 0.25 * gs_ref[...].astype(F32)
    out_ref[...] = value.astype(BF16).reshape(out_ref.shape)


ALL = ("clip", "outer", "inner")
CHIPS = ("clip", "outer")
SP = ("outer", "inner")


def share(rows):
    return lax.all_to_all(rows, ALL, 0, 0)


def gather(value):
    return share(jnp.broadcast_to(value[None], (lax.axis_size(ALL),) + value.shape))


def neighbours(near, far):
    peers = lax.axis_size(SP)
    first = [(i, i + 1) for i in range(0, peers - 1, 2)]
    second = [(i, i + 1) for i in range(1, peers - 1, 2)]
    near = lax.ppermute(near, SP, first + [(j, i) for i, j in first])
    far = lax.ppermute(far, SP, second + [(j, i) for i, j in second])
    return near, far


def swap(value):
    peers = lax.axis_size("inner")
    return lax.ppermute(value, "inner", [(i, (i + 1) % peers) for i in range(peers)])


def after(value, other):
    return lax.optimization_barrier((value, other))[0]


def on_device(
    features, strides, cotangent, w_reduce, w_mix, w_expand, w_depth,
    gains_mid, biases_mid, gains_out, biases_out,
):
    clips, frames, rows, columns, wide = features.shape
    width = w_mix.shape[2]
    peers, chips = lax.axis_size(ALL), lax.axis_size(CHIPS)
    inner = lax.axis_size("inner")
    sp_size = lax.axis_size(SP)
    part, place = lax.axis_index("inner"), lax.axis_index(ALL)
    sp_at = lax.axis_index(SP)
    line = columns * frames
    per_clip = rows * line
    voxels = clips * per_clip
    r1, r2 = w_reduce.shape[1], w_mix.shape[1]
    r4 = w_depth.shape[2]
    r5 = gains_out.shape[1] // r4
    blocks = wide // width

    def from_chips(packed, ready):
        packed = jnp.pad(packed, ((0, -packed.shape[0] % 16), (0, 0)))
        packed = jnp.broadcast_to(packed[None], (chips,) + packed.shape)
        return lax.all_to_all(after(packed, ready), CHIPS, 0, 0)

    def from_cores(near):
        held = [near]
        for _ in range(inner - 1):
            held.append(swap(held[-1]))
        turns = [lax.rem(part - c + inner, inner) for c in range(inner)]
        whole = jnp.stack([lax.select_n(turn, *held) for turn in turns], axis=1)
        return whole.reshape((peers,) + near.shape[1:])

    def wide_weight(rows_of_all):
        one = rows_of_all.reshape(peers, blocks, r2, width).transpose(0, 2, 1, 3)
        return one.reshape(peers * r2, wide)

    height = r1 + r2 + 8
    height += -height % 16
    whole = lambda value: full(value.shape)
    raw = (w_reduce, w_mix, w_depth.transpose(0, 2, 1), gains_mid, biases_mid, gains_out,
           biases_out)
    packed = call(
        pack_kernel, 1, [whole(one) for one in raw], full((chips, height, width)),
        jax.ShapeDtypeStruct((chips, height, width), BF16), [], 1,
    )(*raw)
    near = lax.all_to_all(packed, CHIPS, 0, 0)
    x = features.transpose(0, 2, 3, 1, 4).reshape(voxels // frames, frames, wide)
    early = from_cores(near)
    w2 = [early[:, r1 : r1 + r2].reshape(-1, width)]
    at = r1 + r2
    taps = early[:, at : at + r4, 0:64].reshape(-1, 64).T
    taps = [taps[32 * k : 32 * k + 27] for k in range(2)]
    mids = early[:, at : at + 8, 64 : 64 + r4].transpose(1, 0, 2).reshape(8, width)
    par = jnp.concatenate([*taps, mids, jnp.zeros((2, width), BF16)], axis=0).astype(F32)
    pout = early[:, at : at + 4, 96 : 96 + r4 * r5].transpose(1, 0, 2).reshape(4, wide)
    pout = pout.astype(F32)

    counts = frames // strides
    by_group = jnp.sum(counts.reshape(-1, clips), axis=1) * (rows * columns)
    by_device = jnp.repeat(by_group, sp_size).astype(F32)
    local = lax.dynamic_slice_in_dim(counts, lax.axis_index("clip") * clips, clips)
    odd = lax.rem(sp_at, 2)
    has_near = (odd == 1) | (sp_at < sp_size - 1)
    has_far = jnp.where(odd == 1, sp_at < sp_size - 1, sp_at > 0)
    way = jnp.where(odd == 1, -1, 1)
    base = lax.axis_index("clip") * sp_size
    near_place = base + jnp.clip(sp_at + way, 0, sp_size - 1)
    far_place = base + jnp.clip(sp_at - way, 0, sp_size - 1)
    edges = jnp.stack(
        [has_near.astype(jnp.int32), has_far.astype(jnp.int32), near_place, far_place, odd]
    )
    scal = jnp.concatenate([local.astype(jnp.int32), edges])
    own = jnp.sum(local).astype(F32) * (rows * columns)
    total = jnp.sum(by_device)
    nf = jnp.stack([own, total, 1.0 / own, 1.0 / total])
    cnt = jnp.broadcast_to(by_device[:, None, None], (peers, 1, LANE))
    rinv = jnp.broadcast_to(1.0 / by_device[:, None], (peers, LANE))

    struct = jax.ShapeDtypeStruct
    dims = (frames, rows, line)
    lines = rows
    steps = clips * rows // lines
    tall = (rows + 2) * line
    by_step = lambda size: pl.BlockSpec((lines * line, size), lambda s: (s, 0))
    thin, broad = by_step(width), by_step(wide)

    def by_clip(name):
        per = PER[name] if clips % PER[name] == 0 else 1
        field = pl.BlockSpec((per * per_clip, width), lambda c: (c, 0))
        tall_field = pl.BlockSpec((per * tall, width), lambda c: (c, 0))
        edge_one = pl.BlockSpec((per, line, width), lambda c: (c, 0, 0))
        edge_two = pl.BlockSpec((per, 2, line, width), lambda c: (c, 0, 0, 0))
        return per, field, tall_field, edge_one, edge_two

    native = pl.BlockSpec((lines * line // frames, frames, wide), lambda s: (s, 0, 0))
    native_shape = struct((voxels // frames, frames, wide), BF16)
    narrow = lambda kind: struct((voxels, width), kind)
    wide_shape = struct((voxels, wide), BF16)
    edge = struct((clips, line, width), BF16)
    lines_kept = pltpu.VMEM((2, clips, line, width), F32)
    pair = struct((clips, 2, line, width), BF16)
    flat = lambda *shape: struct(shape, F32)
    two = (peers, 1, 2 * width)
    three = (peers, 1, width + wide)
    many = (peers, 2 * wide // LANE, LANE)
    vec, vec_wide = (8, width), (8, wide)
    owned = struct((chips, r1, width), BF16)
    owned_taps = struct((chips, 2 * r2, width), BF16)

    reduced, up, dn, stats = call(
        functools.partial(first_kernel, dims, lines), steps,
        [smem(), smem(), native, full((peers, r1, width))],
        [thin, full(edge.shape), full(edge.shape), full(two)],
        [narrow(F32), edge, edge, flat(*two)],
        [pltpu.VMEM((24, width), F32), lines_kept], 6,
    )(scal, nf, x, early)

    depth_scratch = [
        pltpu.VMEM((tall, width), F32), pltpu.VMEM((3, tall, width), BF16),
        pltpu.VMEM((width // LANE, 9 * LANE, 2 * LANE), BF16),
        pltpu.VMEM((width // LANE, per_clip, 2 * LANE), F32),
    ]
    above, below = neighbours(up, dn)
    got = share(stats)
    wide_rows = w_expand.reshape(2, r2, blocks, width).transpose(0, 2, 1, 3)
    wide_rows = wide_rows.reshape(2, r2 * blocks, width)

    got, cnt, par, w2[0] = lax.optimization_barrier((got, cnt, par, w2[0]))
    near = from_chips(
        jnp.concatenate([wide_rows[0], w_reduce[1]], axis=0), (got, above, below)
    )
    w1, w3 = [early], []
    stored = []
    for layer in range(2):
        if layer == 1:
            above, below = neighbours(up, dn)
            got = share(stats)
            late = from_cores(after(near, stats))
            w3.append(wide_weight(late[:, : r2 * blocks]))
            w2.append(late[:, r2 * blocks : r2 * blocks + r2].reshape(-1, width))
        per, field, tall_field, edge_one, edge_two = by_clip("mix")
        mixed, spatial, z1, u1, h1, stats, vec1 = call(
            functools.partial(mix_kernel, dims, layer, per), clips // per,
            [smem(), smem(), field, edge_one, edge_one, full(two),
             full((peers, 1, LANE)), full((64, width)), full((width, width))],
            [tall_field, field, field, field, field, full(two), full(vec)],
            [struct((clips * tall, width), BF16), narrow(F32), narrow(BF16), narrow(BF16),
             narrow(BF16), flat(*two), flat(*vec)],
            [pltpu.VMEM((tall, width), BF16), *depth_scratch, pltpu.VMEM((24, width), F32)], 10,
        )(scal, nf, reduced, above, below, got, cnt, par, w2[layer])
        got = share(stats)
        if layer == 0:
            late = from_cores(after(near, stats))
            w3.append(wide_weight(late[:, : r2 * blocks]))
            w1.append(late[:, r2 * blocks :].reshape(-1, width))
        per, field, tall_field, edge_one, edge_two = by_clip("hidden")
        z2, u2, h2, stats, gram, vec2 = call(
            functools.partial(hidden_kernel, dims, layer, per), clips // per,
            [smem(), smem(), field, full(two), full((peers, 1, LANE)),
             full((64, width)), full((width, wide))],
            [field, field, field, full(three), full((width + 8, width)), full(vec)],
            [narrow(BF16), narrow(BF16), narrow(BF16), flat(*three), flat(width + 8, width),
             flat(*vec)],
            [pltpu.VMEM((8, width), F32)], 5,
        )(scal, nf, spatial, got, cnt, par, w3[layer])
        got = share(stats)
        if layer == 0:
            got, pout, rinv, w1[1] = lax.optimization_barrier((got, pout, rinv, w1[1]))
            near = from_chips(jnp.concatenate([wide_rows[1], w_mix[1]], axis=0), got)
        norm_specs = [full(three), full((peers, 1, LANE)), full((peers, LANE)),
                      full((4, wide)), full((width, wide))]
        norm_args = (got, cnt, rinv, pout, w3[layer])
        if layer == 0:
            carried, slope, reduced, up, dn, stats, vec3 = call(
                functools.partial(join_kernel, dims, lines), steps,
                [smem(), smem(), native, thin] + norm_specs + [full((wide, width))],
                [broad, broad, thin, full(edge.shape), full(edge.shape), full(two),
                 full(vec_wide)],
                [wide_shape, wide_shape, narrow(F32), edge, edge, flat(*two), flat(*vec_wide)],
                [pltpu.VMEM((2, lines * line, 256), F32), pltpu.VMEM((24, width), F32),
                 lines_kept], 12,
            )(scal, nf, x, h2, *norm_args, w1[1])
        else:
            cot = cotangent.transpose(0, 2, 3, 1, 4).reshape(voxels // frames, frames, wide)
            output, gs, low, t, sums, vec3 = call(
                functools.partial(out_kernel, dims, lines), steps,
                [smem(), smem(), broad, thin, native] + norm_specs,
                [native, broad, thin, full((width, wide)), full(many), full(vec_wide)],
                [native_shape, wide_shape, narrow(F32), flat(width, wide), struct(many, BF16),
                 flat(*vec_wide)],
                [pltpu.VMEM((2, lines * line, 256), F32), pltpu.VMEM((width, wide), BF16),
                 pltpu.VMEM((8, wide), F32)], 15,
            )(scal, nf, carried, h2, cot, *norm_args)
        stored.append((z1, u1, h1, vec1, mixed, z2, u2, h2, vec2, gram, vec3))

    def voxel_form(value):
        return value.reshape(clips, rows, columns, frames, wide).transpose(0, 3, 1, 2, 4)

    def sum_cores(*pieces):
        if inner == 1:
            return jnp.concatenate([mine for mine, _ in pieces], axis=1)
        return jnp.concatenate([mine + swap(sent) for mine, sent in pieces], axis=1)

    results = [None, None]
    for layer in (1, 0):
        z1, u1, h1, vec1, mixed, z2, u2, h2, vec2, gram, vec3 = stored[layer]
        if layer == 0:
            sums = after(sums, first)
        got = share(sums)
        if layer == 0:
            got, reduce_mine, reduce_sent = lax.optimization_barrier(
                (got, reduce_mine, reduce_sent)
            )
        per, field, tall_field, edge_one, edge_two = by_clip("expand")
        go2, up, dn, sums, tot3 = call(
            functools.partial(expand_back_kernel, dims, per), clips // per,
            [smem(), smem(), field, field, field, field, full(many), full(vec_wide),
             full((width, wide))],
            [field, edge_two, edge_two, full(two), full((1, 2 * wide))],
            [narrow(BF16), pair, pair, flat(*two), flat(1, 2 * wide)],
            [pltpu.VMEM((width, width), BF16), pltpu.VMEM(vec, F32),
             pltpu.VMEM((per * per_clip, width), F32), pltpu.VMEM((16, width), F32)], 6,
        )(scal, nf, low, h2, z2, u2, got, vec3, w3[layer])
        expand_mine, expand_sent = call(
            expand_grad_kernel, 1,
            [smem(), smem(), full((1, 2 * wide)), full(vec_wide), full((width, wide)),
             full((width + 8, width)), full((width, wide))],
            [full(owned.shape), full(owned.shape)], [owned, owned], [], 3,
        )(scal, nf, tot3, vec3, t, gram, w3[layer])
        above, below = neighbours(up, dn)
        got = share(sums)
        got, expand_mine, expand_sent = lax.optimization_barrier((got, expand_mine, expand_sent))
        expands = (expand_mine, expand_sent)
        if layer == 0:
            second = sum_cores((reduce_mine, reduce_sent), expands)
            second = lax.all_to_all(after(second, (got, above, below)), CHIPS, 0, 0)
        per, field, tall_field, edge_one, edge_two = by_clip("depth")
        go1, sums, gm, gp, tot2 = call(
            functools.partial(depth_back_kernel, dims, layer, per), clips // per,
            [smem(), smem(), field, edge_two, edge_two, field, full(two), full(vec), field,
             field, full((64, width)), full((width, width))],
            [field, full(two), field, field, full((1, 2 * width))],
            [narrow(BF16), flat(*two), narrow(BF16), narrow(BF16), flat(1, 2 * width)],
            [*depth_scratch, pltpu.VMEM((per_clip, width), F32), pltpu.VMEM(vec, F32),
             pltpu.VMEM((16, width), F32)], 12,
        )(scal, nf, go2, above, below, z2, got, vec2, z1, u1, par, w2[layer])
        if layer == 0:
            sums = after(sums, second)
        got = share(sums)
        per, field, tall_field, edge_one, edge_two = by_clip("grads")
        taps_mine, taps_sent = call(
            functools.partial(kernel_grads, dims, per), clips // per,
            [smem(), tall_field, field, field, field],
            [full(owned_taps.shape), full(owned_taps.shape)],
            [owned_taps, owned_taps],
            [pltpu.VMEM((width, width), F32), pltpu.VMEM((LANE, width), F32),
             pltpu.VMEM((3, tall, width), BF16),
             pltpu.VMEM((width // LANE, per_clip, 2 * LANE), BF16),
             pltpu.VMEM((width // LANE, 2 * LANE, 9 * LANE), F32),
             pltpu.VMEM((9, 8, width), F32)], 12,
        )(scal, mixed, gp, gm, h1)
        got, taps_mine, taps_sent = lax.optimization_barrier((got, taps_mine, taps_sent))
        if layer == 1:
            first = lax.all_to_all(sum_cores((taps_mine, taps_sent), expands), CHIPS, 0, 0)
        if layer == 1:
            h2_0, vec3_0 = stored[0][7], stored[0][10]
            gs, low, t, sums, gr, tot1 = call(
                functools.partial(cross_kernel, dims, lines), steps,
                [smem(), smem(), thin, thin, full(two), full(vec), broad, broad, thin,
                 full(vec_wide), full((wide, width)), full((width, wide))],
                [broad, thin, full((width, wide)), full(many), thin, full((1, 2 * width))],
                [wide_shape, narrow(F32), flat(width, wide), struct(many, BF16), narrow(BF16),
                 flat(1, 2 * width)],
                [pltpu.VMEM((2, lines * line, 256), F32), pltpu.VMEM((wide, width), BF16),
                 pltpu.VMEM((width, wide), BF16), pltpu.VMEM(vec, F32),
                 pltpu.VMEM((8, wide), F32)], 15,
            )(scal, nf, go1, z1, got, vec1, gs, slope, h2_0, vec3_0, w1[1], w3[0])
            reduce_mine, reduce_sent = call(
                functools.partial(reduce_grad_kernel, 2.0), steps,
                [smem(), broad, thin], [full(owned.shape), full(owned.shape)], [owned, owned],
                [pltpu.VMEM((width, wide), F32)], 5,
            )(scal, carried, gr)
        else:
            gr, mine, sent, tot1 = call(
                functools.partial(last_grad_kernel, dims, lines), steps,
                [smem(), smem(), thin, thin, full(two), full(vec), native],
                [thin, full(owned.shape), full(owned.shape), full((1, 2 * width))],
                [narrow(BF16), owned, owned, flat(1, 2 * width)],
                [pltpu.VMEM(vec, F32), pltpu.VMEM((width, wide), F32)], 6,
            )(scal, nf, go1, z1, got, vec1, x)
            input_grad = call(
                input_kernel, steps, [thin, broad, full((peers, r1, width))], native,
                native_shape, [], 6,
            )(gr, gs, early)
        results[layer] = (tot1, tot2, tot3)

    last = sum_cores((mine, sent), (taps_mine, taps_sent))
    last = jnp.sum(lax.all_to_all(last, CHIPS, 0, 0).astype(F32), axis=0)
    first = jnp.sum(first.astype(F32), axis=0)
    second = jnp.sum(second.astype(F32), axis=0)
    to_wide = lambda one: one.reshape(blocks, r2, width).transpose(1, 0, 2).reshape(r2, wide)
    grad_reduce = jnp.stack([last[0:r1], second[0:r1]])
    grad_mix = jnp.stack([last[r1 : r1 + r2], first[0:r2]])
    depths = (last[r1 + r2 : r1 + r2 + r4], first[r2 : r2 + r4])
    grad_depth = jnp.stack([one[:, 0:27].T for one in depths])
    grad_expand = jnp.stack([to_wide(second[r1:]), to_wide(first[r2 + r4 :])])

    mid_sums = jnp.concatenate(
        [
            jnp.concatenate([results[layer][0], results[layer][1]], axis=0).reshape(2, 2, width)
            for layer in range(2)
        ],
        axis=0,
    )
    mid = lax.dynamic_slice_in_dim(mid_sums, place * r4, r4, axis=2)
    out_sums = jnp.concatenate([results[layer][2].reshape(1, 2, wide) for layer in range(2)])
    r6 = gains_out.shape[1]
    outs = lax.dynamic_slice_in_dim(out_sums, place * r6, r6, axis=2)

    return (
        voxel_form(output),
        voxel_form(input_grad),
        grad_reduce,
        grad_mix,
        grad_expand,
        grad_depth,
        mid[:, 1].reshape(2, 2, r4),
        mid[:, 0].reshape(2, 2, r4),
        outs[:, 1],
        outs[:, 0],
    )


def solution(mesh):
    clip_size, sp_size = mesh.shape["clip"], mesh.shape["sp"]
    inner = 2 if sp_size % 2 == 0 else 1
    divided = Mesh(mesh.devices.reshape(clip_size, sp_size // inner, inner), ALL)
    activations = P("clip", None, SP, None, None)
    middle, last, vectors = P(None, ALL, None), P(None, None, ALL), P(None, ALL)
    return jax.shard_map(
        on_device,
        mesh=divided,
        in_specs=(
            activations, P(), activations, middle, middle, middle, last, last, last, vectors,
            vectors,
        ),
        out_specs=(
            activations, activations, middle, middle, middle, last, last, last, vectors, vectors,
        ),
        check_vma=False,
    )
```

```python
import functools

import jax
import jax.numpy as jnp
from jax import lax
from jax.experimental import pallas as pl
from jax.experimental.pallas import tpu as pltpu
from jax.sharding import Mesh, PartitionSpec as P

epsilon = 1e-05
F32 = jnp.float32
BF16 = jnp.bfloat16
LANE = 128
STEP = 16
COST = 3.0e6
PER = {"mix": 1, "hidden": 2, "expand": 2, "depth": 1, "grads": 1, "slopes": 2}


def dot_nn(left, right):
    return lax.dot_general(left, right, (((1,), (0,)), ((), ())), preferred_element_type=F32)


def dot_nt(left, right):
    return lax.dot_general(left, right, (((1,), (1,)), ((), ())), preferred_element_type=F32)


def dot_tn(left, right):
    return lax.dot_general(left, right, (((0,), (0,)), ((), ())), preferred_element_type=F32)


def split(value):
    high = value.astype(BF16)
    return high, (value - high.astype(F32)).astype(BF16)


def dot_split(left, right):
    high, rest = split(left)
    return dot_nn(high, right) + dot_nn(rest, right)


def fold(value):
    return jnp.sum(value.reshape(-1, 8, value.shape[-1]), axis=0)


def row_sum(value):
    return jnp.sum(value, axis=0, keepdims=True)


def live_rows(count, frames, rows, width):
    at = lax.rem(lax.broadcasted_iota(jnp.int32, (rows, width), 0), frames)
    return jnp.where(at < count, 1.0, 0.0)


def live_cap(count, frames, rows, width):
    return jnp.where(live_rows(count, frames, rows, width) > 0.5, 3e38, -60.0)


def full(shape):
    return pl.BlockSpec(shape, lambda *_: (0,) * len(shape))


def smem():
    return pl.BlockSpec(memory_space=pltpu.SMEM)


def call(body, steps, in_specs, out_specs, out_shape, scratch, micros):
    return pl.pallas_call(
        body,
        grid=(steps,),
        in_specs=in_specs,
        out_specs=out_specs,
        out_shape=out_shape,
        scratch_shapes=scratch,
        cost_estimate=pl.CostEstimate(
            flops=0, transcendentals=0, bytes_accessed=int(micros * COST)
        ),
        compiler_params=pltpu.CompilerParams(
            dimension_semantics=("arbitrary",), vmem_limit_bytes=58 * 2**20
        ),
    )


def each(count, body, unroll=1):
    def step(i, carry):
        body(pl.multiple_of(i * STEP, STEP))
        return carry

    lax.fori_loop(0, count // STEP, step, 0, unroll=unroll)


def clip_loop(dims, per, body):
    frames, rows, line = dims
    size = rows * line
    step = pl.program_id(0)

    def one(k, carry):
        def view(ref, extra=0):
            length = size + extra * line
            return ref.at[pl.ds(pl.multiple_of(k * length, STEP), length), :]

        body(step * per + k, k, view)
        return carry

    lax.fori_loop(0, per, one, 0)


def merge_stats(means, squares, counts, total):
    mean = jnp.sum(means * counts, axis=0) / total
    away = means - mean[None]
    spread = jnp.sum(squares + counts * away * away, axis=0) / total
    return mean, lax.rsqrt(spread + epsilon)


def narrow_norm(nf, got_ref, cnt_ref, gain, bias, vec_ref):
    width = vec_ref.shape[1]
    mean, inverse = merge_stats(
        got_ref[:, :, 0:width], got_ref[:, :, width:], cnt_ref[:, :, 0:1], nf[1]
    )
    scale = gain * inverse
    vec_ref[...] = jnp.zeros_like(vec_ref)
    vec_ref[0:1, :] = inverse
    vec_ref[1:2, :] = -mean * inverse
    vec_ref[2:3, :] = 0.5 * scale
    vec_ref[3:4, :] = 0.5 * (bias - mean * scale)
    vec_ref[4:5, :] = scale


def silu_half(half):
    both = jnp.tanh(half) + 1.0
    return half * both, both


def slope_of(value, both):
    return 0.5 * slope_twice(value, both)


def slope_twice(value, both):
    return both + value * (2.0 - both)


def line_stats(nf, scal, dims, read, lines, first_line, is_first, acc, st_ref):
    frames, rows, line = dims
    width = acc.shape[1]

    @pl.when(is_first)
    def _():
        mask = live_rows(scal[0], frames, STEP, width)
        total = jnp.zeros((8, width), F32)
        for i in range(line // STEP):
            total = total + fold(read(0, i * STEP) * mask)
        acc[...] = jnp.zeros_like(acc)
        alive = (scal[0] * (line // frames)).astype(F32)
        acc[0:1, :] = row_sum(total) / alive

    pivot = acc[0:1, :]

    def one(at, carry):
        plain, square = carry
        mask = live_rows(scal[(first_line + at) // rows], frames, STEP, width)
        for i in range(line // STEP):
            away = (read(at, i * STEP) - pivot) * mask
            plain = plain + fold(away)
            square = square + fold(away * away)
        return plain, square

    zero = jnp.zeros((8, width), F32)
    plain, square = lax.fori_loop(0, lines, one, (zero, zero), unroll=True)
    acc[8:16, :] += plain
    acc[16:24, :] += square


def edge_places(scal, clips, line, rows):
    last = line * (rows + 1)
    near = jnp.where(scal[scal.shape[0] - 1] == 0, last, 0)
    return pl.multiple_of(near, STEP), pl.multiple_of(last - near, STEP)


def hand_over(scal, value, mine_ref, sent_ref):
    even = scal[scal.shape[0] - 1] == 0
    other = value.shape[1] - 1
    mine_ref[...] = jnp.where(even, value[:, 0], value[:, other]).astype(BF16)
    sent_ref[...] = jnp.where(even, value[:, other], value[:, 0]).astype(BF16)


def finish_stats(nf, acc, st_ref):
    plain, square = row_sum(acc[8:16, :]), row_sum(acc[16:24, :])
    width = acc.shape[1]
    peers = st_ref.shape[0]
    st_ref[:, :, 0:width] = jnp.broadcast_to(acc[0:1, :] + plain * nf[2], (peers, 1, width))
    spread = square - plain * plain * nf[2]
    st_ref[:, :, width:] = jnp.broadcast_to(spread, (peers, 1, width))


def share_sums(acc, sum_ref):
    width = acc.shape[1]
    peers = sum_ref.shape[0]
    for k in range(2):
        one = row_sum(acc[8 * k : 8 * k + 8, :])
        sum_ref[:, :, width * k : width * (k + 1)] = jnp.broadcast_to(one, (peers, 1, width))


def depth_weights(par_ref, layer, wd, flip):
    one = lax.broadcasted_iota(jnp.int32, (LANE, LANE), 0)
    two = lax.broadcasted_iota(jnp.int32, (LANE, LANE), 1)
    eye = jnp.where(one == two, 1.0, 0.0)
    for half in range(wd.shape[0]):
        for i in range(9):
            for e in (0, 2):
                tap = 3 * i + e
                at = 27 * layer + (26 - tap if flip else tap)
                row = par_ref[at : at + 1, LANE * half : LANE * (half + 1)]
                k = LANE * (e // 2)
                wd[half, LANE * i : LANE * (i + 1), k : k + LANE] = (eye * row).astype(BF16)


def frame_moves(frames, value):
    width = value.shape[1]
    groups = value.reshape(-1, 8, width)
    here = lax.rem(lax.broadcasted_iota(jnp.int32, (1, 8, width), 1), frames)
    onward = jnp.where(here > 0, pltpu.roll(groups, 1, 1), 0.0)
    back = jnp.where(here < frames - 1, pltpu.roll(groups, 7, 1), 0.0)
    return onward.reshape(value.shape), back.reshape(value.shape)


def frame_shifts(dims, value, tv, at):
    onward, back = frame_moves(dims[0], value)
    part = pl.ds(at, value.shape[0])
    tv[0, part, :] = onward.astype(BF16)
    tv[1, part, :] = value.astype(BF16)
    tv[2, part, :] = back.astype(BF16)


def column_moves(dims, value):
    frames, rows, line = dims
    at = lax.broadcasted_iota(jnp.int32, (8, value.shape[1]), 0)
    onward = pltpu.roll(value, frames, 0)
    top = jnp.where(at >= frames, onward[0:8], 0.0)
    onward = jnp.concatenate([top, onward[8:]], axis=0)
    back = pltpu.roll(value, line - frames, 0)
    bottom = jnp.where(at < 8 - frames, back[line - 8 :], 0.0)
    return onward, jnp.concatenate([back[: line - 8], bottom], axis=0)


def depth_sum(dims, layer, flip, par_ref, ms, tv, wd, ds, temp, store):
    frames, rows, line = dims
    halves = wd.shape[0]
    piece = line // 2 if line % (2 * 8) == 0 else line
    for half in range(halves):
        lanes = slice(LANE * half, LANE * (half + 1))
        views = [tv[a, line * b : line * (b + rows), lanes] for a in range(3) for b in range(3)]
        ds[half] = dot_nn(jnp.concatenate(views, axis=1), wd[half])
        taps = []
        for i in range(9):
            tap = 3 * i + 1
            at = 27 * layer + (26 - tap if flip else tap)
            taps.append(par_ref[at : at + 1, lanes])
        for start in range(0, rows * line, piece):
            seen = [ms[start + line * b : start + line * b + piece, lanes] for b in range(3)]
            sums = []
            for a in range(3):
                one = seen[0] * taps[3 * a]
                one = one + seen[1] * taps[3 * a + 1]
                sums.append(one + seen[2] * taps[3 * a + 2])
            onward, _ = frame_moves(frames, sums[0])
            _, back = frame_moves(frames, sums[2])
            temp[start : start + piece, lanes] = onward + sums[1] + back
    for half in range(halves):
        lanes = slice(LANE * half, LANE * (half + 1))
        for r in range(rows):
            part = slice(line * r, line * (r + 1))
            onward, _ = column_moves(dims, ds[half, part, 0:LANE])
            _, back = column_moves(dims, ds[half, part, LANE : 2 * LANE])
            store(r, lanes, onward + temp[part, lanes] + back)


def pack_kernel(wr_ref, wm_ref, wd_ref, gm_ref, bm_ref, go_ref, bo_ref, out_ref):
    r1, width = wr_ref.shape[1:]
    r2 = wm_ref.shape[1]
    r4, taps = wd_ref.shape[1:]
    r6 = go_ref.shape[1]
    zeros = lambda rows, size: jnp.zeros((rows, size), F32)
    part = [wd_ref[k].astype(F32) for k in range(2)]
    if r4 < 8:
        part = [jnp.concatenate([one, zeros(8 - r4, taps)], axis=0) for one in part]
    pad = zeros(8, 32 - taps)
    mids = [gm_ref[k].astype(F32) for k in range(2)] + [bm_ref[k].astype(F32) for k in range(2)]
    mids = jnp.concatenate(mids, axis=0)
    outs = jnp.concatenate([go_ref[...].astype(F32), bo_ref[...].astype(F32)], axis=0)
    mids = jnp.concatenate([mids, zeros(8, 32 - r4)], axis=1)
    outs = jnp.concatenate([outs, zeros(4, r6)], axis=0)
    small = [part[0], pad, part[1], pad, mids, outs]
    small.append(zeros(8, width - 96 - r6))
    rest = out_ref.shape[1] - r1 - r2 - 8
    rows = [wr_ref[0].astype(F32), wm_ref[0].astype(F32), jnp.concatenate(small, axis=1)]
    if rest:
        rows.append(zeros(rest, width))
    block = jnp.concatenate(rows, axis=0).astype(BF16)
    for k in range(out_ref.shape[0]):
        out_ref[k] = block


def late_pack_kernel(wr_ref, wm_ref, we_ref, one_ref, two_ref):
    width = wr_ref.shape[2]
    zeros = lambda rows: jnp.zeros((rows, width), F32)
    for layer, out_ref in enumerate((one_ref, two_ref)):
        wide = we_ref[layer].astype(F32)
        rows = [wide[:, k : k + width] for k in range(0, wide.shape[1], width)]
        rows.append((wr_ref if layer == 0 else wm_ref)[1].astype(F32))
        rest = out_ref.shape[1] - sum(one.shape[0] for one in rows)
        if rest:
            rows.append(zeros(rest))
        block = jnp.concatenate(rows, axis=0).astype(BF16)
        for k in range(out_ref.shape[0]):
            out_ref[k] = block


def first_kernel(dims, lines, scal, nf, x_ref, w_ref, red_ref, up_ref, dn_ref, st_ref, acc, lines_kept):
    step = pl.program_id(0)
    x = x_ref[...].reshape(-1, x_ref.shape[2])
    red_ref[...] = dot_nn(x, w_ref[...].reshape(-1, w_ref.shape[2]))
    reduced_tail(dims, lines, step, scal, nf, red_ref, up_ref, dn_ref, st_ref, acc, lines_kept)


def reduced_tail(dims, lines, step, scal, nf, red_ref, up_ref, dn_ref, st_ref, acc, lines_kept):
    frames, rows, line = dims
    read = lambda at, i: red_ref[pl.ds(pl.multiple_of(line * at, STEP) + i, STEP), :]
    line_stats(nf, scal, dims, read, lines, step * lines, step == 0, acc, st_ref)
    for k in range(lines // rows):
        clip, at = step * (lines // rows) + k, k * rows * line
        even = scal[scal.shape[0] - 1] == 0
        last = line * (rows - 1)
        near = jnp.where(even, last, 0)
        for way, start in enumerate((near, last - near)):
            part = pl.ds(pl.multiple_of(at + start, STEP), line)
            lines_kept[way, clip] = red_ref[part, :]

    @pl.when(step == pl.num_programs(0) - 1)
    def _():
        finish_stats(nf, acc, st_ref)
        mean = acc[0:1, :] + row_sum(acc[8:16, :]) * nf[2]
        for at in range(up_ref.shape[0]):
            up_ref[at] = (lines_kept[0, at] - mean).astype(BF16)
            dn_ref[at] = (lines_kept[1, at] - mean).astype(BF16)


def mix_kernel(
    dims, layer, per, scal, nf, red_ref, up_ref, dn_ref, got_ref, cnt_ref, par_ref, w_ref,
    mix_ref, spa_ref, st_ref, vec_ref, hs, ms, tv, wd, ds, acc,
):
    step, last = pl.program_id(0), pl.num_programs(0) - 1
    width = w_ref.shape[0]

    @pl.when(step == 0)
    def _():
        at = 2 * layer
        narrow_norm(
            nf, got_ref, cnt_ref, par_ref[54 + at : 55 + at, :], par_ref[58 + at : 59 + at, :],
            vec_ref,
        )
        for k in range(2):
            mean = got_ref[scal[scal.shape[0] - 3 + k], :, 0:width]
            vec_ref[5 + k : 6 + k, :] = vec_ref[3:4, :] + vec_ref[2:3, :] * mean
        depth_weights(par_ref, layer, wd, False)

    def body(clip, k, view):
        mix_clip(
            dims, layer, scal, nf, view(red_ref), up_ref.at[k], dn_ref.at[k], par_ref, w_ref,
            view(mix_ref, 2), view(spa_ref), st_ref,
            vec_ref, hs, ms, tv, wd, ds, acc, clip, per * (last + 1),
        )

    clip_loop(dims, per, body)

    @pl.when(step == last)
    def _():
        finish_stats(nf, acc, st_ref)


def mix_clip(
    dims, layer, scal, nf, red_ref, up_ref, dn_ref, par_ref, w_ref, mix_ref, spa_ref, st_ref, vec_ref, hs, ms, tv, wd, ds, acc, clip, clips,
):
    frames, rows, line = dims
    width = w_ref.shape[0]
    mask = live_rows(scal[clip], frames, STEP, width)
    near = mask * scal[clips].astype(F32)
    far = mask * scal[clips + 1].astype(F32)
    near_at, far_at = edge_places(scal, clips, line, rows)

    def edge(i):
        h, _ = silu_half(up_ref[pl.ds(i, STEP), :].astype(F32) * vec_ref[2:3, :] + vec_ref[5:6, :])
        hs[pl.ds(near_at + i, STEP), :] = (h * near).astype(BF16)
        h, _ = silu_half(dn_ref[pl.ds(i, STEP), :].astype(F32) * vec_ref[2:3, :] + vec_ref[6:7, :])
        hs[pl.ds(far_at + i, STEP), :] = (h * far).astype(BF16)

    each(line, edge, 7)

    def own(i):
        value = red_ref[pl.ds(i, STEP), :]
        h, _ = silu_half(value * vec_ref[2:3, :] + vec_ref[3:4, :])
        hs[pl.ds(i + line, STEP), :] = (h * mask).astype(BF16)

    each(line * rows, own, 49)
    ms[...] = dot_nn(hs[...], w_ref[...])

    def shifts(r, carry):
        at = pl.multiple_of(r * line, STEP)
        for half in range(width // LANE):
            lanes = slice(LANE * half, LANE * (half + 1))
            part = pl.ds(at, line)
            value = ms[part, lanes].astype(BF16).astype(F32)
            ms[part, lanes] = value
            frame_shifts(dims, value, tv.at[:, :, lanes], at)
        return carry

    lax.fori_loop(0, rows + 2, shifts, 0, unroll=True)
    mix_ref[...] = tv[1]

    def store(r, lanes, value):
        spa_ref[line * r : line * (r + 1), lanes] = value

    depth_sum(dims, layer, False, par_ref, ms, tv, wd, ds, spa_ref, store)
    read = lambda at, i: spa_ref[pl.ds(pl.multiple_of(line * at, STEP) + i, STEP), :]
    line_stats(nf, scal, dims, read, rows, clip * rows, clip == 0, acc, st_ref)

def hidden_rows(i, mask, spa_ref, h_ref, vec_ref, acc):
    part = pl.ds(i, STEP)
    h, _ = silu_half(spa_ref[part, :] * vec_ref[2:3, :] + vec_ref[3:4, :])
    low = (h * mask).astype(BF16)
    h_ref[part, :] = low
    acc[...] += fold(low.astype(F32))


def slopes_kernel(dims, per, scal, src_ref, vec_ref, z_ref, u_ref, *h_refs):
    frames, rows, line = dims
    width = src_ref.shape[1]

    def body(clip, k, view):
        mask = live_rows(scal[clip], frames, STEP, width)
        src, z_out, u_out = view(src_ref), view(z_ref), view(u_ref)
        h_out = view(h_refs[0]) if h_refs else None

        def own(i):
            part = pl.ds(i, STEP)
            value = src[part, :]
            h, both = silu_half(value * vec_ref[2:3, :] + vec_ref[3:4, :])
            if h_refs:
                h_out[part, :] = (h * mask).astype(BF16)
            u_out[part, :] = (slope_of(h, both) * mask).astype(BF16)
            z_out[part, :] = (value * vec_ref[0:1, :] + vec_ref[1:2, :]).astype(BF16)

        each(line * rows, own, 49)

    clip_loop(dims, per, body)


def hidden_kernel(
    dims, layer, per, scal, nf, spa_ref, got_ref, cnt_ref, par_ref, w_ref,
    h_ref, st_ref, gram_ref, vec_ref, acc,
):
    frames, rows, line = dims
    step = pl.program_id(0)
    width = par_ref.shape[1]

    @pl.when(step == 0)
    def _():
        at = 2 * layer
        narrow_norm(
            nf, got_ref, cnt_ref, par_ref[55 + at : 56 + at, :], par_ref[59 + at : 60 + at, :],
            vec_ref,
        )
        gram_ref[...] = jnp.zeros_like(gram_ref)
        acc[...] = jnp.zeros_like(acc)

    def body(clip, k, view):
        mask = live_rows(scal[clip], frames, STEP, width)
        spa, h_out = view(spa_ref), view(h_ref)

        def own(i):
            hidden_rows(i, mask, spa, h_out, vec_ref, acc)

        each(line * rows, own, 49)

    clip_loop(dims, per, body)
    gram_ref[0:width, :] += dot_tn(h_ref[...], h_ref[...])

    @pl.when(step == pl.num_programs(0) - 1)
    def _():
        total = row_sum(acc[...])
        gram_ref[width : width + 8, :] = jnp.broadcast_to(total, (8, width))
        across = jnp.broadcast_to(total, (width, width))
        centered = gram_ref[0:width, :] - across.T * across * nf[2]
        spread = row_sum(dot_split(centered, w_ref[...]) * w_ref[...].astype(F32))
        peers = st_ref.shape[0]
        st_ref[:, :, 0:width] = jnp.broadcast_to(total, (peers, 1, width))
        st_ref[:, :, width:] = jnp.broadcast_to(spread, (peers, 1, spread.shape[1]))


def wide_norm(nf, got_ref, cnt_ref, rinv_ref, pout_ref, layer, w_ref, vec_ref):
    width = w_ref.shape[0]
    hidden_means = got_ref[:, 0, 0:width] * rinv_ref[:, 0:1]
    means = dot_split(hidden_means, w_ref[...])
    counts = cnt_ref[:, 0, 0:1]
    mean = row_sum(means * counts) / nf[1]
    away = means - mean
    spread = row_sum(got_ref[:, 0, width:] + counts * away * away) / nf[1]
    inverse = lax.rsqrt(spread + epsilon)
    scale = pout_ref[layer : layer + 1, :] * inverse
    vec_ref[...] = jnp.zeros_like(vec_ref)
    vec_ref[0:1, :] = scale
    vec_ref[1:2, :] = 0.5 * (pout_ref[2 + layer : 3 + layer, :] - mean * scale)
    vec_ref[2:3, :] = inverse
    vec_ref[3:4, :] = mean
    vec_ref[4:5, :] = 0.5 * scale


def each_line(dims, lines, step, scal, width, body, make=live_cap):
    frames, rows, line = dims

    def run(carry):
        for at in range(lines):
            mask = make(scal[(step * lines + at) // rows], frames, STEP, width)
            for i in range(at * line, (at + 1) * line, STEP):
                carry = body(slice(i, i + STEP), mask, carry)
        return carry

    return run


def join_kernel(
    dims, lines, scal, nf, x_ref, h_ref, got_ref, cnt_ref, rinv_ref, pout_ref, w3_ref, w1_ref,
    next_ref, du_ref, red_ref, up_ref, dn_ref, st_ref, vec_ref, es, acc, lines_kept,
):
    step = pl.program_id(0)
    wide, width = w1_ref.shape
    frames = dims[0]
    block = 256

    @pl.when(step == 0)
    def _():
        wide_norm(nf, got_ref, cnt_ref, rinv_ref, pout_ref, 0, w3_ref, vec_ref)

    for j in range(wide // block):
        lanes = slice(block * j, block * (j + 1))
        es[j % 2] = dot_nn(h_ref[...], w3_ref[:, lanes])
        scale, shift = vec_ref[4:5, lanes], vec_ref[1:2, lanes]

        def own(part, cap, carry):
            spot = slice(part.start // frames, part.stop // frames)
            x = x_ref[spot, :, lanes].reshape(-1, block).astype(F32)
            half = x * 0.5 + (es[j % 2, part, :] * scale + shift)
            o, both = silu_half(jnp.minimum(half, cap))
            next_ref[part, lanes] = (0.5 * o).astype(BF16)
            du_ref[part, lanes] = slope_twice(o, both).astype(BF16)
            return carry

        each_line(dims, lines, step, scal, block, own)(0)
    red_ref[...] = 2.0 * dot_nn(next_ref[...], w1_ref[...])
    reduced_tail(dims, lines, step, scal, nf, red_ref, up_ref, dn_ref, st_ref, acc, lines_kept)


def wide_tail(hT, gs_ref, w3s, low_ref, t_ref):
    t_ref[...] += dot_nn(hT, gs_ref[...])
    low_ref[...] = dot_nt(gs_ref[...], w3s[...])


def wide_sums(w3_ref, t_ref, sacc, vec_ref, sum_ref, unit):
    wide = w3_ref.shape[1]
    t_ref[...] = unit * t_ref[...]
    plain = unit * row_sum(sacc[...])
    along = row_sum(w3_ref[...].astype(F32) * t_ref[...])
    along = (along - vec_ref[3:4, :] * plain) * vec_ref[2:3, :]
    pieces = [
        one[:, LANE * k : LANE * (k + 1)] for one in (plain, along) for k in range(wide // LANE)
    ]
    sum_ref[...] = jnp.broadcast_to(jnp.concatenate(pieces, axis=0)[None], sum_ref.shape).astype(
        BF16
    )


def out_kernel(
    dims, lines, scal, nf, x_ref, h_ref, cot_ref, got_ref, cnt_ref, rinv_ref, pout_ref, w3_ref,
    out_ref, gs_ref, low_ref, t_ref, sum_ref, vec_ref, es, w3s, sacc,
):
    step = pl.program_id(0)
    width, wide = w3_ref.shape
    frames = dims[0]
    block = 256
    unit = 0.5

    @pl.when(step == 0)
    def _():
        wide_norm(nf, got_ref, cnt_ref, rinv_ref, pout_ref, 1, w3_ref, vec_ref)
        t_ref[...] = jnp.zeros_like(t_ref)
        sacc[...] = jnp.zeros_like(sacc)
        w3s[...] = (w3_ref[...].astype(F32) * (unit * vec_ref[0:1, :])).astype(BF16)

    hT = h_ref[...].T
    for j in range(wide // block):
        lanes = slice(block * j, block * (j + 1))
        es[j % 2] = dot_nn(h_ref[...], w3_ref[:, lanes])
        scale, shift = vec_ref[4:5, lanes], vec_ref[1:2, lanes]

        def own(part, cap, total):
            half = x_ref[part, lanes].astype(F32) + (es[j % 2, part, :] * scale + shift)
            o, both = silu_half(jnp.minimum(half, cap))
            spot = slice(part.start // frames, part.stop // frames)
            out_ref[spot, :, lanes] = o.astype(BF16).reshape(-1, frames, block)
            grad = cot_ref[spot, :, lanes].reshape(-1, block).astype(F32)
            grad = grad * slope_twice(o, both)
            gs_ref[part, lanes] = grad.astype(BF16)
            return total + fold(grad)

        total = each_line(dims, lines, step, scal, block, own)(jnp.zeros((8, block), F32))
        sacc[:, lanes] += total
    wide_tail(hT, gs_ref, w3s, low_ref, t_ref)

    @pl.when(step == pl.num_programs(0) - 1)
    def _():
        wide_sums(w3_ref, t_ref, sacc, vec_ref, sum_ref, unit)


def expand_back_kernel(
    dims, per, scal, nf, low_ref, h_ref, z_ref, u_ref, got_ref, vec_ref, w3_ref,
    go_ref, up_ref, dn_ref, sum_ref, tot_ref, ks, crow, hk, acc,
):
    frames, rows, line = dims
    step = pl.program_id(0)
    width, wide = w3_ref.shape

    @pl.when(step == 0)
    def _():
        totals = jnp.sum(got_ref[...].astype(F32), axis=0)
        count = wide // LANE
        plain = jnp.concatenate([totals[k : k + 1, :] for k in range(count)], axis=1)
        along = jnp.concatenate([totals[k : k + 1, :] for k in range(count, 2 * count)], axis=1)
        tot_ref[:, 0:wide] = plain
        tot_ref[:, wide:] = along
        w3 = w3_ref[...]
        rise, flat = wide_rows_of(nf, plain, along, vec_ref)
        ks[...] = dot_nt((w3.astype(F32) * rise).astype(BF16), w3).astype(BF16)
        spread = [jnp.broadcast_to(one, (16, wide)) for one in split(flat)]
        crow[...] = (dot_nt(spread[0], w3) + dot_nt(spread[1], w3))[0:8]
        acc[...] = jnp.zeros_like(acc)

    hk[...] = dot_nn(h_ref[...], ks[...])

    def own(i):
        part = pl.ds(i, STEP)
        grad = (low_ref[part, :] - crow[0:1, :] - hk[part, :]) * u_ref[part, :].astype(F32)
        go_ref[part, :] = grad.astype(BF16)
        acc[0:8, :] += fold(grad)
        acc[8:16, :] += fold(grad * z_ref[part, :].astype(F32))

    each(line * rows * per, own, 49)
    for k in range(per):
        expand_edges(dims, scal, k * rows * line, go_ref, z_ref, up_ref.at[k], dn_ref.at[k])

    @pl.when(step == pl.num_programs(0) - 1)
    def _():
        share_sums(acc, sum_ref)


def wide_rows_of(nf, plain, along, vec_ref):
    scale, inverse, mean = vec_ref[0:1, :], vec_ref[2:3, :], vec_ref[3:4, :]
    rise = scale * inverse * along * nf[3]
    return rise, scale * plain * nf[3] - rise * mean


def expand_grad_kernel(
    scal, nf, tot_ref, vec_ref, t_ref, gram_ref, w3_ref, mine_ref, sent_ref
):
    width, wide = w3_ref.shape
    rise, flat = wide_rows_of(nf, tot_ref[:, 0:wide], tot_ref[:, wide:], vec_ref)
    column = jnp.broadcast_to(gram_ref[width : width + 1, :], (LANE, width)).T[:, 0:1]
    cross = dot_split(gram_ref[0:width, :], w3_ref[...])
    ge = t_ref[...] * vec_ref[0:1, :] - column * flat - cross * rise
    chips, size = mine_ref.shape[0:2]
    parts = [ge[:, width * k : width * (k + 1)] for k in range(wide // width)]
    parts = [one.reshape(chips, -1, size * width // wide, width) for one in parts]
    hand_over(scal, jnp.concatenate(parts, axis=2), mine_ref, sent_ref)


def expand_edges(dims, scal, base, go_ref, z_ref, up_ref, dn_ref):
    frames, rows, line = dims
    even = scal[scal.shape[0] - 1] == 0
    last = line * (rows - 1)
    first = jnp.where(even, last, 0)
    near = pl.multiple_of(base + first, STEP)
    far = pl.multiple_of(base + last - first, STEP)
    up_ref[0] = go_ref[pl.ds(near, line), :]
    up_ref[1] = z_ref[pl.ds(near, line), :]
    dn_ref[0] = go_ref[pl.ds(far, line), :]
    dn_ref[1] = z_ref[pl.ds(far, line), :]


def norm_rows(nf, got_ref, vec_ref, tot_ref, rows3):
    width = vec_ref.shape[1]
    totals = jnp.sum(got_ref[...], axis=0)
    tot_ref[...] = totals
    rows3[0:1, :] = vec_ref[4:5, :]
    rows3[1:2, :] = vec_ref[4:5, :] * totals[:, 0:width] * nf[3]
    rows3[2:3, :] = vec_ref[4:5, :] * totals[:, width:] * nf[3]


def norm_back(rows3, go, z, mask):
    value = rows3[0:1, :] * go.astype(F32) - rows3[1:2, :] - rows3[2:3, :] * z.astype(F32)
    return value * mask


def depth_back_kernel(
    dims, layer, per, scal, nf, go_ref, above_ref, below_ref, z_ref, got_ref, vec_ref,
    z1_ref, u1_ref, par_ref, w_ref,
    go1_ref, sum_ref, gm_ref, gp_ref, tot_ref, ms, tv, wd, ds, gh, rows3, acc,
):
    step, last = pl.program_id(0), pl.num_programs(0) - 1
    width = w_ref.shape[0]

    @pl.when(step == 0)
    def _():
        norm_rows(nf, got_ref, vec_ref, tot_ref, rows3)
        depth_weights(par_ref, layer, wd, True)
        acc[...] = jnp.zeros_like(acc)

    def body(clip, k, view):
        depth_back_clip(
            dims, layer, scal, view(go_ref), above_ref.at[k], below_ref.at[k], view(z_ref),
            view(z1_ref), view(u1_ref), par_ref, w_ref, view(go1_ref), view(gm_ref), view(gp_ref),
            ms, tv, wd, ds, gh, rows3, acc, clip, per * (last + 1),
        )

    clip_loop(dims, per, body)

    @pl.when(step == last)
    def _():
        share_sums(acc, sum_ref)


def depth_back_clip(
    dims, layer, scal, go_ref, above_ref, below_ref, z_ref, z1_ref, u1_ref, par_ref, w_ref,
    go1_ref, gm_ref, gp_ref, ms, tv, wd, ds, gh, rows3, acc, clip, clips,
):
    frames, rows, line = dims
    width = w_ref.shape[0]
    mask = live_rows(scal[clip], frames, STEP, width)
    near = mask * scal[clips].astype(F32)
    far = mask * scal[clips + 1].astype(F32)
    near_at, far_at = edge_places(scal, clips, line, rows)

    def edge(i):
        part = pl.ds(i, STEP)
        ms[pl.ds(near_at + i, STEP), :] = norm_back(
            rows3, above_ref[0, part, :], above_ref[1, part, :], near
        )
        ms[pl.ds(far_at + i, STEP), :] = norm_back(
            rows3, below_ref[0, part, :], below_ref[1, part, :], far
        )

    each(line, edge, 7)

    def own(i):
        part = pl.ds(i, STEP)
        ms[pl.ds(i + line, STEP), :] = norm_back(rows3, go_ref[part, :], z_ref[part, :], mask)

    each(line * rows, own, 49)

    def shifts(r, carry):
        at = pl.multiple_of(r * line, STEP)
        for half in range(width // LANE):
            lanes = slice(LANE * half, LANE * (half + 1))
            part = pl.ds(at, line)
            value = ms[part, lanes].astype(BF16).astype(F32)
            ms[part, lanes] = value
            frame_shifts(dims, value, tv.at[:, :, lanes], at)
        return carry

    lax.fori_loop(0, rows + 2, shifts, 0, unroll=True)
    gp_ref[...] = tv[1, line : line * (rows + 1), :]

    def store(r, lanes, value):
        gm_ref[line * r : line * (r + 1), lanes] = value.astype(BF16)

    depth_sum(dims, layer, True, par_ref, ms, tv, wd, ds, gh, store)
    gh[...] = dot_nt(gm_ref[...], w_ref[...])

    def first(i):
        part = pl.ds(i, STEP)
        value = gh[part, :] * u1_ref[part, :].astype(F32)
        go1_ref[part, :] = value.astype(BF16)
        acc[0:8, :] += fold(value)
        acc[8:16, :] += fold(value * z1_ref[part, :].astype(F32))

    each(line * rows, first, 49)

def kernel_grads(
    dims, per, scal, mix_ref, gp_ref, gm_ref, h_ref,
    mine_ref, sent_ref, gmix_ref, gdep_ref, tv, mv, gacc, vacc,
):
    step = pl.program_id(0)
    width = h_ref.shape[1]
    halves = width // LANE

    @pl.when(step == 0)
    def _():
        gmix_ref[...] = jnp.zeros_like(gmix_ref)
        gacc[...] = jnp.zeros_like(gacc)
        vacc[...] = jnp.zeros_like(vacc)

    gmix_ref[...] += dot_tn(h_ref[...], gm_ref[...])

    def body(clip, k, view):
        kernel_clip(dims, halves, view(mix_ref, 2), view(gp_ref), tv, mv, gacc, vacc)

    clip_loop(dims, per, body)

    @pl.when(step == pl.num_programs(0) - 1)
    def _():
        one = lax.broadcasted_iota(jnp.int32, (LANE, LANE), 0)
        two = lax.broadcasted_iota(jnp.int32, (LANE, LANE), 1)
        gdep_ref[...] = jnp.zeros_like(gdep_ref)
        for half in range(halves):
            lanes = slice(LANE * half, LANE * (half + 1))
            for i in range(9):
                gdep_ref[3 * i + 1 : 3 * i + 2, lanes] = row_sum(vacc[i, :, lanes])
                for e in (0, 2):
                    k = LANE * (e // 2)
                    part = gacc[half, k : k + LANE, LANE * i : LANE * (i + 1)]
                    gdep_ref[3 * i + e : 3 * i + e + 1, lanes] = row_sum(
                        jnp.where(one == two, part, 0.0)
                    )
        chips, size = mine_ref.shape[0:2]
        taps = jnp.concatenate([gdep_ref[...].T, jnp.zeros((width, width - LANE), F32)], axis=1)
        parts = [gmix_ref[...], taps]
        parts = [one.reshape(chips, -1, size // 2, width) for one in parts]
        hand_over(scal, jnp.concatenate(parts, axis=2), mine_ref, sent_ref)


def kernel_clip(dims, halves, mix_ref, gp_ref, tv, mv, gacc, vacc):
    frames, rows, line = dims

    def shifts(r, carry):
        at = pl.multiple_of(r * line, STEP)
        for half in range(halves):
            lanes = slice(LANE * half, LANE * (half + 1))
            value = mix_ref[pl.ds(at, line), lanes].astype(F32)
            frame_shifts(dims, value, tv.at[:, :, lanes], at)
        return carry

    lax.fori_loop(0, rows + 2, shifts, 0, unroll=True)

    def moves(r, carry):
        at = pl.multiple_of(r * line, STEP)
        for half in range(halves):
            lanes = slice(LANE * half, LANE * (half + 1))
            value = gp_ref[pl.ds(at, line), lanes].astype(F32)
            onward, back = column_moves(dims, value)
            mv[half, pl.ds(at, line), 0:LANE] = back.astype(BF16)
            mv[half, pl.ds(at, line), LANE : 2 * LANE] = onward.astype(BF16)
        return carry

    lax.fori_loop(0, rows, moves, 0, unroll=True)
    for half in range(halves):
        lanes = slice(LANE * half, LANE * (half + 1))
        views = [tv[a, line * b : line * (b + rows), lanes] for a in range(3) for b in range(3)]
        gacc[half] += dot_tn(mv[half], jnp.concatenate(views, axis=1))
        sums = [vacc[i, :, lanes] for i in range(9)]
        for start in range(0, rows * line, line):
            own = gp_ref[start : start + line, lanes].astype(F32)
            onward, back = frame_moves(frames, own)
            for b in range(3):
                seen = mix_ref[start + line * b : start + line * b + line, lanes].astype(F32)
                for a, moved in enumerate((back, own, onward)):
                    sums[3 * a + b] = sums[3 * a + b] + fold(moved * seen)
        for i in range(9):
            vacc[i, :, lanes] = sums[i]


def reduced_grad(dims, lines, step, scal, go_ref, z_ref, rows3, gr_ref):
    def own(part, mask, carry):
        gr_ref[part, :] = norm_back(rows3, go_ref[part, :], z_ref[part, :], mask).astype(BF16)
        return carry

    each_line(dims, lines, step, scal, rows3.shape[1], own, live_rows)(0)


def cross_kernel(
    dims, lines, scal, nf, go_ref, z_ref, got_ref, vec1_ref, gs_ref, du_ref, h_ref,
    vec3_ref, w1_ref, w3_ref,
    gs0_ref, low_ref, t_ref, sum_ref, gr_ref, tot_ref, ds, w1s, w3s, rows3, sacc,
):
    step = pl.program_id(0)
    width, wide = w3_ref.shape
    block = 256
    unit = 0.25

    @pl.when(step == 0)
    def _():
        norm_rows(nf, got_ref, vec1_ref, tot_ref, rows3)
        t_ref[...] = jnp.zeros_like(t_ref)
        sacc[...] = jnp.zeros_like(sacc)
        w3s[...] = (w3_ref[...].astype(F32) * (unit * vec3_ref[0:1, :])).astype(BF16)
        w1s[...] = (w1_ref[...].astype(F32) * 2.0).astype(BF16)

    reduced_grad(dims, lines, step, scal, go_ref, z_ref, rows3, gr_ref)
    hT = h_ref[...].T
    for j in range(wide // block):
        lanes = slice(block * j, block * (j + 1))
        ds[j % 2] = dot_nt(gr_ref[...], w1s[lanes, :])

        def own(part, mask, total):
            value = gs_ref[part, lanes].astype(F32) + ds[j % 2, part, :]
            value = value * du_ref[part, lanes].astype(F32)
            gs0_ref[part, lanes] = value.astype(BF16)
            return total + fold(value)

        total = each_line(dims, lines, step, scal, block, own)(jnp.zeros((8, block), F32))
        sacc[:, lanes] += total
    wide_tail(hT, gs0_ref, w3s, low_ref, t_ref)

    @pl.when(step == pl.num_programs(0) - 1)
    def _():
        wide_sums(w3_ref, t_ref, sacc, vec3_ref, sum_ref, unit)


def reduce_grad_kernel(unit, scal, x_ref, gr_ref, mine_ref, sent_ref, gacc):
    step = pl.program_id(0)

    @pl.when(step == 0)
    def _():
        gacc[...] = jnp.zeros_like(gacc)

    gacc[...] += dot_tn(gr_ref[...], x_ref[...])

    @pl.when(step == pl.num_programs(0) - 1)
    def _():
        chips, size, width = mine_ref.shape
        value = (unit * gacc[...].T).reshape(chips, -1, size, width)
        hand_over(scal, value, mine_ref, sent_ref)


def last_grad_kernel(
    dims, lines, scal, nf, go_ref, z_ref, got_ref, vec1_ref, x_ref,
    gr_ref, mine_ref, sent_ref, tot_ref, rows3, gacc,
):
    step = pl.program_id(0)

    @pl.when(step == 0)
    def _():
        norm_rows(nf, got_ref, vec1_ref, tot_ref, rows3)
        gacc[...] = jnp.zeros_like(gacc)

    reduced_grad(dims, lines, step, scal, go_ref, z_ref, rows3, gr_ref)
    gacc[...] += dot_tn(gr_ref[...], x_ref[...].reshape(-1, x_ref.shape[2]))

    @pl.when(step == pl.num_programs(0) - 1)
    def _():
        chips, size, width = mine_ref.shape
        hand_over(scal, gacc[...].T.reshape(chips, -1, size, width), mine_ref, sent_ref)


def input_kernel(gr_ref, gs_ref, w1_ref, out_ref):
    w1 = w1_ref[...].reshape(-1, w1_ref.shape[2])
    value = dot_nt(gr_ref[...], w1) + 0.25 * gs_ref[...].astype(F32)
    out_ref[...] = value.astype(BF16).reshape(out_ref.shape)


ALL = ("clip", "outer", "inner")
CHIPS = ("clip", "outer")
SP = ("outer", "inner")


def share(rows):
    return lax.all_to_all(rows, ALL, 0, 0)


def gather(value):
    return share(jnp.broadcast_to(value[None], (lax.axis_size(ALL),) + value.shape))


def neighbours(near, far):
    peers = lax.axis_size(SP)
    first = [(i, i + 1) for i in range(0, peers - 1, 2)]
    second = [(i, i + 1) for i in range(1, peers - 1, 2)]
    near = lax.ppermute(near, SP, first + [(j, i) for i, j in first])
    far = lax.ppermute(far, SP, second + [(j, i) for i, j in second])
    return near, far


def swap(value):
    peers = lax.axis_size("inner")
    return lax.ppermute(value, "inner", [(i, (i + 1) % peers) for i in range(peers)])


def after(value, other):
    return lax.optimization_barrier((value, other))[0]


def on_device(
    features, strides, cotangent, w_reduce, w_mix, w_expand, w_depth,
    gains_mid, biases_mid, gains_out, biases_out,
):
    clips, frames, rows, columns, wide = features.shape
    width = w_mix.shape[2]
    peers, chips = lax.axis_size(ALL), lax.axis_size(CHIPS)
    inner = lax.axis_size("inner")
    sp_size = lax.axis_size(SP)
    part, place = lax.axis_index("inner"), lax.axis_index(ALL)
    sp_at = lax.axis_index(SP)
    line = columns * frames
    per_clip = rows * line
    voxels = clips * per_clip
    r1, r2 = w_reduce.shape[1], w_mix.shape[1]
    r4 = w_depth.shape[2]
    r5 = gains_out.shape[1] // r4
    blocks = wide // width

    def from_cores(near):
        held = [near]
        for _ in range(inner - 1):
            held.append(swap(held[-1]))
        turns = [lax.rem(part - c + inner, inner) for c in range(inner)]
        whole = jnp.stack([lax.select_n(turn, *held) for turn in turns], axis=1)
        return whole.reshape((peers,) + near.shape[1:])

    def wide_weight(rows_of_all):
        one = rows_of_all.reshape(peers, blocks, r2, width).transpose(0, 2, 1, 3)
        return one.reshape(peers * r2, wide)

    height = r1 + r2 + 8
    height += -height % 16
    whole = lambda value: full(value.shape)
    raw = (w_reduce, w_mix, w_depth.transpose(0, 2, 1), gains_mid, biases_mid, gains_out,
           biases_out)
    packed = call(
        pack_kernel, 1, [whole(one) for one in raw], full((chips, height, width)),
        jax.ShapeDtypeStruct((chips, height, width), BF16), [], 1,
    )(*raw)
    near = lax.all_to_all(packed, CHIPS, 0, 0)
    x = features.transpose(0, 2, 3, 1, 4).reshape(voxels // frames, frames, wide)
    counts = frames // strides
    by_group = jnp.sum(counts.reshape(-1, clips), axis=1) * (rows * columns)
    by_device = jnp.repeat(by_group, sp_size).astype(F32)
    local = lax.dynamic_slice_in_dim(counts, lax.axis_index("clip") * clips, clips)
    odd = lax.rem(sp_at, 2)
    has_near = (odd == 1) | (sp_at < sp_size - 1)
    has_far = jnp.where(odd == 1, sp_at < sp_size - 1, sp_at > 0)
    way = jnp.where(odd == 1, -1, 1)
    base = lax.axis_index("clip") * sp_size
    near_place = base + jnp.clip(sp_at + way, 0, sp_size - 1)
    far_place = base + jnp.clip(sp_at - way, 0, sp_size - 1)
    edges = jnp.stack(
        [has_near.astype(jnp.int32), has_far.astype(jnp.int32), near_place, far_place, odd]
    )
    scal = jnp.concatenate([local.astype(jnp.int32), edges])
    own = jnp.sum(local).astype(F32) * (rows * columns)
    total = jnp.sum(by_device)
    nf = jnp.stack([own, total, 1.0 / own, 1.0 / total])
    cnt = jnp.broadcast_to(by_device[:, None, None], (peers, 1, LANE))
    rinv = jnp.broadcast_to(1.0 / by_device[:, None], (peers, LANE))

    sizes = [r2 * blocks + r1, r2 * blocks + r2]
    sizes = [(chips, one + -one % 16, width) for one in sizes]
    raw = (w_reduce, w_mix, w_expand)
    late_one, late_two = call(
        late_pack_kernel, 1, [whole(one) for one in raw], [full(one) for one in sizes],
        [jax.ShapeDtypeStruct(one, BF16) for one in sizes], [], 1,
    )(*raw)
    near, late_one, late_two, scal, nf, cnt, rinv = lax.optimization_barrier(
        (near, late_one, late_two, scal, nf, cnt, rinv)
    )
    early = from_cores(near)
    w2 = [early[:, r1 : r1 + r2].reshape(-1, width)]
    at = r1 + r2
    taps = early[:, at : at + r4, 0:64].reshape(-1, 64).T
    taps = [taps[32 * k : 32 * k + 27] for k in range(2)]
    mids = early[:, at : at + 8, 64 : 64 + r4].transpose(1, 0, 2).reshape(8, width)
    par = jnp.concatenate([*taps, mids, jnp.zeros((2, width), BF16)], axis=0).astype(F32)
    pout = early[:, at : at + 4, 96 : 96 + r4 * r5].transpose(1, 0, 2).reshape(4, wide)
    pout = pout.astype(F32)

    struct = jax.ShapeDtypeStruct
    dims = (frames, rows, line)
    lines = rows
    steps = clips * rows // lines
    many_lines = 2 * rows if clips % 2 == 0 else rows
    few = clips * rows // many_lines
    tall = (rows + 2) * line
    by_step = lambda size: pl.BlockSpec((lines * line, size), lambda s: (s, 0))
    thin, broad = by_step(width), by_step(wide)

    def by_clip(name):
        per = PER[name] if clips % PER[name] == 0 else 1
        field = pl.BlockSpec((per * per_clip, width), lambda c: (c, 0))
        tall_field = pl.BlockSpec((per * tall, width), lambda c: (c, 0))
        edge_one = pl.BlockSpec((per, line, width), lambda c: (c, 0, 0))
        edge_two = pl.BlockSpec((per, 2, line, width), lambda c: (c, 0, 0, 0))
        return per, field, tall_field, edge_one, edge_two

    native = pl.BlockSpec((lines * line // frames, frames, wide), lambda s: (s, 0, 0))
    size = many_lines * line
    big_thin = pl.BlockSpec((size, width), lambda s: (s, 0))
    big_broad = pl.BlockSpec((size, wide), lambda s: (s, 0))
    big_native = pl.BlockSpec((size // frames, frames, wide), lambda s: (s, 0, 0))
    native_shape = struct((voxels // frames, frames, wide), BF16)
    narrow = lambda kind: struct((voxels, width), kind)
    wide_shape = struct((voxels, wide), BF16)
    edge = struct((clips, line, width), BF16)
    lines_kept = pltpu.VMEM((2, clips, line, width), F32)
    pair = struct((clips, 2, line, width), BF16)
    flat = lambda *shape: struct(shape, F32)
    two = (peers, 1, 2 * width)
    three = (peers, 1, width + wide)
    many = (peers, 2 * wide // LANE, LANE)
    vec, vec_wide = (8, width), (8, wide)
    owned = struct((chips, r1, width), BF16)
    owned_taps = struct((chips, 2 * r2, width), BF16)

    reduced, up, dn, stats = call(
        functools.partial(first_kernel, dims, many_lines), few,
        [smem(), smem(), big_native, full((peers, r1, width))],
        [big_thin, full(edge.shape), full(edge.shape), full(two)],
        [narrow(F32), edge, edge, flat(*two)],
        [pltpu.VMEM((24, width), F32), lines_kept], 6,
    )(scal, nf, x, early)

    depth_scratch = [
        pltpu.VMEM((tall, width), F32), pltpu.VMEM((3, tall, width), BF16),
        pltpu.VMEM((width // LANE, 9 * LANE, 2 * LANE), BF16),
        pltpu.VMEM((width // LANE, per_clip, 2 * LANE), F32),
    ]
    above, below = neighbours(up, dn)
    got = share(stats)
    got, cnt, par, w2[0] = lax.optimization_barrier((got, cnt, par, w2[0]))
    late_one = after(late_one, (got, above, below))
    near = lax.all_to_all(late_one, CHIPS, 0, 0)
    w1, w3 = [early], []
    stored = []
    for layer in range(2):
        if layer == 1:
            above, below = neighbours(up, dn)
            stats, near = lax.optimization_barrier((stats, near))
            got = share(stats)
            late = from_cores(near)
            w2.append(late[:, r2 * blocks : r2 * blocks + r2].reshape(-1, width))
        per, field, tall_field, edge_one, edge_two = by_clip("mix")
        mixed, spatial, stats, vec1 = call(
            functools.partial(mix_kernel, dims, layer, per), clips // per,
            [smem(), smem(), field, edge_one, edge_one, full(two),
             full((peers, 1, LANE)), full((64, width)), full((width, width))],
            [tall_field, field, full(two), full(vec)],
            [struct((clips * tall, width), BF16), narrow(F32), flat(*two), flat(*vec)],
            [pltpu.VMEM((tall, width), BF16), *depth_scratch, pltpu.VMEM((24, width), F32)], 10,
        )(scal, nf, reduced, above, below, got, cnt, par, w2[layer])
        got = share(stats)
        per, field, tall_field, edge_one, edge_two = by_clip("slopes")
        z1, u1, h1 = call(
            functools.partial(slopes_kernel, dims, per), clips // per,
            [smem(), field, full(vec)], [field] * 3, [narrow(BF16)] * 3, [], 5,
        )(scal, reduced, vec1)
        got, z1, u1, h1 = lax.optimization_barrier((got, z1, u1, h1))
        if layer == 1:
            w3.append(wide_weight(late[:, : r2 * blocks]))
        else:
            late = from_cores(after(near, stats))
            w3.append(wide_weight(late[:, : r2 * blocks]))
            at = r2 * blocks
            w1.append(late[:, at : at + r1].reshape(-1, width))
        per, field, tall_field, edge_one, edge_two = by_clip("hidden")
        h2, stats, gram, vec2 = call(
            functools.partial(hidden_kernel, dims, layer, per), clips // per,
            [smem(), smem(), field, full(two), full((peers, 1, LANE)),
             full((64, width)), full((width, wide))],
            [field, full(three), full((width + 8, width)), full(vec)],
            [narrow(BF16), flat(*three), flat(width + 8, width), flat(*vec)],
            [pltpu.VMEM((8, width), F32)], 5,
        )(scal, nf, spatial, got, cnt, par, w3[layer])
        got = share(stats)
        per, field, tall_field, edge_one, edge_two = by_clip("slopes")
        z2, u2 = call(
            functools.partial(slopes_kernel, dims, per), clips // per,
            [smem(), field, full(vec)], [field] * 2, [narrow(BF16)] * 2, [], 5,
        )(scal, spatial, vec2)
        got, z2, u2 = lax.optimization_barrier((got, z2, u2))
        if layer == 0:
            got, pout, rinv, w1[1] = lax.optimization_barrier((got, pout, rinv, w1[1]))
            near = lax.all_to_all(after(late_two, got), CHIPS, 0, 0)
        norm_specs = [full(three), full((peers, 1, LANE)), full((peers, LANE)),
                      full((4, wide)), full((width, wide))]
        norm_args = (got, cnt, rinv, pout, w3[layer])
        if layer == 0:
            carried, slope, reduced, up, dn, stats, vec3 = call(
                functools.partial(join_kernel, dims, lines), steps,
                [smem(), smem(), native, thin] + norm_specs + [full((wide, width))],
                [broad, broad, thin, full(edge.shape), full(edge.shape), full(two),
                 full(vec_wide)],
                [wide_shape, wide_shape, narrow(F32), edge, edge, flat(*two), flat(*vec_wide)],
                [pltpu.VMEM((2, lines * line, 256), F32), pltpu.VMEM((24, width), F32),
                 lines_kept], 12,
            )(scal, nf, x, h2, *norm_args, w1[1])
        else:
            cot = cotangent.transpose(0, 2, 3, 1, 4).reshape(voxels // frames, frames, wide)
            output, gs, low, t, sums, vec3 = call(
                functools.partial(out_kernel, dims, lines), steps,
                [smem(), smem(), broad, thin, native] + norm_specs,
                [native, broad, thin, full((width, wide)), full(many), full(vec_wide)],
                [native_shape, wide_shape, narrow(F32), flat(width, wide), struct(many, BF16),
                 flat(*vec_wide)],
                [pltpu.VMEM((2, lines * line, 256), F32), pltpu.VMEM((width, wide), BF16),
                 pltpu.VMEM((8, wide), F32)], 15,
            )(scal, nf, carried, h2, cot, *norm_args)
        stored.append((z1, u1, h1, vec1, mixed, z2, u2, h2, vec2, gram, vec3))

    def voxel_form(value):
        return value.reshape(clips, rows, columns, frames, wide).transpose(0, 3, 1, 2, 4)

    def sum_cores(*pieces):
        if inner == 1:
            return jnp.concatenate([mine for mine, _ in pieces], axis=1)
        return jnp.concatenate([mine + swap(sent) for mine, sent in pieces], axis=1)

    results = [None, None]
    for layer in (1, 0):
        z1, u1, h1, vec1, mixed, z2, u2, h2, vec2, gram, vec3 = stored[layer]
        if layer == 0:
            sums = after(sums, first)
        got = share(sums)
        if layer == 0:
            got, reduce_mine, reduce_sent = lax.optimization_barrier(
                (got, reduce_mine, reduce_sent)
            )
        per, field, tall_field, edge_one, edge_two = by_clip("expand")
        go2, up, dn, sums, tot3 = call(
            functools.partial(expand_back_kernel, dims, per), clips // per,
            [smem(), smem(), field, field, field, field, full(many), full(vec_wide),
             full((width, wide))],
            [field, edge_two, edge_two, full(two), full((1, 2 * wide))],
            [narrow(BF16), pair, pair, flat(*two), flat(1, 2 * wide)],
            [pltpu.VMEM((width, width), BF16), pltpu.VMEM(vec, F32),
             pltpu.VMEM((per * per_clip, width), F32), pltpu.VMEM((16, width), F32)], 6,
        )(scal, nf, low, h2, z2, u2, got, vec3, w3[layer])
        expand_mine, expand_sent = call(
            expand_grad_kernel, 1,
            [smem(), smem(), full((1, 2 * wide)), full(vec_wide), full((width, wide)),
             full((width + 8, width)), full((width, wide))],
            [full(owned.shape), full(owned.shape)], [owned, owned], [], 3,
        )(scal, nf, tot3, vec3, t, gram, w3[layer])
        above, below = neighbours(up, dn)
        got = share(sums)
        got, expand_mine, expand_sent = lax.optimization_barrier((got, expand_mine, expand_sent))
        expands = (expand_mine, expand_sent)
        if layer == 0:
            second = sum_cores((reduce_mine, reduce_sent), expands)
            second = lax.all_to_all(after(second, (got, above, below)), CHIPS, 0, 0)
        per, field, tall_field, edge_one, edge_two = by_clip("depth")
        go1, sums, gm, gp, tot2 = call(
            functools.partial(depth_back_kernel, dims, layer, per), clips // per,
            [smem(), smem(), field, edge_two, edge_two, field, full(two), full(vec), field,
             field, full((64, width)), full((width, width))],
            [field, full(two), field, field, full((1, 2 * width))],
            [narrow(BF16), flat(*two), narrow(BF16), narrow(BF16), flat(1, 2 * width)],
            [*depth_scratch, pltpu.VMEM((per_clip, width), F32), pltpu.VMEM(vec, F32),
             pltpu.VMEM((16, width), F32)], 12,
        )(scal, nf, go2, above, below, z2, got, vec2, z1, u1, par, w2[layer])
        if layer == 0:
            sums = after(sums, second)
        got = share(sums)
        per, field, tall_field, edge_one, edge_two = by_clip("grads")
        taps_mine, taps_sent = call(
            functools.partial(kernel_grads, dims, per), clips // per,
            [smem(), tall_field, field, field, field],
            [full(owned_taps.shape), full(owned_taps.shape)],
            [owned_taps, owned_taps],
            [pltpu.VMEM((width, width), F32), pltpu.VMEM((LANE, width), F32),
             pltpu.VMEM((3, tall, width), BF16),
             pltpu.VMEM((width // LANE, per_clip, 2 * LANE), BF16),
             pltpu.VMEM((width // LANE, 2 * LANE, 9 * LANE), F32),
             pltpu.VMEM((9, 8, width), F32)], 12,
        )(scal, mixed, gp, gm, h1)
        got, taps_mine, taps_sent = lax.optimization_barrier((got, taps_mine, taps_sent))
        if layer == 1:
            first = lax.all_to_all(sum_cores((taps_mine, taps_sent), expands), CHIPS, 0, 0)
        if layer == 1:
            h2_0, vec3_0 = stored[0][7], stored[0][10]
            gs, low, t, sums, gr, tot1 = call(
                functools.partial(cross_kernel, dims, lines), steps,
                [smem(), smem(), thin, thin, full(two), full(vec), broad, broad, thin,
                 full(vec_wide), full((wide, width)), full((width, wide))],
                [broad, thin, full((width, wide)), full(many), thin, full((1, 2 * width))],
                [wide_shape, narrow(F32), flat(width, wide), struct(many, BF16), narrow(BF16),
                 flat(1, 2 * width)],
                [pltpu.VMEM((2, lines * line, 256), F32), pltpu.VMEM((wide, width), BF16),
                 pltpu.VMEM((width, wide), BF16), pltpu.VMEM(vec, F32),
                 pltpu.VMEM((8, wide), F32)], 15,
            )(scal, nf, go1, z1, got, vec1, gs, slope, h2_0, vec3_0, w1[1], w3[0])
            reduce_mine, reduce_sent = call(
                functools.partial(reduce_grad_kernel, 2.0), few,
                [smem(), big_broad, big_thin], [full(owned.shape), full(owned.shape)], [owned, owned],
                [pltpu.VMEM((width, wide), F32)], 5,
            )(scal, carried, gr)
        else:
            gr, mine, sent, tot1 = call(
                functools.partial(last_grad_kernel, dims, many_lines), few,
                [smem(), smem(), big_thin, big_thin, full(two), full(vec), big_native],
                [big_thin, full(owned.shape), full(owned.shape), full((1, 2 * width))],
                [narrow(BF16), owned, owned, flat(1, 2 * width)],
                [pltpu.VMEM(vec, F32), pltpu.VMEM((width, wide), F32)], 6,
            )(scal, nf, go1, z1, got, vec1, x)
            input_grad = call(
                input_kernel, few, [big_thin, big_broad, full((peers, r1, width))], big_native,
                native_shape, [], 6,
            )(gr, gs, early)
        results[layer] = (tot1, tot2, tot3)

    last = sum_cores((mine, sent), (taps_mine, taps_sent))
    last = jnp.sum(lax.all_to_all(last, CHIPS, 0, 0).astype(F32), axis=0)
    first = jnp.sum(first.astype(F32), axis=0)
    second = jnp.sum(second.astype(F32), axis=0)
    to_wide = lambda one: one.reshape(blocks, r2, width).transpose(1, 0, 2).reshape(r2, wide)
    grad_reduce = jnp.stack([last[0:r1], second[0:r1]])
    grad_mix = jnp.stack([last[r1 : r1 + r2], first[0:r2]])
    depths = (last[r1 + r2 : r1 + r2 + r4], first[r2 : r2 + r4])
    grad_depth = jnp.stack([one[:, 0:27].T for one in depths])
    grad_expand = jnp.stack([to_wide(second[r1:]), to_wide(first[r2 + r4 :])])

    mid_sums = jnp.concatenate(
        [
            jnp.concatenate([results[layer][0], results[layer][1]], axis=0).reshape(2, 2, width)
            for layer in range(2)
        ],
        axis=0,
    )
    mid = lax.dynamic_slice_in_dim(mid_sums, place * r4, r4, axis=2)
    out_sums = jnp.concatenate([results[layer][2].reshape(1, 2, wide) for layer in range(2)])
    r6 = gains_out.shape[1]
    outs = lax.dynamic_slice_in_dim(out_sums, place * r6, r6, axis=2)

    return (
        voxel_form(output),
        voxel_form(input_grad),
        grad_reduce,
        grad_mix,
        grad_expand,
        grad_depth,
        mid[:, 1].reshape(2, 2, r4),
        mid[:, 0].reshape(2, 2, r4),
        outs[:, 1],
        outs[:, 0],
    )


def solution(mesh):
    clip_size, sp_size = mesh.shape["clip"], mesh.shape["sp"]
    inner = 2 if sp_size % 2 == 0 else 1
    divided = Mesh(mesh.devices.reshape(clip_size, sp_size // inner, inner), ALL)
    activations = P("clip", None, SP, None, None)
    middle, last, vectors = P(None, ALL, None), P(None, None, ALL), P(None, ALL)
    return jax.shard_map(
        on_device,
        mesh=divided,
        in_specs=(
            activations, P(), activations, middle, middle, middle, last, last, last, vectors,
            vectors,
        ),
        out_specs=(
            activations, activations, middle, middle, middle, last, last, last, vectors, vectors,
        ),
        check_vma=False,
    )
```

```python
import functools

import jax
import jax.numpy as jnp
from jax import lax
from jax.experimental import pallas as pl
from jax.experimental.pallas import tpu as pltpu
from jax.sharding import Mesh, PartitionSpec as P

epsilon = 1e-05
F32 = jnp.float32
BF16 = jnp.bfloat16
LANE = 128
STEP = 16
COST = 3.0e6
PER = {"mix": 1, "hidden": 2, "expand": 2, "depth": 1, "grads": 1, "slopes": 2}


def dot_nn(left, right):
    return lax.dot_general(left, right, (((1,), (0,)), ((), ())), preferred_element_type=F32)


def dot_nt(left, right):
    return lax.dot_general(left, right, (((1,), (1,)), ((), ())), preferred_element_type=F32)


def dot_tn(left, right):
    return lax.dot_general(left, right, (((0,), (0,)), ((), ())), preferred_element_type=F32)


def split(value):
    high = value.astype(BF16)
    return high, (value - high.astype(F32)).astype(BF16)


def dot_split(left, right):
    high, rest = split(left)
    return dot_nn(high, right) + dot_nn(rest, right)


def fold(value):
    return jnp.sum(value.reshape(-1, 8, value.shape[-1]), axis=0)


def row_sum(value):
    return jnp.sum(value, axis=0, keepdims=True)


def live_rows(count, frames, rows, width):
    at = lax.rem(lax.broadcasted_iota(jnp.int32, (rows, width), 0), frames)
    return jnp.where(at < count, 1.0, 0.0)


def live_cap(count, frames, rows, width):
    return jnp.where(live_rows(count, frames, rows, width) > 0.5, 3e38, -60.0)


def full(shape):
    return pl.BlockSpec(shape, lambda *_: (0,) * len(shape))


def smem():
    return pl.BlockSpec(memory_space=pltpu.SMEM)


def call(body, steps, in_specs, out_specs, out_shape, scratch, micros):
    return pl.pallas_call(
        body,
        grid=(steps,),
        in_specs=in_specs,
        out_specs=out_specs,
        out_shape=out_shape,
        scratch_shapes=scratch,
        cost_estimate=pl.CostEstimate(
            flops=0, transcendentals=0, bytes_accessed=int(micros * COST)
        ),
        compiler_params=pltpu.CompilerParams(
            dimension_semantics=("arbitrary",), vmem_limit_bytes=58 * 2**20
        ),
    )


def each(count, body, unroll=1):
    def step(i, carry):
        body(pl.multiple_of(i * STEP, STEP))
        return carry

    lax.fori_loop(0, count // STEP, step, 0, unroll=unroll)


def clip_loop(dims, per, body):
    frames, rows, line = dims
    size = rows * line
    step = pl.program_id(0)

    def one(k, carry):
        def view(ref, extra=0):
            length = size + extra * line
            return ref.at[pl.ds(pl.multiple_of(k * length, STEP), length), :]

        body(step * per + k, k, view)
        return carry

    lax.fori_loop(0, per, one, 0)


def merge_stats(means, squares, counts, total):
    mean = jnp.sum(means * counts, axis=0) / total
    away = means - mean[None]
    spread = jnp.sum(squares + counts * away * away, axis=0) / total
    return mean, lax.rsqrt(jnp.maximum(spread, 0.0) + epsilon)


def narrow_norm(nf, got_ref, cnt_ref, gain, bias, vec_ref):
    width = vec_ref.shape[1]
    mean, inverse = merge_stats(
        got_ref[:, :, 0:width], got_ref[:, :, width:], cnt_ref[:, :, 0:1], nf[1]
    )
    scale = gain * inverse
    vec_ref[...] = jnp.zeros_like(vec_ref)
    vec_ref[0:1, :] = inverse
    vec_ref[1:2, :] = -mean * inverse
    vec_ref[2:3, :] = 0.5 * scale
    vec_ref[3:4, :] = 0.5 * (bias - mean * scale)
    vec_ref[4:5, :] = scale


def silu_half(half):
    both = jnp.tanh(half) + 1.0
    return half * both, both


def slope_of(value, both):
    return 0.5 * slope_twice(value, both)


def slope_twice(value, both):
    return both + value * (2.0 - both)


def line_stats(nf, scal, dims, read, lines, first_line, is_first, acc, st_ref):
    frames, rows, line = dims
    width = acc.shape[1]

    @pl.when(is_first)
    def _():
        mask = live_rows(scal[0], frames, STEP, width)
        total = jnp.zeros((8, width), F32)
        for i in range(line // STEP):
            total = total + fold(read(0, i * STEP) * mask)
        acc[...] = jnp.zeros_like(acc)
        alive = (scal[0] * (line // frames)).astype(F32)
        acc[0:1, :] = row_sum(total) / alive

    pivot = acc[0:1, :]

    def one(at, carry):
        plain, square = carry
        mask = live_rows(scal[(first_line + at) // rows], frames, STEP, width)
        for i in range(line // STEP):
            away = (read(at, i * STEP) - pivot) * mask
            plain = plain + fold(away)
            square = square + fold(away * away)
        return plain, square

    zero = jnp.zeros((8, width), F32)
    plain, square = lax.fori_loop(0, lines, one, (zero, zero), unroll=True)
    acc[8:16, :] += plain
    acc[16:24, :] += square


def edge_places(scal, clips, line, rows):
    last = line * (rows + 1)
    near = jnp.where(scal[scal.shape[0] - 1] == 0, last, 0)
    return pl.multiple_of(near, STEP), pl.multiple_of(last - near, STEP)


def hand_over(scal, value, mine_ref, sent_ref):
    even = scal[scal.shape[0] - 1] == 0
    other = value.shape[1] - 1
    mine_ref[...] = jnp.where(even, value[:, 0], value[:, other]).astype(BF16)
    sent_ref[...] = jnp.where(even, value[:, other], value[:, 0]).astype(BF16)


def finish_stats(nf, acc, st_ref):
    plain, square = row_sum(acc[8:16, :]), row_sum(acc[16:24, :])
    width = acc.shape[1]
    peers = st_ref.shape[0]
    st_ref[:, :, 0:width] = jnp.broadcast_to(acc[0:1, :] + plain * nf[2], (peers, 1, width))
    spread = square - plain * plain * nf[2]
    st_ref[:, :, width:] = jnp.broadcast_to(spread, (peers, 1, width))


def share_sums(acc, sum_ref):
    width = acc.shape[1]
    peers = sum_ref.shape[0]
    for k in range(2):
        one = row_sum(acc[8 * k : 8 * k + 8, :])
        sum_ref[:, :, width * k : width * (k + 1)] = jnp.broadcast_to(one, (peers, 1, width))


def depth_weights(par_ref, layer, wd, flip):
    one = lax.broadcasted_iota(jnp.int32, (LANE, LANE), 0)
    two = lax.broadcasted_iota(jnp.int32, (LANE, LANE), 1)
    eye = jnp.where(one == two, 1.0, 0.0)
    for half in range(wd.shape[0]):
        for i in range(9):
            for e in (0, 2):
                tap = 3 * i + e
                at = 27 * layer + (26 - tap if flip else tap)
                row = par_ref[at : at + 1, LANE * half : LANE * (half + 1)]
                k = LANE * (e // 2)
                wd[half, LANE * i : LANE * (i + 1), k : k + LANE] = (eye * row).astype(BF16)


def frame_moves(frames, value):
    width = value.shape[1]
    groups = value.reshape(-1, 8, width)
    here = lax.rem(lax.broadcasted_iota(jnp.int32, (1, 8, width), 1), frames)
    onward = jnp.where(here > 0, pltpu.roll(groups, 1, 1), 0.0)
    back = jnp.where(here < frames - 1, pltpu.roll(groups, 7, 1), 0.0)
    return onward.reshape(value.shape), back.reshape(value.shape)


def frame_shifts(dims, value, tv, at):
    onward, back = frame_moves(dims[0], value)
    part = pl.ds(at, value.shape[0])
    tv[0, part, :] = onward.astype(BF16)
    tv[1, part, :] = value.astype(BF16)
    tv[2, part, :] = back.astype(BF16)


def column_moves(dims, value):
    frames, rows, line = dims
    at = lax.broadcasted_iota(jnp.int32, (8, value.shape[1]), 0)
    onward = pltpu.roll(value, frames, 0)
    top = jnp.where(at >= frames, onward[0:8], 0.0)
    onward = jnp.concatenate([top, onward[8:]], axis=0)
    back = pltpu.roll(value, line - frames, 0)
    bottom = jnp.where(at < 8 - frames, back[line - 8 :], 0.0)
    return onward, jnp.concatenate([back[: line - 8], bottom], axis=0)


def depth_sum(dims, layer, flip, par_ref, ms, tv, wd, ds, temp, store):
    frames, rows, line = dims
    halves = wd.shape[0]
    piece = line // 2 if line % (2 * 8) == 0 else line
    for half in range(halves):
        lanes = slice(LANE * half, LANE * (half + 1))
        views = [tv[a, line * b : line * (b + rows), lanes] for a in range(3) for b in range(3)]
        ds[half] = dot_nn(jnp.concatenate(views, axis=1), wd[half])
        taps = []
        for i in range(9):
            tap = 3 * i + 1
            at = 27 * layer + (26 - tap if flip else tap)
            taps.append(par_ref[at : at + 1, lanes])
        for start in range(0, rows * line, piece):
            seen = [ms[start + line * b : start + line * b + piece, lanes] for b in range(3)]
            sums = []
            for a in range(3):
                one = seen[0] * taps[3 * a]
                one = one + seen[1] * taps[3 * a + 1]
                sums.append(one + seen[2] * taps[3 * a + 2])
            onward, _ = frame_moves(frames, sums[0])
            _, back = frame_moves(frames, sums[2])
            temp[start : start + piece, lanes] = onward + sums[1] + back
    for half in range(halves):
        lanes = slice(LANE * half, LANE * (half + 1))
        for r in range(rows):
            part = slice(line * r, line * (r + 1))
            onward, _ = column_moves(dims, ds[half, part, 0:LANE])
            _, back = column_moves(dims, ds[half, part, LANE : 2 * LANE])
            store(r, lanes, onward + temp[part, lanes] + back)


def pack_kernel(wr_ref, wm_ref, wd_ref, gm_ref, bm_ref, go_ref, bo_ref, out_ref):
    r1, width = wr_ref.shape[1:]
    r2 = wm_ref.shape[1]
    r4, taps = wd_ref.shape[1:]
    r6 = go_ref.shape[1]
    zeros = lambda rows, size: jnp.zeros((rows, size), F32)
    part = [wd_ref[k].astype(F32) for k in range(2)]
    if r4 < 8:
        part = [jnp.concatenate([one, zeros(8 - r4, taps)], axis=0) for one in part]
    pad = zeros(8, 32 - taps)
    mids = [gm_ref[k].astype(F32) for k in range(2)] + [bm_ref[k].astype(F32) for k in range(2)]
    mids = jnp.concatenate(mids, axis=0)
    outs = jnp.concatenate([go_ref[...].astype(F32), bo_ref[...].astype(F32)], axis=0)
    mids = jnp.concatenate([mids, zeros(8, 32 - r4)], axis=1)
    outs = jnp.concatenate([outs, zeros(4, r6)], axis=0)
    small = [part[0], pad, part[1], pad, mids, outs]
    small.append(zeros(8, width - 96 - r6))
    rest = out_ref.shape[1] - r1 - r2 - 8
    rows = [wr_ref[0].astype(F32), wm_ref[0].astype(F32), jnp.concatenate(small, axis=1)]
    if rest:
        rows.append(zeros(rest, width))
    block = jnp.concatenate(rows, axis=0).astype(BF16)
    for k in range(out_ref.shape[0]):
        out_ref[k] = block


def late_pack_kernel(by, wr_ref, wm_ref, we_ref, one_ref, two_ref, cnt_ref, rinv_ref):
    width = wr_ref.shape[2]
    for k in range(cnt_ref.shape[0]):
        count = jnp.full((1, LANE), by[k], F32)
        cnt_ref[k] = count
        rinv_ref[k : k + 1, :] = 1.0 / count
    zeros = lambda rows: jnp.zeros((rows, width), F32)
    for layer, out_ref in enumerate((one_ref, two_ref)):
        wide = we_ref[layer].astype(F32)
        rows = [wide[:, k : k + width] for k in range(0, wide.shape[1], width)]
        rows.append((wr_ref if layer == 0 else wm_ref)[1].astype(F32))
        rest = out_ref.shape[1] - sum(one.shape[0] for one in rows)
        if rest:
            rows.append(zeros(rest))
        block = jnp.concatenate(rows, axis=0).astype(BF16)
        for k in range(out_ref.shape[0]):
            out_ref[k] = block


def first_kernel(dims, lines, scal, nf, x_ref, w_ref, red_ref, up_ref, dn_ref, st_ref, acc, lines_kept):
    step = pl.program_id(0)
    x = x_ref[...].reshape(-1, x_ref.shape[2])
    red_ref[...] = dot_nn(x, w_ref[...].reshape(-1, w_ref.shape[2]))
    reduced_tail(dims, lines, step, scal, nf, red_ref, up_ref, dn_ref, st_ref, acc, lines_kept)


def reduced_tail(dims, lines, step, scal, nf, red_ref, up_ref, dn_ref, st_ref, acc, lines_kept):
    frames, rows, line = dims
    read = lambda at, i: red_ref[pl.ds(pl.multiple_of(line * at, STEP) + i, STEP), :]
    line_stats(nf, scal, dims, read, lines, step * lines, step == 0, acc, st_ref)
    for k in range(lines // rows):
        clip, at = step * (lines // rows) + k, k * rows * line
        even = scal[scal.shape[0] - 1] == 0
        last = line * (rows - 1)
        near = jnp.where(even, last, 0)
        for way, start in enumerate((near, last - near)):
            part = pl.ds(pl.multiple_of(at + start, STEP), line)
            lines_kept[way, clip] = red_ref[part, :]

    @pl.when(step == pl.num_programs(0) - 1)
    def _():
        finish_stats(nf, acc, st_ref)
        mean = acc[0:1, :] + row_sum(acc[8:16, :]) * nf[2]
        for at in range(up_ref.shape[0]):
            up_ref[at] = (lines_kept[0, at] - mean).astype(BF16)
            dn_ref[at] = (lines_kept[1, at] - mean).astype(BF16)


def mix_kernel(
    dims, layer, per, scal, nf, red_ref, up_ref, dn_ref, got_ref, cnt_ref, par_ref, w_ref,
    mix_ref, spa_ref, st_ref, vec_ref, hs, ms, tv, wd, ds, acc,
):
    step, last = pl.program_id(0), pl.num_programs(0) - 1
    width = w_ref.shape[0]

    @pl.when(step == 0)
    def _():
        at = 2 * layer
        narrow_norm(
            nf, got_ref, cnt_ref, par_ref[54 + at : 55 + at, :], par_ref[58 + at : 59 + at, :],
            vec_ref,
        )
        for k in range(2):
            mean = got_ref[scal[scal.shape[0] - 3 + k], :, 0:width]
            vec_ref[5 + k : 6 + k, :] = vec_ref[3:4, :] + vec_ref[2:3, :] * mean
        depth_weights(par_ref, layer, wd, False)

    def body(clip, k, view):
        mix_clip(
            dims, layer, scal, nf, view(red_ref), up_ref.at[k], dn_ref.at[k], par_ref, w_ref,
            view(mix_ref, 2), view(spa_ref), st_ref,
            vec_ref, hs, ms, tv, wd, ds, acc, clip, per * (last + 1),
        )

    clip_loop(dims, per, body)

    @pl.when(step == last)
    def _():
        finish_stats(nf, acc, st_ref)


def mix_clip(
    dims, layer, scal, nf, red_ref, up_ref, dn_ref, par_ref, w_ref, mix_ref, spa_ref, st_ref, vec_ref, hs, ms, tv, wd, ds, acc, clip, clips,
):
    frames, rows, line = dims
    width = w_ref.shape[0]
    mask = live_rows(scal[clip], frames, STEP, width)
    near = mask * scal[clips].astype(F32)
    far = mask * scal[clips + 1].astype(F32)
    near_at, far_at = edge_places(scal, clips, line, rows)

    def edge(i):
        h, _ = silu_half(up_ref[pl.ds(i, STEP), :].astype(F32) * vec_ref[2:3, :] + vec_ref[5:6, :])
        hs[pl.ds(near_at + i, STEP), :] = (h * near).astype(BF16)
        h, _ = silu_half(dn_ref[pl.ds(i, STEP), :].astype(F32) * vec_ref[2:3, :] + vec_ref[6:7, :])
        hs[pl.ds(far_at + i, STEP), :] = (h * far).astype(BF16)

    each(line, edge, 7)

    def own(i):
        value = red_ref[pl.ds(i, STEP), :]
        h, _ = silu_half(value * vec_ref[2:3, :] + vec_ref[3:4, :])
        hs[pl.ds(i + line, STEP), :] = (h * mask).astype(BF16)

    each(line * rows, own, 49)
    ms[...] = dot_nn(hs[...], w_ref[...])

    def shifts(r, carry):
        at = pl.multiple_of(r * line, STEP)
        for half in range(width // LANE):
            lanes = slice(LANE * half, LANE * (half + 1))
            part = pl.ds(at, line)
            value = ms[part, lanes].astype(BF16).astype(F32)
            ms[part, lanes] = value
            frame_shifts(dims, value, tv.at[:, :, lanes], at)
        return carry

    lax.fori_loop(0, rows + 2, shifts, 0, unroll=True)
    mix_ref[...] = tv[1]

    def store(r, lanes, value):
        spa_ref[line * r : line * (r + 1), lanes] = value

    depth_sum(dims, layer, False, par_ref, ms, tv, wd, ds, spa_ref, store)
    read = lambda at, i: spa_ref[pl.ds(pl.multiple_of(line * at, STEP) + i, STEP), :]
    line_stats(nf, scal, dims, read, rows, clip * rows, clip == 0, acc, st_ref)

def hidden_rows(i, mask, spa_ref, h_ref, vec_ref, acc):
    part = pl.ds(i, STEP)
    h, _ = silu_half(spa_ref[part, :] * vec_ref[2:3, :] + vec_ref[3:4, :])
    low = (h * mask).astype(BF16)
    h_ref[part, :] = low
    acc[...] += fold(low.astype(F32))


def slopes_kernel(dims, per, scal, src_ref, vec_ref, z_ref, u_ref, *h_refs):
    frames, rows, line = dims
    width = src_ref.shape[1]

    def body(clip, k, view):
        mask = live_rows(scal[clip], frames, STEP, width)
        src, z_out, u_out = view(src_ref), view(z_ref), view(u_ref)
        h_out = view(h_refs[0]) if h_refs else None

        def own(i):
            part = pl.ds(i, STEP)
            value = src[part, :]
            h, both = silu_half(value * vec_ref[2:3, :] + vec_ref[3:4, :])
            if h_refs:
                h_out[part, :] = (h * mask).astype(BF16)
            u_out[part, :] = (slope_of(h, both) * mask).astype(BF16)
            z_out[part, :] = (value * vec_ref[0:1, :] + vec_ref[1:2, :]).astype(BF16)

        each(line * rows, own, 49)

    clip_loop(dims, per, body)


def hidden_kernel(
    dims, layer, per, scal, nf, spa_ref, got_ref, cnt_ref, par_ref, w_ref,
    h_ref, st_ref, gram_ref, vec_ref, acc,
):
    frames, rows, line = dims
    step = pl.program_id(0)
    width = par_ref.shape[1]

    @pl.when(step == 0)
    def _():
        at = 2 * layer
        narrow_norm(
            nf, got_ref, cnt_ref, par_ref[55 + at : 56 + at, :], par_ref[59 + at : 60 + at, :],
            vec_ref,
        )
        gram_ref[...] = jnp.zeros_like(gram_ref)
        acc[...] = jnp.zeros_like(acc)

    def body(clip, k, view):
        mask = live_rows(scal[clip], frames, STEP, width)
        spa, h_out = view(spa_ref), view(h_ref)

        def own(i):
            hidden_rows(i, mask, spa, h_out, vec_ref, acc)

        each(line * rows, own, 49)

    clip_loop(dims, per, body)
    gram_ref[0:width, :] += dot_tn(h_ref[...], h_ref[...])

    @pl.when(step == pl.num_programs(0) - 1)
    def _():
        total = row_sum(acc[...])
        gram_ref[width : width + 8, :] = jnp.broadcast_to(total, (8, width))
        across = jnp.broadcast_to(total, (width, width))
        centered = gram_ref[0:width, :] - across.T * across * nf[2]
        spread = row_sum(dot_split(centered, w_ref[...]) * w_ref[...].astype(F32))
        peers = st_ref.shape[0]
        st_ref[:, :, 0:width] = jnp.broadcast_to(total, (peers, 1, width))
        st_ref[:, :, width:] = jnp.broadcast_to(spread, (peers, 1, spread.shape[1]))


def wide_norm(nf, got_ref, cnt_ref, rinv_ref, pout_ref, layer, w_ref, vec_ref):
    width = w_ref.shape[0]
    hidden_means = got_ref[:, 0, 0:width] * rinv_ref[:, 0:1]
    means = dot_split(hidden_means, w_ref[...])
    counts = cnt_ref[:, 0, 0:1]
    mean = row_sum(means * counts) / nf[1]
    away = means - mean
    spread = row_sum(got_ref[:, 0, width:] + counts * away * away) / nf[1]
    inverse = lax.rsqrt(jnp.maximum(spread, 0.0) + epsilon)
    scale = pout_ref[layer : layer + 1, :] * inverse
    vec_ref[...] = jnp.zeros_like(vec_ref)
    vec_ref[0:1, :] = scale
    vec_ref[1:2, :] = 0.5 * (pout_ref[2 + layer : 3 + layer, :] - mean * scale)
    vec_ref[2:3, :] = inverse
    vec_ref[3:4, :] = mean
    vec_ref[4:5, :] = 0.5 * scale


def each_line(dims, lines, step, scal, width, body, make=live_cap):
    frames, rows, line = dims

    def run(carry):
        for at in range(lines):
            mask = make(scal[(step * lines + at) // rows], frames, STEP, width)
            for i in range(at * line, (at + 1) * line, STEP):
                carry = body(slice(i, i + STEP), mask, carry)
        return carry

    return run


def join_kernel(
    dims, lines, scal, nf, x_ref, h_ref, got_ref, cnt_ref, rinv_ref, pout_ref, w3_ref, w1_ref,
    next_ref, du_ref, red_ref, up_ref, dn_ref, st_ref, vec_ref, es, acc, lines_kept,
):
    step = pl.program_id(0)
    wide, width = w1_ref.shape
    frames = dims[0]
    block = 256

    @pl.when(step == 0)
    def _():
        wide_norm(nf, got_ref, cnt_ref, rinv_ref, pout_ref, 0, w3_ref, vec_ref)

    for j in range(wide // block):
        lanes = slice(block * j, block * (j + 1))
        es[j % 2] = dot_nn(h_ref[...], w3_ref[:, lanes])
        scale, shift = vec_ref[4:5, lanes], vec_ref[1:2, lanes]

        def own(part, cap, carry):
            spot = slice(part.start // frames, part.stop // frames)
            x = x_ref[spot, :, lanes].reshape(-1, block).astype(F32)
            half = x * 0.5 + (es[j % 2, part, :] * scale + shift)
            o, both = silu_half(jnp.minimum(half, cap))
            next_ref[part, lanes] = (0.5 * o).astype(BF16)
            du_ref[part, lanes] = slope_twice(o, both).astype(BF16)
            return carry

        each_line(dims, lines, step, scal, block, own)(0)
    red_ref[...] = 2.0 * dot_nn(next_ref[...], w1_ref[...])
    reduced_tail(dims, lines, step, scal, nf, red_ref, up_ref, dn_ref, st_ref, acc, lines_kept)


def wide_tail(hT, gs_ref, w3s, low_ref, t_ref):
    t_ref[...] += dot_nn(hT, gs_ref[...])
    low_ref[...] = dot_nt(gs_ref[...], w3s[...]).astype(BF16)


def wide_sums(w3_ref, t_ref, sacc, vec_ref, sum_ref, unit):
    wide = w3_ref.shape[1]
    t_ref[...] = unit * t_ref[...]
    plain = unit * row_sum(sacc[...])
    along = row_sum(w3_ref[...].astype(F32) * t_ref[...])
    along = (along - vec_ref[3:4, :] * plain) * vec_ref[2:3, :]
    pieces = [
        one[:, LANE * k : LANE * (k + 1)] for one in (plain, along) for k in range(wide // LANE)
    ]
    sum_ref[...] = jnp.broadcast_to(jnp.concatenate(pieces, axis=0)[None], sum_ref.shape).astype(
        BF16
    )


def out_kernel(
    dims, lines, scal, nf, x_ref, h_ref, cot_ref, got_ref, cnt_ref, rinv_ref, pout_ref, w3_ref,
    out_ref, gs_ref, low_ref, t_ref, sum_ref, vec_ref, es, w3s, sacc,
):
    step = pl.program_id(0)
    width, wide = w3_ref.shape
    frames = dims[0]
    block = 256
    unit = 0.5

    @pl.when(step == 0)
    def _():
        wide_norm(nf, got_ref, cnt_ref, rinv_ref, pout_ref, 1, w3_ref, vec_ref)
        t_ref[...] = jnp.zeros_like(t_ref)
        sacc[...] = jnp.zeros_like(sacc)
        w3s[...] = (w3_ref[...].astype(F32) * (unit * vec_ref[0:1, :])).astype(BF16)

    hT = h_ref[...].T
    for j in range(wide // block):
        lanes = slice(block * j, block * (j + 1))
        es[j % 2] = dot_nn(h_ref[...], w3_ref[:, lanes])
        scale, shift = vec_ref[4:5, lanes], vec_ref[1:2, lanes]

        def own(part, cap, total):
            half = x_ref[part, lanes].astype(F32) + (es[j % 2, part, :] * scale + shift)
            o, both = silu_half(jnp.minimum(half, cap))
            spot = slice(part.start // frames, part.stop // frames)
            out_ref[spot, :, lanes] = o.astype(BF16).reshape(-1, frames, block)
            grad = cot_ref[spot, :, lanes].reshape(-1, block).astype(F32)
            grad = grad * slope_twice(o, both)
            gs_ref[part, lanes] = grad.astype(BF16)
            return total + fold(grad)

        total = each_line(dims, lines, step, scal, block, own)(jnp.zeros((8, block), F32))
        sacc[:, lanes] += total
    wide_tail(hT, gs_ref, w3s, low_ref, t_ref)

    @pl.when(step == pl.num_programs(0) - 1)
    def _():
        wide_sums(w3_ref, t_ref, sacc, vec_ref, sum_ref, unit)


def expand_back_kernel(
    dims, per, scal, nf, low_ref, h_ref, z_ref, u_ref, got_ref, vec_ref, w3_ref,
    go_ref, up_ref, dn_ref, sum_ref, tot_ref, ks, crow, hk, acc,
):
    frames, rows, line = dims
    step = pl.program_id(0)
    width, wide = w3_ref.shape

    @pl.when(step == 0)
    def _():
        totals = jnp.sum(got_ref[...].astype(F32), axis=0)
        count = wide // LANE
        plain = jnp.concatenate([totals[k : k + 1, :] for k in range(count)], axis=1)
        along = jnp.concatenate([totals[k : k + 1, :] for k in range(count, 2 * count)], axis=1)
        tot_ref[:, 0:wide] = plain
        tot_ref[:, wide:] = along
        w3 = w3_ref[...]
        rise, flat = wide_rows_of(nf, plain, along, vec_ref)
        ks[...] = dot_nt((w3.astype(F32) * rise).astype(BF16), w3).astype(BF16)
        spread = [jnp.broadcast_to(one, (16, wide)) for one in split(flat)]
        crow[...] = (dot_nt(spread[0], w3) + dot_nt(spread[1], w3))[0:8]
        acc[...] = jnp.zeros_like(acc)

    hk[...] = dot_nn(h_ref[...], ks[...])

    def own(i):
        part = pl.ds(i, STEP)
        grad = low_ref[part, :].astype(F32) - crow[0:1, :] - hk[part, :]
        grad = grad * u_ref[part, :].astype(F32)
        go_ref[part, :] = grad.astype(BF16)
        acc[0:8, :] += fold(grad)
        acc[8:16, :] += fold(grad * z_ref[part, :].astype(F32))

    each(line * rows * per, own, 49)
    for k in range(per):
        expand_edges(dims, scal, k * rows * line, go_ref, z_ref, up_ref.at[k], dn_ref.at[k])

    @pl.when(step == pl.num_programs(0) - 1)
    def _():
        share_sums(acc, sum_ref)


def wide_rows_of(nf, plain, along, vec_ref):
    scale, inverse, mean = vec_ref[0:1, :], vec_ref[2:3, :], vec_ref[3:4, :]
    rise = scale * inverse * along * nf[3]
    return rise, scale * plain * nf[3] - rise * mean


def expand_grad_kernel(
    scal, nf, tot_ref, vec_ref, t_ref, gram_ref, w3_ref, mine_ref, sent_ref
):
    width, wide = w3_ref.shape
    rise, flat = wide_rows_of(nf, tot_ref[:, 0:wide], tot_ref[:, wide:], vec_ref)
    column = jnp.broadcast_to(gram_ref[width : width + 1, :], (LANE, width)).T[:, 0:1]
    cross = dot_split(gram_ref[0:width, :], w3_ref[...])
    ge = t_ref[...] * vec_ref[0:1, :] - column * flat - cross * rise
    chips, size = mine_ref.shape[0:2]
    parts = [ge[:, width * k : width * (k + 1)] for k in range(wide // width)]
    parts = [one.reshape(chips, -1, size * width // wide, width) for one in parts]
    hand_over(scal, jnp.concatenate(parts, axis=2), mine_ref, sent_ref)


def expand_edges(dims, scal, base, go_ref, z_ref, up_ref, dn_ref):
    frames, rows, line = dims
    even = scal[scal.shape[0] - 1] == 0
    last = line * (rows - 1)
    first = jnp.where(even, last, 0)
    near = pl.multiple_of(base + first, STEP)
    far = pl.multiple_of(base + last - first, STEP)
    up_ref[0] = go_ref[pl.ds(near, line), :]
    up_ref[1] = z_ref[pl.ds(near, line), :]
    dn_ref[0] = go_ref[pl.ds(far, line), :]
    dn_ref[1] = z_ref[pl.ds(far, line), :]


def norm_rows(nf, got_ref, vec_ref, tot_ref, rows3):
    totals = jnp.sum(got_ref[...], axis=0)
    tot_ref[...] = totals
    norm_terms(nf, totals, vec_ref, rows3)


def norm_terms(nf, totals, vec_ref, rows3):
    width = vec_ref.shape[1]
    rows3[0:1, :] = vec_ref[4:5, :]
    rows3[1:2, :] = vec_ref[4:5, :] * totals[:, 0:width] * nf[3]
    rows3[2:3, :] = vec_ref[4:5, :] * totals[:, width:] * nf[3]


def norm_back(rows3, go, z, mask):
    value = rows3[0:1, :] * go.astype(F32) - rows3[1:2, :] - rows3[2:3, :] * z.astype(F32)
    return value * mask


def depth_back_kernel(
    dims, layer, per, scal, nf, go_ref, above_ref, below_ref, z_ref, got_ref, vec_ref,
    z1_ref, u1_ref, par_ref, w_ref,
    go1_ref, sum_ref, gm_ref, gp_ref, tot_ref, ms, tv, wd, ds, gh, rows3, acc,
):
    step, last = pl.program_id(0), pl.num_programs(0) - 1
    width = w_ref.shape[0]

    @pl.when(step == 0)
    def _():
        norm_rows(nf, got_ref, vec_ref, tot_ref, rows3)
        depth_weights(par_ref, layer, wd, True)
        acc[...] = jnp.zeros_like(acc)

    def body(clip, k, view):
        depth_back_clip(
            dims, layer, scal, view(go_ref), above_ref.at[k], below_ref.at[k], view(z_ref),
            view(z1_ref), view(u1_ref), par_ref, w_ref, view(go1_ref), view(gm_ref), view(gp_ref),
            ms, tv, wd, ds, gh, rows3, acc, clip, per * (last + 1),
        )

    clip_loop(dims, per, body)

    @pl.when(step == last)
    def _():
        share_sums(acc, sum_ref)


def depth_back_clip(
    dims, layer, scal, go_ref, above_ref, below_ref, z_ref, z1_ref, u1_ref, par_ref, w_ref,
    go1_ref, gm_ref, gp_ref, ms, tv, wd, ds, gh, rows3, acc, clip, clips,
):
    frames, rows, line = dims
    width = w_ref.shape[0]
    mask = live_rows(scal[clip], frames, STEP, width)
    near = mask * scal[clips].astype(F32)
    far = mask * scal[clips + 1].astype(F32)
    near_at, far_at = edge_places(scal, clips, line, rows)

    def edge(i):
        part = pl.ds(i, STEP)
        ms[pl.ds(near_at + i, STEP), :] = norm_back(
            rows3, above_ref[0, part, :], above_ref[1, part, :], near
        )
        ms[pl.ds(far_at + i, STEP), :] = norm_back(
            rows3, below_ref[0, part, :], below_ref[1, part, :], far
        )

    each(line, edge, 7)

    def own(i):
        part = pl.ds(i, STEP)
        ms[pl.ds(i + line, STEP), :] = norm_back(rows3, go_ref[part, :], z_ref[part, :], mask)

    each(line * rows, own, 49)

    def shifts(r, carry):
        at = pl.multiple_of(r * line, STEP)
        for half in range(width // LANE):
            lanes = slice(LANE * half, LANE * (half + 1))
            part = pl.ds(at, line)
            value = ms[part, lanes].astype(BF16).astype(F32)
            ms[part, lanes] = value
            frame_shifts(dims, value, tv.at[:, :, lanes], at)
        return carry

    lax.fori_loop(0, rows + 2, shifts, 0, unroll=True)
    gp_ref[...] = tv[1, line : line * (rows + 1), :]

    def store(r, lanes, value):
        gm_ref[line * r : line * (r + 1), lanes] = value.astype(BF16)

    depth_sum(dims, layer, True, par_ref, ms, tv, wd, ds, gh, store)
    gh[...] = dot_nt(gm_ref[...], w_ref[...])

    def first(i):
        part = pl.ds(i, STEP)
        value = gh[part, :] * u1_ref[part, :].astype(F32)
        go1_ref[part, :] = value.astype(BF16)
        acc[0:8, :] += fold(value)
        acc[8:16, :] += fold(value * z1_ref[part, :].astype(F32))

    each(line * rows, first, 49)

def kernel_grads(
    dims, per, scal, mix_ref, gp_ref, gm_ref, h_ref,
    mine_ref, sent_ref, gmix_ref, gdep_ref, tv, mv, gacc, vacc,
):
    step = pl.program_id(0)
    width = h_ref.shape[1]
    halves = width // LANE

    @pl.when(step == 0)
    def _():
        gmix_ref[...] = jnp.zeros_like(gmix_ref)
        gacc[...] = jnp.zeros_like(gacc)
        vacc[...] = jnp.zeros_like(vacc)

    gmix_ref[...] += dot_tn(h_ref[...], gm_ref[...])

    def body(clip, k, view):
        kernel_clip(dims, halves, view(mix_ref, 2), view(gp_ref), tv, mv, gacc, vacc)

    clip_loop(dims, per, body)

    @pl.when(step == pl.num_programs(0) - 1)
    def _():
        one = lax.broadcasted_iota(jnp.int32, (LANE, LANE), 0)
        two = lax.broadcasted_iota(jnp.int32, (LANE, LANE), 1)
        gdep_ref[...] = jnp.zeros_like(gdep_ref)
        for half in range(halves):
            lanes = slice(LANE * half, LANE * (half + 1))
            for i in range(9):
                gdep_ref[3 * i + 1 : 3 * i + 2, lanes] = row_sum(vacc[i, :, lanes])
                for e in (0, 2):
                    k = LANE * (e // 2)
                    part = gacc[half, k : k + LANE, LANE * i : LANE * (i + 1)]
                    gdep_ref[3 * i + e : 3 * i + e + 1, lanes] = row_sum(
                        jnp.where(one == two, part, 0.0)
                    )
        chips, size = mine_ref.shape[0:2]
        taps = jnp.concatenate([gdep_ref[...].T, jnp.zeros((width, width - LANE), F32)], axis=1)
        parts = [gmix_ref[...], taps]
        parts = [one.reshape(chips, -1, size // 2, width) for one in parts]
        hand_over(scal, jnp.concatenate(parts, axis=2), mine_ref, sent_ref)


def kernel_clip(dims, halves, mix_ref, gp_ref, tv, mv, gacc, vacc):
    frames, rows, line = dims

    def shifts(r, carry):
        at = pl.multiple_of(r * line, STEP)
        for half in range(halves):
            lanes = slice(LANE * half, LANE * (half + 1))
            value = mix_ref[pl.ds(at, line), lanes].astype(F32)
            frame_shifts(dims, value, tv.at[:, :, lanes], at)
        return carry

    lax.fori_loop(0, rows + 2, shifts, 0, unroll=True)

    def moves(r, carry):
        at = pl.multiple_of(r * line, STEP)
        for half in range(halves):
            lanes = slice(LANE * half, LANE * (half + 1))
            value = gp_ref[pl.ds(at, line), lanes].astype(F32)
            onward, back = column_moves(dims, value)
            mv[half, pl.ds(at, line), 0:LANE] = back.astype(BF16)
            mv[half, pl.ds(at, line), LANE : 2 * LANE] = onward.astype(BF16)
        return carry

    lax.fori_loop(0, rows, moves, 0, unroll=True)
    for half in range(halves):
        lanes = slice(LANE * half, LANE * (half + 1))
        views = [tv[a, line * b : line * (b + rows), lanes] for a in range(3) for b in range(3)]
        gacc[half] += dot_tn(mv[half], jnp.concatenate(views, axis=1))
        sums = [vacc[i, :, lanes] for i in range(9)]
        for start in range(0, rows * line, line):
            own = gp_ref[start : start + line, lanes].astype(F32)
            onward, back = frame_moves(frames, own)
            for b in range(3):
                seen = mix_ref[start + line * b : start + line * b + line, lanes].astype(F32)
                for a, moved in enumerate((back, own, onward)):
                    sums[3 * a + b] = sums[3 * a + b] + fold(moved * seen)
        for i in range(9):
            vacc[i, :, lanes] = sums[i]


def reduced_grad(dims, lines, step, scal, go_ref, z_ref, rows3, gr_ref):
    def own(part, mask, carry):
        gr_ref[part, :] = norm_back(rows3, go_ref[part, :], z_ref[part, :], mask).astype(BF16)
        return carry

    each_line(dims, lines, step, scal, rows3.shape[1], own, live_rows)(0)


def cross_kernel(
    dims, lines, scal, nf, go_ref, z_ref, got_ref, vec1_ref, gs_ref, du_ref, h_ref,
    vec3_ref, w1_ref, w3_ref,
    gs0_ref, low_ref, t_ref, sum_ref, tot_ref, gr_ref, ds, w1s, w3s, rows3, sacc,
):
    step = pl.program_id(0)
    width, wide = w3_ref.shape
    block = 256
    unit = 0.25

    @pl.when(step == 0)
    def _():
        norm_rows(nf, got_ref, vec1_ref, tot_ref, rows3)
        t_ref[...] = jnp.zeros_like(t_ref)
        sacc[...] = jnp.zeros_like(sacc)
        w3s[...] = (w3_ref[...].astype(F32) * (unit * vec3_ref[0:1, :])).astype(BF16)
        w1s[...] = (w1_ref[...].astype(F32) * 2.0).astype(BF16)

    reduced_grad(dims, lines, step, scal, go_ref, z_ref, rows3, gr_ref)
    hT = h_ref[...].T
    for j in range(wide // block):
        lanes = slice(block * j, block * (j + 1))
        ds[j % 2] = dot_nt(gr_ref[...], w1s[lanes, :])

        def own(part, mask, total):
            value = gs_ref[part, lanes].astype(F32) + ds[j % 2, part, :]
            value = value * du_ref[part, lanes].astype(F32)
            gs0_ref[part, lanes] = value.astype(BF16)
            return total + fold(value)

        total = each_line(dims, lines, step, scal, block, own)(jnp.zeros((8, block), F32))
        sacc[:, lanes] += total
    wide_tail(hT, gs0_ref, w3s, low_ref, t_ref)

    @pl.when(step == pl.num_programs(0) - 1)
    def _():
        wide_sums(w3_ref, t_ref, sacc, vec3_ref, sum_ref, unit)


def reduce_grad_kernel(
    dims, lines, unit, scal, nf, go_ref, z_ref, tot_ref, vec1_ref, x_ref,
    mine_ref, sent_ref, gr, rows3, gacc,
):
    step = pl.program_id(0)

    @pl.when(step == 0)
    def _():
        norm_terms(nf, tot_ref[...], vec1_ref, rows3)
        gacc[...] = jnp.zeros_like(gacc)

    reduced_grad(dims, lines, step, scal, go_ref, z_ref, rows3, gr)
    gacc[...] += dot_tn(gr[...], x_ref[...])

    @pl.when(step == pl.num_programs(0) - 1)
    def _():
        chips, size, width = mine_ref.shape
        value = (unit * gacc[...].T).reshape(chips, -1, size, width)
        hand_over(scal, value, mine_ref, sent_ref)


def last_grad_kernel(
    dims, lines, scal, nf, go_ref, z_ref, got_ref, vec1_ref, x_ref,
    gr_ref, mine_ref, sent_ref, tot_ref, rows3, gacc,
):
    step = pl.program_id(0)

    @pl.when(step == 0)
    def _():
        norm_rows(nf, got_ref, vec1_ref, tot_ref, rows3)
        gacc[...] = jnp.zeros_like(gacc)

    reduced_grad(dims, lines, step, scal, go_ref, z_ref, rows3, gr_ref)
    gacc[...] += dot_tn(gr_ref[...], x_ref[...].reshape(-1, x_ref.shape[2]))

    @pl.when(step == pl.num_programs(0) - 1)
    def _():
        chips, size, width = mine_ref.shape
        hand_over(scal, gacc[...].T.reshape(chips, -1, size, width), mine_ref, sent_ref)


def input_kernel(gr_ref, gs_ref, w1_ref, out_ref):
    w1 = w1_ref[...].reshape(-1, w1_ref.shape[2])
    value = dot_nt(gr_ref[...], w1) + 0.25 * gs_ref[...].astype(F32)
    out_ref[...] = value.astype(BF16).reshape(out_ref.shape)


ALL = ("clip", "outer", "inner")
CHIPS = ("clip", "outer")
SP = ("outer", "inner")


def share(rows):
    return lax.all_to_all(rows, ALL, 0, 0)


def gather(value):
    return share(jnp.broadcast_to(value[None], (lax.axis_size(ALL),) + value.shape))


def neighbours(near, far):
    peers = lax.axis_size(SP)
    first = [(i, i + 1) for i in range(0, peers - 1, 2)]
    second = [(i, i + 1) for i in range(1, peers - 1, 2)]
    near = lax.ppermute(near, SP, first + [(j, i) for i, j in first])
    far = lax.ppermute(far, SP, second + [(j, i) for i, j in second])
    return near, far


def swap(value):
    peers = lax.axis_size("inner")
    return lax.ppermute(value, "inner", [(i, (i + 1) % peers) for i in range(peers)])


def after(value, other):
    return lax.optimization_barrier((value, other))[0]


def on_device(
    features, strides, cotangent, w_reduce, w_mix, w_expand, w_depth,
    gains_mid, biases_mid, gains_out, biases_out,
):
    clips, frames, rows, columns, wide = features.shape
    width = w_mix.shape[2]
    peers, chips = lax.axis_size(ALL), lax.axis_size(CHIPS)
    inner = lax.axis_size("inner")
    sp_size = lax.axis_size(SP)
    part, place = lax.axis_index("inner"), lax.axis_index(ALL)
    sp_at = lax.axis_index(SP)
    line = columns * frames
    per_clip = rows * line
    voxels = clips * per_clip
    r1, r2 = w_reduce.shape[1], w_mix.shape[1]
    r4 = w_depth.shape[2]
    r5 = gains_out.shape[1] // r4
    blocks = wide // width

    def from_cores(near):
        held = [near]
        for _ in range(inner - 1):
            held.append(swap(held[-1]))
        turns = [lax.rem(part - c + inner, inner) for c in range(inner)]
        whole = jnp.stack([lax.select_n(turn, *held) for turn in turns], axis=1)
        return whole.reshape((peers,) + near.shape[1:])

    def wide_weight(rows_of_all):
        one = rows_of_all.reshape(peers, blocks, r2, width).transpose(0, 2, 1, 3)
        return one.reshape(peers * r2, wide)

    height = r1 + r2 + 8
    height += -height % 16
    whole = lambda value: full(value.shape)
    raw = (w_reduce, w_mix, w_depth.transpose(0, 2, 1), gains_mid, biases_mid, gains_out,
           biases_out)
    packed = call(
        pack_kernel, 1, [whole(one) for one in raw], full((chips, height, width)),
        jax.ShapeDtypeStruct((chips, height, width), BF16), [], 1,
    )(*raw)
    near = lax.all_to_all(packed, CHIPS, 0, 0)
    x = features.transpose(0, 2, 3, 1, 4).reshape(voxels // frames, frames, wide)
    counts = frames // strides
    by_group = jnp.sum(counts.reshape(-1, clips), axis=1) * (rows * columns)
    by_device = jnp.repeat(by_group, sp_size).astype(F32)
    local = lax.dynamic_slice_in_dim(counts, lax.axis_index("clip") * clips, clips)
    odd = lax.rem(sp_at, 2)
    has_near = (odd == 1) | (sp_at < sp_size - 1)
    has_far = jnp.where(odd == 1, sp_at < sp_size - 1, sp_at > 0)
    way = jnp.where(odd == 1, -1, 1)
    base = lax.axis_index("clip") * sp_size
    near_place = base + jnp.clip(sp_at + way, 0, sp_size - 1)
    far_place = base + jnp.clip(sp_at - way, 0, sp_size - 1)
    edges = jnp.stack(
        [has_near.astype(jnp.int32), has_far.astype(jnp.int32), near_place, far_place, odd]
    )
    scal = jnp.concatenate([local.astype(jnp.int32), edges])
    own = jnp.sum(local).astype(F32) * (rows * columns)
    total = jnp.sum(by_device)
    nf = jnp.stack([own, total, 1.0 / own, 1.0 / total])

    sizes = [r2 * blocks + r1, r2 * blocks + r2]
    sizes = [(chips, one + -one % 16, width) for one in sizes]
    raw = (w_reduce, w_mix, w_expand)
    spaces = [full(one) for one in sizes] + [full((peers, 1, LANE)), full((peers, LANE))]
    late_one, late_two, cnt, rinv = call(
        late_pack_kernel, 1, [smem()] + [whole(one) for one in raw], spaces,
        [jax.ShapeDtypeStruct(one, BF16) for one in sizes]
        + [jax.ShapeDtypeStruct(one, F32) for one in ((peers, 1, LANE), (peers, LANE))], [], 1,
    )(by_device, *raw)
    near, late_one, late_two, scal, nf, cnt, rinv = lax.optimization_barrier(
        (near, late_one, late_two, scal, nf, cnt, rinv)
    )
    early = from_cores(near)
    w2 = [early[:, r1 : r1 + r2].reshape(-1, width)]
    at = r1 + r2
    taps = early[:, at : at + r4, 0:64].reshape(-1, 64).T
    taps = [taps[32 * k : 32 * k + 27] for k in range(2)]
    mids = early[:, at : at + 8, 64 : 64 + r4].transpose(1, 0, 2).reshape(8, width)
    par = jnp.concatenate([*taps, mids, jnp.zeros((2, width), BF16)], axis=0).astype(F32)
    pout = early[:, at : at + 4, 96 : 96 + r4 * r5].transpose(1, 0, 2).reshape(4, wide)
    pout = pout.astype(F32)

    struct = jax.ShapeDtypeStruct
    dims = (frames, rows, line)
    lines = rows
    steps = clips * rows // lines
    many_lines = 2 * rows if clips % 2 == 0 else rows
    few = clips * rows // many_lines
    tall = (rows + 2) * line
    by_step = lambda size: pl.BlockSpec((lines * line, size), lambda s: (s, 0))
    thin, broad = by_step(width), by_step(wide)

    def by_clip(name):
        per = PER[name] if clips % PER[name] == 0 else 1
        field = pl.BlockSpec((per * per_clip, width), lambda c: (c, 0))
        tall_field = pl.BlockSpec((per * tall, width), lambda c: (c, 0))
        edge_one = pl.BlockSpec((per, line, width), lambda c: (c, 0, 0))
        edge_two = pl.BlockSpec((per, 2, line, width), lambda c: (c, 0, 0, 0))
        return per, field, tall_field, edge_one, edge_two

    native = pl.BlockSpec((lines * line // frames, frames, wide), lambda s: (s, 0, 0))
    size = many_lines * line
    big_thin = pl.BlockSpec((size, width), lambda s: (s, 0))
    big_broad = pl.BlockSpec((size, wide), lambda s: (s, 0))
    big_native = pl.BlockSpec((size // frames, frames, wide), lambda s: (s, 0, 0))
    native_shape = struct((voxels // frames, frames, wide), BF16)
    narrow = lambda kind: struct((voxels, width), kind)
    wide_shape = struct((voxels, wide), BF16)
    edge = struct((clips, line, width), BF16)
    lines_kept = pltpu.VMEM((2, clips, line, width), F32)
    pair = struct((clips, 2, line, width), BF16)
    flat = lambda *shape: struct(shape, F32)
    two = (peers, 1, 2 * width)
    three = (peers, 1, width + wide)
    many = (peers, 2 * wide // LANE, LANE)
    vec, vec_wide = (8, width), (8, wide)
    owned = struct((chips, r1, width), BF16)
    owned_taps = struct((chips, 2 * r2, width), BF16)

    reduced, up, dn, stats = call(
        functools.partial(first_kernel, dims, many_lines), few,
        [smem(), smem(), big_native, full((peers, r1, width))],
        [big_thin, full(edge.shape), full(edge.shape), full(two)],
        [narrow(F32), edge, edge, flat(*two)],
        [pltpu.VMEM((24, width), F32), lines_kept], 6,
    )(scal, nf, x, early)

    depth_scratch = [
        pltpu.VMEM((tall, width), F32), pltpu.VMEM((3, tall, width), BF16),
        pltpu.VMEM((width // LANE, 9 * LANE, 2 * LANE), BF16),
        pltpu.VMEM((width // LANE, per_clip, 2 * LANE), F32),
    ]
    above, below = neighbours(up, dn)
    got = share(stats)
    got, cnt, par, w2[0] = lax.optimization_barrier((got, cnt, par, w2[0]))
    late_one = after(late_one, (got, above, below))
    near = lax.all_to_all(late_one, CHIPS, 0, 0)
    w1, w3 = [early], []
    stored = []
    for layer in range(2):
        if layer == 1:
            above, below = neighbours(up, dn)
            stats, near = lax.optimization_barrier((stats, near))
            got = share(stats)
            late = from_cores(near)
            w2.append(late[:, r2 * blocks : r2 * blocks + r2].reshape(-1, width))
        per, field, tall_field, edge_one, edge_two = by_clip("mix")
        mixed, spatial, stats, vec1 = call(
            functools.partial(mix_kernel, dims, layer, per), clips // per,
            [smem(), smem(), field, edge_one, edge_one, full(two),
             full((peers, 1, LANE)), full((64, width)), full((width, width))],
            [tall_field, field, full(two), full(vec)],
            [struct((clips * tall, width), BF16), narrow(F32), flat(*two), flat(*vec)],
            [pltpu.VMEM((tall, width), BF16), *depth_scratch, pltpu.VMEM((24, width), F32)], 10,
        )(scal, nf, reduced, above, below, got, cnt, par, w2[layer])
        got = share(stats)
        per, field, tall_field, edge_one, edge_two = by_clip("slopes")
        z1, u1, h1 = call(
            functools.partial(slopes_kernel, dims, per), clips // per,
            [smem(), field, full(vec)], [field] * 3, [narrow(BF16)] * 3, [], 5,
        )(scal, reduced, vec1)
        if layer == 1:
            w3.append(wide_weight(late[:, : r2 * blocks]))
        else:
            late = from_cores(after(near, stats))
            w3.append(wide_weight(late[:, : r2 * blocks]))
            at = r2 * blocks
            w1.append(late[:, at : at + r1].reshape(-1, width))
        got, z1, u1, h1, w3[layer] = lax.optimization_barrier((got, z1, u1, h1, w3[layer]))
        per, field, tall_field, edge_one, edge_two = by_clip("hidden")
        h2, stats, gram, vec2 = call(
            functools.partial(hidden_kernel, dims, layer, per), clips // per,
            [smem(), smem(), field, full(two), full((peers, 1, LANE)),
             full((64, width)), full((width, wide))],
            [field, full(three), full((width + 8, width)), full(vec)],
            [narrow(BF16), flat(*three), flat(width + 8, width), flat(*vec)],
            [pltpu.VMEM((8, width), F32)], 5,
        )(scal, nf, spatial, got, cnt, par, w3[layer])
        got = share(stats)
        per, field, tall_field, edge_one, edge_two = by_clip("slopes")
        z2, u2 = call(
            functools.partial(slopes_kernel, dims, per), clips // per,
            [smem(), field, full(vec)], [field] * 2, [narrow(BF16)] * 2, [], 5,
        )(scal, spatial, vec2)
        got, z2, u2 = lax.optimization_barrier((got, z2, u2))
        if layer == 0:
            got, pout, rinv, w1[1] = lax.optimization_barrier((got, pout, rinv, w1[1]))
            near = lax.all_to_all(after(late_two, got), CHIPS, 0, 0)
        norm_specs = [full(three), full((peers, 1, LANE)), full((peers, LANE)),
                      full((4, wide)), full((width, wide))]
        norm_args = (got, cnt, rinv, pout, w3[layer])
        if layer == 0:
            carried, slope, reduced, up, dn, stats, vec3 = call(
                functools.partial(join_kernel, dims, lines), steps,
                [smem(), smem(), native, thin] + norm_specs + [full((wide, width))],
                [broad, broad, thin, full(edge.shape), full(edge.shape), full(two),
                 full(vec_wide)],
                [wide_shape, wide_shape, narrow(F32), edge, edge, flat(*two), flat(*vec_wide)],
                [pltpu.VMEM((2, lines * line, 256), F32), pltpu.VMEM((24, width), F32),
                 lines_kept], 12,
            )(scal, nf, x, h2, *norm_args, w1[1])
        else:
            cot = cotangent.transpose(0, 2, 3, 1, 4).reshape(voxels // frames, frames, wide)
            output, gs, low, t, sums, vec3 = call(
                functools.partial(out_kernel, dims, lines), steps,
                [smem(), smem(), broad, thin, native] + norm_specs,
                [native, broad, thin, full((width, wide)), full(many), full(vec_wide)],
                [native_shape, wide_shape, narrow(BF16), flat(width, wide), struct(many, BF16),
                 flat(*vec_wide)],
                [pltpu.VMEM((2, lines * line, 256), F32), pltpu.VMEM((width, wide), BF16),
                 pltpu.VMEM((8, wide), F32)], 15,
            )(scal, nf, carried, h2, cot, *norm_args)
        stored.append((z1, u1, h1, vec1, mixed, z2, u2, h2, vec2, gram, vec3))

    def voxel_form(value):
        return value.reshape(clips, rows, columns, frames, wide).transpose(0, 3, 1, 2, 4)

    def sum_cores(*pieces):
        if inner == 1:
            return jnp.concatenate([mine for mine, _ in pieces], axis=1)
        return jnp.concatenate([mine + swap(sent) for mine, sent in pieces], axis=1)

    results = [None, None]
    for layer in (1, 0):
        z1, u1, h1, vec1, mixed, z2, u2, h2, vec2, gram, vec3 = stored[layer]
        if layer == 0:
            sums = after(sums, first)
        got = share(sums)
        if layer == 0:
            got, reduce_mine, reduce_sent = lax.optimization_barrier(
                (got, reduce_mine, reduce_sent)
            )
        per, field, tall_field, edge_one, edge_two = by_clip("expand")
        go2, up, dn, sums, tot3 = call(
            functools.partial(expand_back_kernel, dims, per), clips // per,
            [smem(), smem(), field, field, field, field, full(many), full(vec_wide),
             full((width, wide))],
            [field, edge_two, edge_two, full(two), full((1, 2 * wide))],
            [narrow(BF16), pair, pair, flat(*two), flat(1, 2 * wide)],
            [pltpu.VMEM((width, width), BF16), pltpu.VMEM(vec, F32),
             pltpu.VMEM((per * per_clip, width), F32), pltpu.VMEM((16, width), F32)], 6,
        )(scal, nf, low, h2, z2, u2, got, vec3, w3[layer])
        expand_mine, expand_sent = call(
            expand_grad_kernel, 1,
            [smem(), smem(), full((1, 2 * wide)), full(vec_wide), full((width, wide)),
             full((width + 8, width)), full((width, wide))],
            [full(owned.shape), full(owned.shape)], [owned, owned], [], 3,
        )(scal, nf, tot3, vec3, t, gram, w3[layer])
        above, below = neighbours(up, dn)
        got = share(sums)
        got, expand_mine, expand_sent = lax.optimization_barrier((got, expand_mine, expand_sent))
        expands = (expand_mine, expand_sent)
        if layer == 0:
            second = sum_cores((reduce_mine, reduce_sent), expands)
            second = lax.all_to_all(after(second, (got, above, below)), CHIPS, 0, 0)
        per, field, tall_field, edge_one, edge_two = by_clip("depth")
        go1, sums, gm, gp, tot2 = call(
            functools.partial(depth_back_kernel, dims, layer, per), clips // per,
            [smem(), smem(), field, edge_two, edge_two, field, full(two), full(vec), field,
             field, full((64, width)), full((width, width))],
            [field, full(two), field, field, full((1, 2 * width))],
            [narrow(BF16), flat(*two), narrow(BF16), narrow(BF16), flat(1, 2 * width)],
            [*depth_scratch, pltpu.VMEM((per_clip, width), F32), pltpu.VMEM(vec, F32),
             pltpu.VMEM((16, width), F32)], 12,
        )(scal, nf, go2, above, below, z2, got, vec2, z1, u1, par, w2[layer])
        if layer == 0:
            sums = after(sums, second)
        got = share(sums)
        per, field, tall_field, edge_one, edge_two = by_clip("grads")
        taps_mine, taps_sent = call(
            functools.partial(kernel_grads, dims, per), clips // per,
            [smem(), tall_field, field, field, field],
            [full(owned_taps.shape), full(owned_taps.shape)],
            [owned_taps, owned_taps],
            [pltpu.VMEM((width, width), F32), pltpu.VMEM((LANE, width), F32),
             pltpu.VMEM((3, tall, width), BF16),
             pltpu.VMEM((width // LANE, per_clip, 2 * LANE), BF16),
             pltpu.VMEM((width // LANE, 2 * LANE, 9 * LANE), F32),
             pltpu.VMEM((9, 8, width), F32)], 12,
        )(scal, mixed, gp, gm, h1)
        got, taps_mine, taps_sent = lax.optimization_barrier((got, taps_mine, taps_sent))
        if layer == 1:
            first = lax.all_to_all(sum_cores((taps_mine, taps_sent), expands), CHIPS, 0, 0)
        if layer == 1:
            h2_0, vec3_0 = stored[0][7], stored[0][10]
            gs, low, t, sums, tot1 = call(
                functools.partial(cross_kernel, dims, lines), steps,
                [smem(), smem(), thin, thin, full(two), full(vec), broad, broad, thin,
                 full(vec_wide), full((wide, width)), full((width, wide))],
                [broad, thin, full((width, wide)), full(many), full((1, 2 * width))],
                [wide_shape, narrow(BF16), flat(width, wide), struct(many, BF16),
                 flat(1, 2 * width)],
                [pltpu.VMEM((lines * line, width), BF16), pltpu.VMEM((2, lines * line, 256), F32), pltpu.VMEM((wide, width), BF16),
                 pltpu.VMEM((width, wide), BF16), pltpu.VMEM(vec, F32),
                 pltpu.VMEM((8, wide), F32)], 15,
            )(scal, nf, go1, z1, got, vec1, gs, slope, h2_0, vec3_0, w1[1], w3[0])
            reduce_mine, reduce_sent = call(
                functools.partial(reduce_grad_kernel, dims, many_lines, 2.0), few,
                [smem(), smem(), big_thin, big_thin, full((1, 2 * width)), full(vec), big_broad], [full(owned.shape), full(owned.shape)], [owned, owned],
                [pltpu.VMEM((many_lines * line, width), BF16), pltpu.VMEM(vec, F32),
                 pltpu.VMEM((width, wide), F32)], 5,
            )(scal, nf, go1, z1, tot1, vec1, carried)
        else:
            gr, mine, sent, tot1 = call(
                functools.partial(last_grad_kernel, dims, many_lines), few,
                [smem(), smem(), big_thin, big_thin, full(two), full(vec), big_native],
                [big_thin, full(owned.shape), full(owned.shape), full((1, 2 * width))],
                [narrow(BF16), owned, owned, flat(1, 2 * width)],
                [pltpu.VMEM(vec, F32), pltpu.VMEM((width, wide), F32)], 6,
            )(scal, nf, go1, z1, got, vec1, x)
            input_grad = call(
                input_kernel, few, [big_thin, big_broad, full((peers, r1, width))], big_native,
                native_shape, [], 6,
            )(gr, gs, early)
        results[layer] = (tot1, tot2, tot3)

    last = sum_cores((mine, sent), (taps_mine, taps_sent))
    last = jnp.sum(lax.all_to_all(last, CHIPS, 0, 0).astype(F32), axis=0)
    first = jnp.sum(first.astype(F32), axis=0)
    second = jnp.sum(second.astype(F32), axis=0)
    to_wide = lambda one: one.reshape(blocks, r2, width).transpose(1, 0, 2).reshape(r2, wide)
    grad_reduce = jnp.stack([last[0:r1], second[0:r1]])
    grad_mix = jnp.stack([last[r1 : r1 + r2], first[0:r2]])
    depths = (last[r1 + r2 : r1 + r2 + r4], first[r2 : r2 + r4])
    grad_depth = jnp.stack([one[:, 0:27].T for one in depths])
    grad_expand = jnp.stack([to_wide(second[r1:]), to_wide(first[r2 + r4 :])])

    mid_sums = jnp.concatenate(
        [
            jnp.concatenate([results[layer][0], results[layer][1]], axis=0).reshape(2, 2, width)
            for layer in range(2)
        ],
        axis=0,
    )
    mid = lax.dynamic_slice_in_dim(mid_sums, place * r4, r4, axis=2)
    out_sums = jnp.concatenate([results[layer][2].reshape(1, 2, wide) for layer in range(2)])
    r6 = gains_out.shape[1]
    outs = lax.dynamic_slice_in_dim(out_sums, place * r6, r6, axis=2)

    return (
        voxel_form(output),
        voxel_form(input_grad),
        grad_reduce,
        grad_mix,
        grad_expand,
        grad_depth,
        mid[:, 1].reshape(2, 2, r4),
        mid[:, 0].reshape(2, 2, r4),
        outs[:, 1],
        outs[:, 0],
    )


def solution(mesh):
    clip_size, sp_size = mesh.shape["clip"], mesh.shape["sp"]
    inner = 2 if sp_size % 2 == 0 else 1
    divided = Mesh(mesh.devices.reshape(clip_size, sp_size // inner, inner), ALL)
    activations = P("clip", None, SP, None, None)
    middle, last, vectors = P(None, ALL, None), P(None, None, ALL), P(None, ALL)
    return jax.shard_map(
        on_device,
        mesh=divided,
        in_specs=(
            activations, P(), activations, middle, middle, middle, last, last, last, vectors,
            vectors,
        ),
        out_specs=(
            activations, activations, middle, middle, middle, last, last, last, vectors, vectors,
        ),
        check_vma=False,
    )
```

```python
import functools

import jax
import jax.numpy as jnp
from jax import lax
from jax.experimental import pallas as pl
from jax.experimental.pallas import tpu as pltpu
from jax.sharding import Mesh, PartitionSpec as P

epsilon = 1e-05
F32 = jnp.float32
BF16 = jnp.bfloat16
LANE = 128
STEP = 16
COST = 3.0e6
PER = {"mix": 1, "hidden": 2, "expand": 2, "depth": 1, "grads": 1, "slopes": 2}


def dot_nn(left, right):
    return lax.dot_general(left, right, (((1,), (0,)), ((), ())), preferred_element_type=F32)


def dot_nt(left, right):
    return lax.dot_general(left, right, (((1,), (1,)), ((), ())), preferred_element_type=F32)


def dot_tn(left, right):
    return lax.dot_general(left, right, (((0,), (0,)), ((), ())), preferred_element_type=F32)


def split(value):
    high = value.astype(BF16)
    return high, (value - high.astype(F32)).astype(BF16)


def dot_split(left, right):
    high, rest = split(left)
    return dot_nn(high, right) + dot_nn(rest, right)


def fold(value):
    return jnp.sum(value.reshape(-1, 8, value.shape[-1]), axis=0)


def row_sum(value):
    return jnp.sum(value, axis=0, keepdims=True)


def live_rows(count, frames, rows, width):
    at = lax.rem(lax.broadcasted_iota(jnp.int32, (rows, width), 0), frames)
    return jnp.where(at < count, 1.0, 0.0)


def live_cap(count, frames, rows, width):
    return jnp.where(live_rows(count, frames, rows, width) > 0.5, 3e38, -60.0)


def full(shape):
    return pl.BlockSpec(shape, lambda *_: (0,) * len(shape))


def smem():
    return pl.BlockSpec(memory_space=pltpu.SMEM)


def call(body, steps, in_specs, out_specs, out_shape, scratch, micros):
    return pl.pallas_call(
        body,
        grid=(steps,),
        in_specs=in_specs,
        out_specs=out_specs,
        out_shape=out_shape,
        scratch_shapes=scratch,
        cost_estimate=pl.CostEstimate(
            flops=0, transcendentals=0, bytes_accessed=int(micros * COST)
        ),
        compiler_params=pltpu.CompilerParams(
            dimension_semantics=("arbitrary",), vmem_limit_bytes=58 * 2**20
        ),
    )


def each(count, body, unroll=1):
    def step(i, carry):
        body(pl.multiple_of(i * STEP, STEP))
        return carry

    lax.fori_loop(0, count // STEP, step, 0, unroll=unroll)


def clip_loop(dims, per, body):
    frames, rows, line = dims
    size = rows * line
    step = pl.program_id(0)

    def one(k, carry):
        def view(ref, extra=0):
            length = size + extra * line
            return ref.at[pl.ds(pl.multiple_of(k * length, STEP), length), :]

        body(step * per + k, k, view)
        return carry

    lax.fori_loop(0, per, one, 0)


def merge_stats(means, squares, counts, total):
    mean = jnp.sum(means * counts, axis=0) / total
    away = means - mean[None]
    spread = jnp.sum(squares + counts * away * away, axis=0) / total
    return mean, lax.rsqrt(jnp.maximum(spread, 0.0) + epsilon)


def narrow_norm(nf, got_ref, cnt_ref, gain, bias, vec_ref):
    width = vec_ref.shape[1]
    mean, inverse = merge_stats(
        got_ref[:, :, 0:width], got_ref[:, :, width:], cnt_ref[:, :, 0:1], nf[1]
    )
    scale = gain * inverse
    vec_ref[...] = jnp.zeros_like(vec_ref)
    vec_ref[0:1, :] = inverse
    vec_ref[1:2, :] = -mean * inverse
    vec_ref[2:3, :] = 0.5 * scale
    vec_ref[3:4, :] = 0.5 * (bias - mean * scale)
    vec_ref[4:5, :] = scale


def silu_half(half):
    both = jnp.tanh(half) + 1.0
    return half * both, both


def slope_of(value, both):
    return 0.5 * slope_twice(value, both)


def slope_twice(value, both):
    return both + value * (2.0 - both)


def line_stats(nf, scal, dims, read, lines, first_line, is_first, acc, st_ref):
    frames, rows, line = dims
    width = acc.shape[1]

    @pl.when(is_first)
    def _():
        mask = live_rows(scal[0], frames, STEP, width)
        total = jnp.zeros((8, width), F32)
        for i in range(line // STEP):
            total = total + fold(read(0, i * STEP) * mask)
        acc[...] = jnp.zeros_like(acc)
        alive = (scal[0] * (line // frames)).astype(F32)
        acc[0:1, :] = row_sum(total) / alive

    pivot = acc[0:1, :]

    def one(at, carry):
        plain, square = carry
        mask = live_rows(scal[(first_line + at) // rows], frames, STEP, width)
        for i in range(line // STEP):
            away = (read(at, i * STEP) - pivot) * mask
            plain = plain + fold(away)
            square = square + fold(away * away)
        return plain, square

    zero = jnp.zeros((8, width), F32)
    plain, square = lax.fori_loop(0, lines, one, (zero, zero), unroll=True)
    acc[8:16, :] += plain
    acc[16:24, :] += square


def edge_places(scal, clips, line, rows):
    last = line * (rows + 1)
    near = jnp.where(scal[scal.shape[0] - 1] == 0, last, 0)
    return pl.multiple_of(near, STEP), pl.multiple_of(last - near, STEP)


def hand_over(scal, value, mine_ref, sent_ref):
    even = scal[scal.shape[0] - 1] == 0
    other = value.shape[1] - 1
    mine_ref[...] = jnp.where(even, value[:, 0], value[:, other]).astype(BF16)
    sent_ref[...] = jnp.where(even, value[:, other], value[:, 0]).astype(BF16)


def finish_stats(nf, acc, st_ref):
    plain, square = row_sum(acc[8:16, :]), row_sum(acc[16:24, :])
    width = acc.shape[1]
    peers = st_ref.shape[0]
    st_ref[:, :, 0:width] = jnp.broadcast_to(acc[0:1, :] + plain * nf[2], (peers, 1, width))
    spread = square - plain * plain * nf[2]
    st_ref[:, :, width:] = jnp.broadcast_to(spread, (peers, 1, width))


def share_sums(acc, sum_ref):
    width = acc.shape[1]
    peers = sum_ref.shape[0]
    for k in range(2):
        one = row_sum(acc[8 * k : 8 * k + 8, :])
        sum_ref[:, :, width * k : width * (k + 1)] = jnp.broadcast_to(one, (peers, 1, width))


def depth_weights(par_ref, layer, wd, flip):
    one = lax.broadcasted_iota(jnp.int32, (LANE, LANE), 0)
    two = lax.broadcasted_iota(jnp.int32, (LANE, LANE), 1)
    eye = jnp.where(one == two, 1.0, 0.0)
    for half in range(wd.shape[0]):
        for i in range(9):
            for e in (0, 2):
                tap = 3 * i + e
                at = 27 * layer + (26 - tap if flip else tap)
                row = par_ref[at : at + 1, LANE * half : LANE * (half + 1)]
                k = LANE * (e // 2)
                wd[half, LANE * i : LANE * (i + 1), k : k + LANE] = (eye * row).astype(BF16)


def frame_moves(frames, value):
    width = value.shape[1]
    groups = value.reshape(-1, 8, width)
    here = lax.rem(lax.broadcasted_iota(jnp.int32, (1, 8, width), 1), frames)
    onward = jnp.where(here > 0, pltpu.roll(groups, 1, 1), 0.0)
    back = jnp.where(here < frames - 1, pltpu.roll(groups, 7, 1), 0.0)
    return onward.reshape(value.shape), back.reshape(value.shape)


def frame_shifts(dims, value, tv, at):
    onward, back = frame_moves(dims[0], value)
    part = pl.ds(at, value.shape[0])
    tv[0, part, :] = onward.astype(BF16)
    tv[1, part, :] = value.astype(BF16)
    tv[2, part, :] = back.astype(BF16)


def column_moves(dims, value):
    frames, rows, line = dims
    at = lax.broadcasted_iota(jnp.int32, (8, value.shape[1]), 0)
    onward = pltpu.roll(value, frames, 0)
    top = jnp.where(at >= frames, onward[0:8], 0.0)
    onward = jnp.concatenate([top, onward[8:]], axis=0)
    back = pltpu.roll(value, line - frames, 0)
    bottom = jnp.where(at < 8 - frames, back[line - 8 :], 0.0)
    return onward, jnp.concatenate([back[: line - 8], bottom], axis=0)


def depth_sum(dims, layer, flip, par_ref, ms, tv, wd, ds, temp, store):
    frames, rows, line = dims
    halves = wd.shape[0]
    piece = line // 2 if line % (2 * 8) == 0 else line
    for half in range(halves):
        lanes = slice(LANE * half, LANE * (half + 1))
        views = [tv[a, line * b : line * (b + rows), lanes] for a in range(3) for b in range(3)]
        ds[half] = dot_nn(jnp.concatenate(views, axis=1), wd[half])
        taps = []
        for i in range(9):
            tap = 3 * i + 1
            at = 27 * layer + (26 - tap if flip else tap)
            taps.append(par_ref[at : at + 1, lanes])
        for start in range(0, rows * line, piece):
            seen = [ms[start + line * b : start + line * b + piece, lanes] for b in range(3)]
            sums = []
            for a in range(3):
                one = seen[0] * taps[3 * a]
                one = one + seen[1] * taps[3 * a + 1]
                sums.append(one + seen[2] * taps[3 * a + 2])
            onward, _ = frame_moves(frames, sums[0])
            _, back = frame_moves(frames, sums[2])
            temp[start : start + piece, lanes] = onward + sums[1] + back
    for half in range(halves):
        lanes = slice(LANE * half, LANE * (half + 1))
        for r in range(rows):
            part = slice(line * r, line * (r + 1))
            onward, _ = column_moves(dims, ds[half, part, 0:LANE])
            _, back = column_moves(dims, ds[half, part, LANE : 2 * LANE])
            store(r, lanes, onward + temp[part, lanes] + back)


def pack_kernel(wr_ref, wm_ref, wd_ref, gm_ref, bm_ref, go_ref, bo_ref, out_ref):
    r1, width = wr_ref.shape[1:]
    r2 = wm_ref.shape[1]
    r4, taps = wd_ref.shape[1:]
    r6 = go_ref.shape[1]
    zeros = lambda rows, size: jnp.zeros((rows, size), F32)
    part = [wd_ref[k].astype(F32) for k in range(2)]
    if r4 < 8:
        part = [jnp.concatenate([one, zeros(8 - r4, taps)], axis=0) for one in part]
    pad = zeros(8, 32 - taps)
    mids = [gm_ref[k].astype(F32) for k in range(2)] + [bm_ref[k].astype(F32) for k in range(2)]
    mids = jnp.concatenate(mids, axis=0)
    outs = jnp.concatenate([go_ref[...].astype(F32), bo_ref[...].astype(F32)], axis=0)
    mids = jnp.concatenate([mids, zeros(8, 32 - r4)], axis=1)
    outs = jnp.concatenate([outs, zeros(4, r6)], axis=0)
    small = [part[0], pad, part[1], pad, mids, outs]
    small.append(zeros(8, width - 96 - r6))
    rest = out_ref.shape[1] - r1 - r2 - 8
    rows = [wr_ref[0].astype(F32), wm_ref[0].astype(F32), jnp.concatenate(small, axis=1)]
    if rest:
        rows.append(zeros(rest, width))
    block = jnp.concatenate(rows, axis=0).astype(BF16)
    for k in range(out_ref.shape[0]):
        out_ref[k] = block


def late_pack_kernel(by, wr_ref, wm_ref, we_ref, one_ref, two_ref, cnt_ref, rinv_ref):
    width = wr_ref.shape[2]
    for k in range(cnt_ref.shape[0]):
        count = jnp.full((1, LANE), by[k], F32)
        cnt_ref[k] = count
        rinv_ref[k : k + 1, :] = 1.0 / count
    zeros = lambda rows: jnp.zeros((rows, width), F32)
    for layer, out_ref in enumerate((one_ref, two_ref)):
        wide = we_ref[layer].astype(F32)
        rows = [wide[:, k : k + width] for k in range(0, wide.shape[1], width)]
        rows.append((wr_ref if layer == 0 else wm_ref)[1].astype(F32))
        rest = out_ref.shape[1] - sum(one.shape[0] for one in rows)
        if rest:
            rows.append(zeros(rest))
        block = jnp.concatenate(rows, axis=0).astype(BF16)
        for k in range(out_ref.shape[0]):
            out_ref[k] = block


def first_kernel(dims, lines, scal, nf, x_ref, w_ref, red_ref, up_ref, dn_ref, st_ref, acc, lines_kept):
    step = pl.program_id(0)
    x = x_ref[...].reshape(-1, x_ref.shape[2])
    red_ref[...] = dot_nn(x, w_ref[...].reshape(-1, w_ref.shape[2]))
    reduced_tail(dims, lines, step, scal, nf, red_ref, up_ref, dn_ref, st_ref, acc, lines_kept)


def reduced_tail(dims, lines, step, scal, nf, red_ref, up_ref, dn_ref, st_ref, acc, lines_kept):
    frames, rows, line = dims
    read = lambda at, i: red_ref[pl.ds(pl.multiple_of(line * at, STEP) + i, STEP), :]
    line_stats(nf, scal, dims, read, lines, step * lines, step == 0, acc, st_ref)
    for k in range(lines // rows):
        clip, at = step * (lines // rows) + k, k * rows * line
        even = scal[scal.shape[0] - 1] == 0
        last = line * (rows - 1)
        near = jnp.where(even, last, 0)
        for way, start in enumerate((near, last - near)):
            part = pl.ds(pl.multiple_of(at + start, STEP), line)
            lines_kept[way, clip] = red_ref[part, :]

    @pl.when(step == pl.num_programs(0) - 1)
    def _():
        finish_stats(nf, acc, st_ref)
        mean = acc[0:1, :] + row_sum(acc[8:16, :]) * nf[2]
        for at in range(up_ref.shape[0]):
            up_ref[at] = (lines_kept[0, at] - mean).astype(BF16)
            dn_ref[at] = (lines_kept[1, at] - mean).astype(BF16)


def mix_kernel(
    dims, layer, per, scal, nf, red_ref, up_ref, dn_ref, got_ref, cnt_ref, par_ref, w_ref,
    mix_ref, spa_ref, st_ref, vec_ref, hs, ms, tv, wd, ds, acc,
):
    step, last = pl.program_id(0), pl.num_programs(0) - 1
    width = w_ref.shape[0]

    @pl.when(step == 0)
    def _():
        at = 2 * layer
        narrow_norm(
            nf, got_ref, cnt_ref, par_ref[54 + at : 55 + at, :], par_ref[58 + at : 59 + at, :],
            vec_ref,
        )
        for k in range(2):
            mean = got_ref[scal[scal.shape[0] - 3 + k], :, 0:width]
            vec_ref[5 + k : 6 + k, :] = vec_ref[3:4, :] + vec_ref[2:3, :] * mean
        depth_weights(par_ref, layer, wd, False)

    def body(clip, k, view):
        mix_clip(
            dims, layer, scal, nf, view(red_ref), up_ref.at[k], dn_ref.at[k], par_ref, w_ref,
            view(mix_ref, 2), view(spa_ref), st_ref,
            vec_ref, hs, ms, tv, wd, ds, acc, clip, per * (last + 1),
        )

    clip_loop(dims, per, body)

    @pl.when(step == last)
    def _():
        finish_stats(nf, acc, st_ref)


def mix_clip(
    dims, layer, scal, nf, red_ref, up_ref, dn_ref, par_ref, w_ref, mix_ref, spa_ref, st_ref, vec_ref, hs, ms, tv, wd, ds, acc, clip, clips,
):
    frames, rows, line = dims
    width = w_ref.shape[0]
    mask = live_rows(scal[clip], frames, STEP, width)
    near = mask * scal[clips].astype(F32)
    far = mask * scal[clips + 1].astype(F32)
    near_at, far_at = edge_places(scal, clips, line, rows)

    def edge(i):
        h, _ = silu_half(up_ref[pl.ds(i, STEP), :].astype(F32) * vec_ref[2:3, :] + vec_ref[5:6, :])
        hs[pl.ds(near_at + i, STEP), :] = (h * near).astype(BF16)
        h, _ = silu_half(dn_ref[pl.ds(i, STEP), :].astype(F32) * vec_ref[2:3, :] + vec_ref[6:7, :])
        hs[pl.ds(far_at + i, STEP), :] = (h * far).astype(BF16)

    each(line, edge, 7)

    def own(i):
        value = red_ref[pl.ds(i, STEP), :]
        h, _ = silu_half(value * vec_ref[2:3, :] + vec_ref[3:4, :])
        hs[pl.ds(i + line, STEP), :] = (h * mask).astype(BF16)

    each(line * rows, own, 49)
    ms[...] = dot_nn(hs[...], w_ref[...])

    def shifts(r, carry):
        at = pl.multiple_of(r * line, STEP)
        for half in range(width // LANE):
            lanes = slice(LANE * half, LANE * (half + 1))
            part = pl.ds(at, line)
            value = ms[part, lanes].astype(BF16).astype(F32)
            ms[part, lanes] = value
            frame_shifts(dims, value, tv.at[:, :, lanes], at)
        return carry

    lax.fori_loop(0, rows + 2, shifts, 0, unroll=True)
    mix_ref[...] = tv[1]

    def store(r, lanes, value):
        spa_ref[line * r : line * (r + 1), lanes] = value

    depth_sum(dims, layer, False, par_ref, ms, tv, wd, ds, spa_ref, store)
    read = lambda at, i: spa_ref[pl.ds(pl.multiple_of(line * at, STEP) + i, STEP), :]
    line_stats(nf, scal, dims, read, rows, clip * rows, clip == 0, acc, st_ref)

def hidden_rows(i, mask, spa_ref, h_ref, vec_ref, acc):
    part = pl.ds(i, STEP)
    h, _ = silu_half(spa_ref[part, :] * vec_ref[2:3, :] + vec_ref[3:4, :])
    low = (h * mask).astype(BF16)
    h_ref[part, :] = low
    acc[...] += fold(low.astype(F32))


def slopes_kernel(dims, per, scal, src_ref, vec_ref, z_ref, u_ref, *h_refs):
    frames, rows, line = dims
    width = src_ref.shape[1]

    def body(clip, k, view):
        mask = live_rows(scal[clip], frames, STEP, width)
        src, z_out, u_out = view(src_ref), view(z_ref), view(u_ref)
        h_out = view(h_refs[0]) if h_refs else None

        def own(i):
            part = pl.ds(i, STEP)
            value = src[part, :]
            h, both = silu_half(value * vec_ref[2:3, :] + vec_ref[3:4, :])
            if h_refs:
                h_out[part, :] = (h * mask).astype(BF16)
            u_out[part, :] = (slope_of(h, both) * mask).astype(BF16)
            z_out[part, :] = (value * vec_ref[0:1, :] + vec_ref[1:2, :]).astype(BF16)

        each(line * rows, own, 49)

    clip_loop(dims, per, body)


def hidden_kernel(
    dims, layer, per, scal, nf, spa_ref, got_ref, cnt_ref, par_ref, w_ref,
    h_ref, st_ref, gram_ref, vec_ref, acc,
):
    frames, rows, line = dims
    step = pl.program_id(0)
    width = par_ref.shape[1]

    @pl.when(step == 0)
    def _():
        at = 2 * layer
        narrow_norm(
            nf, got_ref, cnt_ref, par_ref[55 + at : 56 + at, :], par_ref[59 + at : 60 + at, :],
            vec_ref,
        )
        gram_ref[...] = jnp.zeros_like(gram_ref)
        acc[...] = jnp.zeros_like(acc)

    def body(clip, k, view):
        mask = live_rows(scal[clip], frames, STEP, width)
        spa, h_out = view(spa_ref), view(h_ref)

        def own(i):
            hidden_rows(i, mask, spa, h_out, vec_ref, acc)

        each(line * rows, own, 49)

    clip_loop(dims, per, body)
    gram_ref[0:width, :] += dot_tn(h_ref[...], h_ref[...])

    @pl.when(step == pl.num_programs(0) - 1)
    def _():
        total = row_sum(acc[...])
        gram_ref[width : width + 8, :] = jnp.broadcast_to(total, (8, width))
        across = jnp.broadcast_to(total, (width, width))
        centered = gram_ref[0:width, :] - across.T * across * nf[2]
        spread = row_sum(dot_split(centered, w_ref[...]) * w_ref[...].astype(F32))
        peers = st_ref.shape[0]
        st_ref[:, :, 0:width] = jnp.broadcast_to(total, (peers, 1, width))
        st_ref[:, :, width:] = jnp.broadcast_to(spread, (peers, 1, spread.shape[1]))


def wide_norm(nf, got_ref, cnt_ref, rinv_ref, pout_ref, layer, w_ref, vec_ref):
    width = w_ref.shape[0]
    hidden_means = got_ref[:, 0, 0:width] * rinv_ref[:, 0:1]
    means = dot_split(hidden_means, w_ref[...])
    counts = cnt_ref[:, 0, 0:1]
    mean = row_sum(means * counts) / nf[1]
    away = means - mean
    spread = row_sum(got_ref[:, 0, width:] + counts * away * away) / nf[1]
    inverse = lax.rsqrt(jnp.maximum(spread, 0.0) + epsilon)
    scale = pout_ref[layer : layer + 1, :] * inverse
    vec_ref[...] = jnp.zeros_like(vec_ref)
    vec_ref[0:1, :] = scale
    vec_ref[1:2, :] = 0.5 * (pout_ref[2 + layer : 3 + layer, :] - mean * scale)
    vec_ref[2:3, :] = inverse
    vec_ref[3:4, :] = mean
    vec_ref[4:5, :] = 0.5 * scale


def each_line(dims, lines, step, scal, width, body, make=live_cap):
    frames, rows, line = dims

    def run(carry):
        for at in range(lines):
            mask = make(scal[(step * lines + at) // rows], frames, STEP, width)
            for i in range(at * line, (at + 1) * line, STEP):
                carry = body(slice(i, i + STEP), mask, carry)
        return carry

    return run


def join_kernel(
    dims, lines, scal, nf, x_ref, h_ref, got_ref, cnt_ref, rinv_ref, pout_ref, w3_ref, w1_ref,
    next_ref, du_ref, red_ref, up_ref, dn_ref, st_ref, vec_ref, es, acc, lines_kept,
):
    step = pl.program_id(0)
    wide, width = w1_ref.shape
    frames = dims[0]
    block = 256

    @pl.when(step == 0)
    def _():
        wide_norm(nf, got_ref, cnt_ref, rinv_ref, pout_ref, 0, w3_ref, vec_ref)

    for j in range(wide // block):
        lanes = slice(block * j, block * (j + 1))
        es[j % 2] = dot_nn(h_ref[...], w3_ref[:, lanes])
        scale, shift = vec_ref[4:5, lanes], vec_ref[1:2, lanes]

        def own(part, cap, carry):
            spot = slice(part.start // frames, part.stop // frames)
            x = x_ref[spot, :, lanes].reshape(-1, block).astype(F32)
            half = x * 0.5 + (es[j % 2, part, :] * scale + shift)
            o, both = silu_half(jnp.minimum(half, cap))
            next_ref[part, lanes] = (0.5 * o).astype(BF16)
            du_ref[part, lanes] = slope_twice(o, both).astype(BF16)
            return carry

        each_line(dims, lines, step, scal, block, own)(0)
    red_ref[...] = 2.0 * dot_nn(next_ref[...], w1_ref[...])
    reduced_tail(dims, lines, step, scal, nf, red_ref, up_ref, dn_ref, st_ref, acc, lines_kept)


def wide_tail(hT, gs_ref, w3s, low_ref, t_ref):
    t_ref[...] += dot_nn(hT, gs_ref[...])
    low_ref[...] = dot_nt(gs_ref[...], w3s[...]).astype(BF16)


def wide_sums(w3_ref, t_ref, sacc, vec_ref, sum_ref, unit):
    wide = w3_ref.shape[1]
    t_ref[...] = unit * t_ref[...]
    plain = unit * row_sum(sacc[...])
    along = row_sum(w3_ref[...].astype(F32) * t_ref[...])
    along = (along - vec_ref[3:4, :] * plain) * vec_ref[2:3, :]
    pieces = [
        one[:, LANE * k : LANE * (k + 1)] for one in (plain, along) for k in range(wide // LANE)
    ]
    sum_ref[...] = jnp.broadcast_to(jnp.concatenate(pieces, axis=0)[None], sum_ref.shape).astype(
        BF16
    )


def out_kernel(
    dims, lines, scal, nf, x_ref, h_ref, cot_ref, got_ref, cnt_ref, rinv_ref, pout_ref, w3_ref,
    out_ref, gs_ref, low_ref, t_ref, sum_ref, vec_ref, es, w3s, sacc,
):
    step = pl.program_id(0)
    width, wide = w3_ref.shape
    frames = dims[0]
    block = 256
    unit = 0.5

    @pl.when(step == 0)
    def _():
        wide_norm(nf, got_ref, cnt_ref, rinv_ref, pout_ref, 1, w3_ref, vec_ref)
        t_ref[...] = jnp.zeros_like(t_ref)
        sacc[...] = jnp.zeros_like(sacc)
        w3s[...] = (w3_ref[...].astype(F32) * (unit * vec_ref[0:1, :])).astype(BF16)

    hT = h_ref[...].T
    for j in range(wide // block):
        lanes = slice(block * j, block * (j + 1))
        es[j % 2] = dot_nn(h_ref[...], w3_ref[:, lanes])
        scale, shift = vec_ref[4:5, lanes], vec_ref[1:2, lanes]

        def own(part, cap, total):
            half = x_ref[part, lanes].astype(F32) + (es[j % 2, part, :] * scale + shift)
            o, both = silu_half(jnp.minimum(half, cap))
            spot = slice(part.start // frames, part.stop // frames)
            out_ref[spot, :, lanes] = o.astype(BF16).reshape(-1, frames, block)
            grad = cot_ref[spot, :, lanes].reshape(-1, block).astype(F32)
            grad = grad * slope_twice(o, both)
            gs_ref[part, lanes] = grad.astype(BF16)
            return total + fold(grad)

        total = each_line(dims, lines, step, scal, block, own)(jnp.zeros((8, block), F32))
        sacc[:, lanes] += total
    wide_tail(hT, gs_ref, w3s, low_ref, t_ref)

    @pl.when(step == pl.num_programs(0) - 1)
    def _():
        wide_sums(w3_ref, t_ref, sacc, vec_ref, sum_ref, unit)


def expand_back_kernel(
    dims, per, scal, nf, low_ref, h_ref, z_ref, u_ref, got_ref, vec_ref, w3_ref,
    go_ref, up_ref, dn_ref, sum_ref, tot_ref, ks, crow, hk, acc,
):
    frames, rows, line = dims
    step = pl.program_id(0)
    width, wide = w3_ref.shape

    @pl.when(step == 0)
    def _():
        totals = jnp.sum(got_ref[...].astype(F32), axis=0)
        count = wide // LANE
        plain = jnp.concatenate([totals[k : k + 1, :] for k in range(count)], axis=1)
        along = jnp.concatenate([totals[k : k + 1, :] for k in range(count, 2 * count)], axis=1)
        tot_ref[:, 0:wide] = plain
        tot_ref[:, wide:] = along
        w3 = w3_ref[...]
        rise, flat = wide_rows_of(nf, plain, along, vec_ref)
        ks[...] = dot_nt((w3.astype(F32) * rise).astype(BF16), w3).astype(BF16)
        spread = [jnp.broadcast_to(one, (16, wide)) for one in split(flat)]
        crow[...] = (dot_nt(spread[0], w3) + dot_nt(spread[1], w3))[0:8]
        acc[...] = jnp.zeros_like(acc)

    hk[...] = dot_nn(h_ref[...], ks[...])

    def own(i):
        part = pl.ds(i, STEP)
        grad = low_ref[part, :].astype(F32) - crow[0:1, :] - hk[part, :]
        grad = grad * u_ref[part, :].astype(F32)
        go_ref[part, :] = grad.astype(BF16)
        acc[0:8, :] += fold(grad)
        acc[8:16, :] += fold(grad * z_ref[part, :].astype(F32))

    each(line * rows * per, own, 49)
    for k in range(per):
        expand_edges(dims, scal, k * rows * line, go_ref, z_ref, up_ref.at[k], dn_ref.at[k])

    @pl.when(step == pl.num_programs(0) - 1)
    def _():
        share_sums(acc, sum_ref)


def wide_rows_of(nf, plain, along, vec_ref):
    scale, inverse, mean = vec_ref[0:1, :], vec_ref[2:3, :], vec_ref[3:4, :]
    rise = scale * inverse * along * nf[3]
    return rise, scale * plain * nf[3] - rise * mean


def expand_grad_kernel(
    scal, nf, tot_ref, vec_ref, t_ref, gram_ref, w3_ref, mine_ref, sent_ref
):
    width, wide = w3_ref.shape
    rise, flat = wide_rows_of(nf, tot_ref[:, 0:wide], tot_ref[:, wide:], vec_ref)
    column = jnp.broadcast_to(gram_ref[width : width + 1, :], (LANE, width)).T[:, 0:1]
    cross = dot_split(gram_ref[0:width, :], w3_ref[...])
    ge = t_ref[...] * vec_ref[0:1, :] - column * flat - cross * rise
    chips, size = mine_ref.shape[0:2]
    parts = [ge[:, width * k : width * (k + 1)] for k in range(wide // width)]
    parts = [one.reshape(chips, -1, size * width // wide, width) for one in parts]
    hand_over(scal, jnp.concatenate(parts, axis=2), mine_ref, sent_ref)


def expand_edges(dims, scal, base, go_ref, z_ref, up_ref, dn_ref):
    frames, rows, line = dims
    even = scal[scal.shape[0] - 1] == 0
    last = line * (rows - 1)
    first = jnp.where(even, last, 0)
    near = pl.multiple_of(base + first, STEP)
    far = pl.multiple_of(base + last - first, STEP)
    up_ref[0] = go_ref[pl.ds(near, line), :]
    up_ref[1] = z_ref[pl.ds(near, line), :]
    dn_ref[0] = go_ref[pl.ds(far, line), :]
    dn_ref[1] = z_ref[pl.ds(far, line), :]


def norm_rows(nf, got_ref, vec_ref, tot_ref, rows3):
    totals = jnp.sum(got_ref[...], axis=0)
    tot_ref[...] = totals
    norm_terms(nf, totals, vec_ref, rows3)


def norm_terms(nf, totals, vec_ref, rows3):
    width = vec_ref.shape[1]
    rows3[0:1, :] = vec_ref[4:5, :]
    rows3[1:2, :] = vec_ref[4:5, :] * totals[:, 0:width] * nf[3]
    rows3[2:3, :] = vec_ref[4:5, :] * totals[:, width:] * nf[3]


def norm_back(rows3, go, z, mask):
    value = rows3[0:1, :] * go.astype(F32) - rows3[1:2, :] - rows3[2:3, :] * z.astype(F32)
    return value * mask


def depth_back_kernel(
    dims, layer, per, scal, nf, go_ref, above_ref, below_ref, z_ref, got_ref, vec_ref,
    z1_ref, u1_ref, par_ref, w_ref,
    go1_ref, sum_ref, gm_ref, gp_ref, tot_ref, ms, tv, wd, ds, gh, rows3, acc,
):
    step, last = pl.program_id(0), pl.num_programs(0) - 1
    width = w_ref.shape[0]

    @pl.when(step == 0)
    def _():
        norm_rows(nf, got_ref, vec_ref, tot_ref, rows3)
        depth_weights(par_ref, layer, wd, True)
        acc[...] = jnp.zeros_like(acc)

    def body(clip, k, view):
        depth_back_clip(
            dims, layer, scal, view(go_ref), above_ref.at[k], below_ref.at[k], view(z_ref),
            view(z1_ref), view(u1_ref), par_ref, w_ref, view(go1_ref), view(gm_ref), view(gp_ref),
            ms, tv, wd, ds, gh, rows3, acc, clip, per * (last + 1),
        )

    clip_loop(dims, per, body)

    @pl.when(step == last)
    def _():
        share_sums(acc, sum_ref)


def depth_back_clip(
    dims, layer, scal, go_ref, above_ref, below_ref, z_ref, z1_ref, u1_ref, par_ref, w_ref,
    go1_ref, gm_ref, gp_ref, ms, tv, wd, ds, gh, rows3, acc, clip, clips,
):
    frames, rows, line = dims
    width = w_ref.shape[0]
    mask = live_rows(scal[clip], frames, STEP, width)
    near = mask * scal[clips].astype(F32)
    far = mask * scal[clips + 1].astype(F32)
    near_at, far_at = edge_places(scal, clips, line, rows)

    def edge(i):
        part = pl.ds(i, STEP)
        ms[pl.ds(near_at + i, STEP), :] = norm_back(
            rows3, above_ref[0, part, :], above_ref[1, part, :], near
        )
        ms[pl.ds(far_at + i, STEP), :] = norm_back(
            rows3, below_ref[0, part, :], below_ref[1, part, :], far
        )

    each(line, edge, 7)

    def own(i):
        part = pl.ds(i, STEP)
        ms[pl.ds(i + line, STEP), :] = norm_back(rows3, go_ref[part, :], z_ref[part, :], mask)

    each(line * rows, own, 49)

    def shifts(r, carry):
        at = pl.multiple_of(r * line, STEP)
        for half in range(width // LANE):
            lanes = slice(LANE * half, LANE * (half + 1))
            part = pl.ds(at, line)
            value = ms[part, lanes].astype(BF16).astype(F32)
            ms[part, lanes] = value
            frame_shifts(dims, value, tv.at[:, :, lanes], at)
        return carry

    lax.fori_loop(0, rows + 2, shifts, 0, unroll=True)
    gp_ref[...] = tv[1, line : line * (rows + 1), :]

    def store(r, lanes, value):
        gm_ref[line * r : line * (r + 1), lanes] = value.astype(BF16)

    depth_sum(dims, layer, True, par_ref, ms, tv, wd, ds, gh, store)
    gh[...] = dot_nt(gm_ref[...], w_ref[...])

    def first(i):
        part = pl.ds(i, STEP)
        value = gh[part, :] * u1_ref[part, :].astype(F32)
        go1_ref[part, :] = value.astype(BF16)
        acc[0:8, :] += fold(value)
        acc[8:16, :] += fold(value * z1_ref[part, :].astype(F32))

    each(line * rows, first, 49)

def kernel_grads(
    dims, per, scal, mix_ref, gp_ref, gm_ref, h_ref,
    mine_ref, sent_ref, gmix_ref, gdep_ref, tv, mv, gacc, vacc,
):
    step = pl.program_id(0)
    width = h_ref.shape[1]
    halves = width // LANE

    @pl.when(step == 0)
    def _():
        gmix_ref[...] = jnp.zeros_like(gmix_ref)
        gacc[...] = jnp.zeros_like(gacc)
        vacc[...] = jnp.zeros_like(vacc)

    gmix_ref[...] += dot_tn(h_ref[...], gm_ref[...])

    def body(clip, k, view):
        kernel_clip(dims, halves, view(mix_ref, 2), view(gp_ref), tv, mv, gacc, vacc)

    clip_loop(dims, per, body)

    @pl.when(step == pl.num_programs(0) - 1)
    def _():
        one = lax.broadcasted_iota(jnp.int32, (LANE, LANE), 0)
        two = lax.broadcasted_iota(jnp.int32, (LANE, LANE), 1)
        gdep_ref[...] = jnp.zeros_like(gdep_ref)
        for half in range(halves):
            lanes = slice(LANE * half, LANE * (half + 1))
            for i in range(9):
                gdep_ref[3 * i + 1 : 3 * i + 2, lanes] = row_sum(vacc[i, :, lanes])
                for e in (0, 2):
                    k = LANE * (e // 2)
                    part = gacc[half, k : k + LANE, LANE * i : LANE * (i + 1)]
                    gdep_ref[3 * i + e : 3 * i + e + 1, lanes] = row_sum(
                        jnp.where(one == two, part, 0.0)
                    )
        chips, size = mine_ref.shape[0:2]
        taps = jnp.concatenate([gdep_ref[...].T, jnp.zeros((width, width - LANE), F32)], axis=1)
        parts = [gmix_ref[...], taps]
        parts = [one.reshape(chips, -1, size // 2, width) for one in parts]
        hand_over(scal, jnp.concatenate(parts, axis=2), mine_ref, sent_ref)


def kernel_clip(dims, halves, mix_ref, gp_ref, tv, mv, gacc, vacc):
    frames, rows, line = dims

    def shifts(r, carry):
        at = pl.multiple_of(r * line, STEP)
        for half in range(halves):
            lanes = slice(LANE * half, LANE * (half + 1))
            value = mix_ref[pl.ds(at, line), lanes].astype(F32)
            frame_shifts(dims, value, tv.at[:, :, lanes], at)
        return carry

    lax.fori_loop(0, rows + 2, shifts, 0, unroll=True)

    def moves(r, carry):
        at = pl.multiple_of(r * line, STEP)
        for half in range(halves):
            lanes = slice(LANE * half, LANE * (half + 1))
            value = gp_ref[pl.ds(at, line), lanes].astype(F32)
            onward, back = column_moves(dims, value)
            mv[half, pl.ds(at, line), 0:LANE] = back.astype(BF16)
            mv[half, pl.ds(at, line), LANE : 2 * LANE] = onward.astype(BF16)
        return carry

    lax.fori_loop(0, rows, moves, 0, unroll=True)
    for half in range(halves):
        lanes = slice(LANE * half, LANE * (half + 1))
        views = [tv[a, line * b : line * (b + rows), lanes] for a in range(3) for b in range(3)]
        gacc[half] += dot_tn(mv[half], jnp.concatenate(views, axis=1))
        sums = [vacc[i, :, lanes] for i in range(9)]
        for start in range(0, rows * line, line):
            own = gp_ref[start : start + line, lanes].astype(F32)
            onward, back = frame_moves(frames, own)
            for b in range(3):
                seen = mix_ref[start + line * b : start + line * b + line, lanes].astype(F32)
                for a, moved in enumerate((back, own, onward)):
                    sums[3 * a + b] = sums[3 * a + b] + fold(moved * seen)
        for i in range(9):
            vacc[i, :, lanes] = sums[i]


def reduced_grad(dims, lines, step, scal, go_ref, z_ref, rows3, gr_ref):
    def own(part, mask, carry):
        gr_ref[part, :] = norm_back(rows3, go_ref[part, :], z_ref[part, :], mask).astype(BF16)
        return carry

    each_line(dims, lines, step, scal, rows3.shape[1], own, live_rows)(0)


def cross_kernel(
    dims, lines, scal, nf, go_ref, z_ref, got_ref, vec1_ref, gs_ref, du_ref, h_ref,
    vec3_ref, w1_ref, w3_ref,
    gs0_ref, low_ref, t_ref, sum_ref, tot_ref, gr_ref, ds, w1s, w3s, rows3, sacc,
):
    step = pl.program_id(0)
    width, wide = w3_ref.shape
    block = 256
    unit = 0.25

    @pl.when(step == 0)
    def _():
        norm_rows(nf, got_ref, vec1_ref, tot_ref, rows3)
        t_ref[...] = jnp.zeros_like(t_ref)
        sacc[...] = jnp.zeros_like(sacc)
        w3s[...] = (w3_ref[...].astype(F32) * (unit * vec3_ref[0:1, :])).astype(BF16)
        w1s[...] = (w1_ref[...].astype(F32) * 2.0).astype(BF16)

    reduced_grad(dims, lines, step, scal, go_ref, z_ref, rows3, gr_ref)
    hT = h_ref[...].T
    for j in range(wide // block):
        lanes = slice(block * j, block * (j + 1))
        ds[j % 2] = dot_nt(gr_ref[...], w1s[lanes, :])

        def own(part, mask, total):
            value = gs_ref[part, lanes].astype(F32) + ds[j % 2, part, :]
            value = value * du_ref[part, lanes].astype(F32)
            gs0_ref[part, lanes] = value.astype(BF16)
            return total + fold(value)

        total = each_line(dims, lines, step, scal, block, own)(jnp.zeros((8, block), F32))
        sacc[:, lanes] += total
    wide_tail(hT, gs0_ref, w3s, low_ref, t_ref)

    @pl.when(step == pl.num_programs(0) - 1)
    def _():
        wide_sums(w3_ref, t_ref, sacc, vec3_ref, sum_ref, unit)


def reduce_grad_kernel(
    dims, lines, unit, scal, nf, go_ref, z_ref, tot_ref, vec1_ref, x_ref,
    mine_ref, sent_ref, gr, rows3, gacc,
):
    step = pl.program_id(0)

    @pl.when(step == 0)
    def _():
        norm_terms(nf, tot_ref[...], vec1_ref, rows3)
        gacc[...] = jnp.zeros_like(gacc)

    reduced_grad(dims, lines, step, scal, go_ref, z_ref, rows3, gr)
    gacc[...] += dot_tn(gr[...], x_ref[...])

    @pl.when(step == pl.num_programs(0) - 1)
    def _():
        chips, size, width = mine_ref.shape
        value = (unit * gacc[...].T).reshape(chips, -1, size, width)
        hand_over(scal, value, mine_ref, sent_ref)


def last_grad_kernel(
    dims, lines, scal, nf, go_ref, z_ref, got_ref, vec1_ref, x_ref,
    gr_ref, mine_ref, sent_ref, tot_ref, rows3, gacc,
):
    step = pl.program_id(0)

    @pl.when(step == 0)
    def _():
        norm_rows(nf, got_ref, vec1_ref, tot_ref, rows3)
        gacc[...] = jnp.zeros_like(gacc)

    reduced_grad(dims, lines, step, scal, go_ref, z_ref, rows3, gr_ref)
    gacc[...] += dot_tn(gr_ref[...], x_ref[...].reshape(-1, x_ref.shape[2]))

    @pl.when(step == pl.num_programs(0) - 1)
    def _():
        chips, size, width = mine_ref.shape
        hand_over(scal, gacc[...].T.reshape(chips, -1, size, width), mine_ref, sent_ref)


def input_kernel(gr_ref, gs_ref, w1_ref, out_ref):
    w1 = w1_ref[...].reshape(-1, w1_ref.shape[2])
    value = dot_nt(gr_ref[...], w1) + 0.25 * gs_ref[...].astype(F32)
    out_ref[...] = value.astype(BF16).reshape(out_ref.shape)


ALL = ("clip", "outer", "inner")
CHIPS = ("clip", "outer")
SP = ("outer", "inner")


def share(rows):
    return lax.all_to_all(rows, ALL, 0, 0)


def gather(value):
    return share(jnp.broadcast_to(value[None], (lax.axis_size(ALL),) + value.shape))


def neighbours(near, far):
    peers = lax.axis_size(SP)
    first = [(i, i + 1) for i in range(0, peers - 1, 2)]
    second = [(i, i + 1) for i in range(1, peers - 1, 2)]
    near = lax.ppermute(near, SP, first + [(j, i) for i, j in first])
    far = lax.ppermute(far, SP, second + [(j, i) for i, j in second])
    return near, far


def swap(value):
    peers = lax.axis_size("inner")
    return lax.ppermute(value, "inner", [(i, (i + 1) % peers) for i in range(peers)])


def after(value, other):
    return lax.optimization_barrier((value, other))[0]


def on_device(
    features, strides, cotangent, w_reduce, w_mix, w_expand, w_depth,
    gains_mid, biases_mid, gains_out, biases_out,
):
    clips, frames, rows, columns, wide = features.shape
    width = w_mix.shape[2]
    peers, chips = lax.axis_size(ALL), lax.axis_size(CHIPS)
    inner = lax.axis_size("inner")
    sp_size = lax.axis_size(SP)
    part, place = lax.axis_index("inner"), lax.axis_index(ALL)
    sp_at = lax.axis_index(SP)
    line = columns * frames
    per_clip = rows * line
    voxels = clips * per_clip
    r1, r2 = w_reduce.shape[1], w_mix.shape[1]
    r4 = w_depth.shape[2]
    r5 = gains_out.shape[1] // r4
    blocks = wide // width

    def from_cores(near):
        held = [near]
        for _ in range(inner - 1):
            held.append(swap(held[-1]))
        turns = [lax.rem(part - c + inner, inner) for c in range(inner)]
        whole = jnp.stack([lax.select_n(turn, *held) for turn in turns], axis=1)
        return whole.reshape((peers,) + near.shape[1:])

    def wide_weight(rows_of_all):
        one = rows_of_all.reshape(peers, blocks, r2, width).transpose(0, 2, 1, 3)
        return one.reshape(peers * r2, wide)

    height = r1 + r2 + 8
    height += -height % 16
    whole = lambda value: full(value.shape)
    raw = (w_reduce, w_mix, w_depth.transpose(0, 2, 1), gains_mid, biases_mid, gains_out,
           biases_out)
    packed = call(
        pack_kernel, 1, [whole(one) for one in raw], full((chips, height, width)),
        jax.ShapeDtypeStruct((chips, height, width), BF16), [], 1,
    )(*raw)
    near = lax.all_to_all(packed, CHIPS, 0, 0)
    x = features.transpose(0, 2, 3, 1, 4).reshape(voxels // frames, frames, wide)
    counts = frames // strides
    by_group = jnp.sum(counts.reshape(-1, clips), axis=1) * (rows * columns)
    by_device = jnp.repeat(by_group, sp_size).astype(F32)
    local = lax.dynamic_slice_in_dim(counts, lax.axis_index("clip") * clips, clips)
    odd = lax.rem(sp_at, 2)
    has_near = (odd == 1) | (sp_at < sp_size - 1)
    has_far = jnp.where(odd == 1, sp_at < sp_size - 1, sp_at > 0)
    way = jnp.where(odd == 1, -1, 1)
    base = lax.axis_index("clip") * sp_size
    near_place = base + jnp.clip(sp_at + way, 0, sp_size - 1)
    far_place = base + jnp.clip(sp_at - way, 0, sp_size - 1)
    edges = jnp.stack(
        [has_near.astype(jnp.int32), has_far.astype(jnp.int32), near_place, far_place, odd]
    )
    scal = jnp.concatenate([local.astype(jnp.int32), edges])
    own = jnp.sum(local).astype(F32) * (rows * columns)
    total = jnp.sum(by_device)
    nf = jnp.stack([own, total, 1.0 / own, 1.0 / total])

    sizes = [r2 * blocks + r1, r2 * blocks + r2]
    sizes = [(chips, one + -one % 16, width) for one in sizes]
    raw = (w_reduce, w_mix, w_expand)
    spaces = [full(one) for one in sizes] + [full((peers, 1, LANE)), full((peers, LANE))]
    late_one, late_two, cnt, rinv = call(
        late_pack_kernel, 1, [smem()] + [whole(one) for one in raw], spaces,
        [jax.ShapeDtypeStruct(one, BF16) for one in sizes]
        + [jax.ShapeDtypeStruct(one, F32) for one in ((peers, 1, LANE), (peers, LANE))], [], 1,
    )(by_device, *raw)
    near, late_one, late_two, scal, nf, cnt, rinv = lax.optimization_barrier(
        (near, late_one, late_two, scal, nf, cnt, rinv)
    )
    early = from_cores(near)
    w2 = [early[:, r1 : r1 + r2].reshape(-1, width)]
    at = r1 + r2
    taps = early[:, at : at + r4, 0:64].reshape(-1, 64).T
    taps = [taps[32 * k : 32 * k + 27] for k in range(2)]
    mids = early[:, at : at + 8, 64 : 64 + r4].transpose(1, 0, 2).reshape(8, width)
    par = jnp.concatenate([*taps, mids, jnp.zeros((2, width), BF16)], axis=0).astype(F32)
    pout = early[:, at : at + 4, 96 : 96 + r4 * r5].transpose(1, 0, 2).reshape(4, wide)
    pout = pout.astype(F32)

    struct = jax.ShapeDtypeStruct
    dims = (frames, rows, line)
    lines = rows
    steps = clips * rows // lines
    many_lines = 2 * rows if clips % 2 == 0 else rows
    few = clips * rows // many_lines
    tall = (rows + 2) * line
    by_step = lambda size: pl.BlockSpec((lines * line, size), lambda s: (s, 0))
    thin, broad = by_step(width), by_step(wide)

    def by_clip(name):
        per = PER[name] if clips % PER[name] == 0 else 1
        field = pl.BlockSpec((per * per_clip, width), lambda c: (c, 0))
        tall_field = pl.BlockSpec((per * tall, width), lambda c: (c, 0))
        edge_one = pl.BlockSpec((per, line, width), lambda c: (c, 0, 0))
        edge_two = pl.BlockSpec((per, 2, line, width), lambda c: (c, 0, 0, 0))
        return per, field, tall_field, edge_one, edge_two

    native = pl.BlockSpec((lines * line // frames, frames, wide), lambda s: (s, 0, 0))
    size = many_lines * line
    big_thin = pl.BlockSpec((size, width), lambda s: (s, 0))
    big_broad = pl.BlockSpec((size, wide), lambda s: (s, 0))
    big_native = pl.BlockSpec((size // frames, frames, wide), lambda s: (s, 0, 0))
    native_shape = struct((voxels // frames, frames, wide), BF16)
    narrow = lambda kind: struct((voxels, width), kind)
    wide_shape = struct((voxels, wide), BF16)
    edge = struct((clips, line, width), BF16)
    lines_kept = pltpu.VMEM((2, clips, line, width), F32)
    pair = struct((clips, 2, line, width), BF16)
    flat = lambda *shape: struct(shape, F32)
    two = (peers, 1, 2 * width)
    three = (peers, 1, width + wide)
    many = (peers, 2 * wide // LANE, LANE)
    vec, vec_wide = (8, width), (8, wide)
    owned = struct((chips, r1, width), BF16)
    owned_taps = struct((chips, 2 * r2, width), BF16)

    reduced, up, dn, stats = call(
        functools.partial(first_kernel, dims, many_lines), few,
        [smem(), smem(), big_native, full((peers, r1, width))],
        [big_thin, full(edge.shape), full(edge.shape), full(two)],
        [narrow(F32), edge, edge, flat(*two)],
        [pltpu.VMEM((24, width), F32), lines_kept], 6,
    )(scal, nf, x, early)

    depth_scratch = [
        pltpu.VMEM((tall, width), F32), pltpu.VMEM((3, tall, width), BF16),
        pltpu.VMEM((width // LANE, 9 * LANE, 2 * LANE), BF16),
        pltpu.VMEM((width // LANE, per_clip, 2 * LANE), F32),
    ]
    above, below = neighbours(up, dn)
    got = share(stats)
    got, cnt, par, w2[0] = lax.optimization_barrier((got, cnt, par, w2[0]))
    late_one = after(late_one, (got, above, below))
    near = lax.all_to_all(late_one, CHIPS, 0, 0)
    w1, w3 = [early], []
    stored = []
    for layer in range(2):
        if layer == 1:
            above, below = neighbours(up, dn)
            stats, near = lax.optimization_barrier((stats, near))
            got = share(stats)
            late = from_cores(near)
            w2.append(late[:, r2 * blocks : r2 * blocks + r2].reshape(-1, width))
        per, field, tall_field, edge_one, edge_two = by_clip("mix")
        mixed, spatial, stats, vec1 = call(
            functools.partial(mix_kernel, dims, layer, per), clips // per,
            [smem(), smem(), field, edge_one, edge_one, full(two),
             full((peers, 1, LANE)), full((64, width)), full((width, width))],
            [tall_field, field, full(two), full(vec)],
            [struct((clips * tall, width), BF16), narrow(F32), flat(*two), flat(*vec)],
            [pltpu.VMEM((tall, width), BF16), *depth_scratch, pltpu.VMEM((24, width), F32)], 10,
        )(scal, nf, reduced, above, below, got, cnt, par, w2[layer])
        got = share(stats)
        per, field, tall_field, edge_one, edge_two = by_clip("slopes")
        z1, u1, h1 = call(
            functools.partial(slopes_kernel, dims, per), clips // per,
            [smem(), field, full(vec)], [field] * 3, [narrow(BF16)] * 3, [], 5,
        )(scal, reduced, vec1)
        if layer == 1:
            w3.append(wide_weight(late[:, : r2 * blocks]))
        else:
            late = from_cores(after(near, stats))
            w3.append(wide_weight(late[:, : r2 * blocks]))
            at = r2 * blocks
            w1.append(late[:, at : at + r1].reshape(-1, width))
        got, z1, u1, h1, w3[layer] = lax.optimization_barrier((got, z1, u1, h1, w3[layer]))
        per, field, tall_field, edge_one, edge_two = by_clip("hidden")
        h2, stats, gram, vec2 = call(
            functools.partial(hidden_kernel, dims, layer, per), clips // per,
            [smem(), smem(), field, full(two), full((peers, 1, LANE)),
             full((64, width)), full((width, wide))],
            [field, full(three), full((width + 8, width)), full(vec)],
            [narrow(BF16), flat(*three), flat(width + 8, width), flat(*vec)],
            [pltpu.VMEM((8, width), F32)], 5,
        )(scal, nf, spatial, got, cnt, par, w3[layer])
        got = share(stats)
        per, field, tall_field, edge_one, edge_two = by_clip("slopes")
        z2, u2 = call(
            functools.partial(slopes_kernel, dims, per), clips // per,
            [smem(), field, full(vec)], [field] * 2, [narrow(BF16)] * 2, [], 5,
        )(scal, spatial, vec2)
        got, z2, u2 = lax.optimization_barrier((got, z2, u2))
        if layer == 0:
            got, pout, rinv, w1[1] = lax.optimization_barrier((got, pout, rinv, w1[1]))
            near = lax.all_to_all(after(late_two, got), CHIPS, 0, 0)
        norm_specs = [full(three), full((peers, 1, LANE)), full((peers, LANE)),
                      full((4, wide)), full((width, wide))]
        norm_args = (got, cnt, rinv, pout, w3[layer])
        if layer == 0:
            carried, slope, reduced, up, dn, stats, vec3 = call(
                functools.partial(join_kernel, dims, lines), steps,
                [smem(), smem(), native, thin] + norm_specs + [full((wide, width))],
                [broad, broad, thin, full(edge.shape), full(edge.shape), full(two),
                 full(vec_wide)],
                [wide_shape, wide_shape, narrow(F32), edge, edge, flat(*two), flat(*vec_wide)],
                [pltpu.VMEM((2, lines * line, 256), F32), pltpu.VMEM((24, width), F32),
                 lines_kept], 12,
            )(scal, nf, x, h2, *norm_args, w1[1])
        else:
            cot = cotangent.transpose(0, 2, 3, 1, 4).reshape(voxels // frames, frames, wide)
            output, gs, low, t, sums, vec3 = call(
                functools.partial(out_kernel, dims, lines), steps,
                [smem(), smem(), broad, thin, native] + norm_specs,
                [native, broad, thin, full((width, wide)), full(many), full(vec_wide)],
                [native_shape, wide_shape, narrow(BF16), flat(width, wide), struct(many, BF16),
                 flat(*vec_wide)],
                [pltpu.VMEM((2, lines * line, 256), F32), pltpu.VMEM((width, wide), BF16),
                 pltpu.VMEM((8, wide), F32)], 15,
            )(scal, nf, carried, h2, cot, *norm_args)
        stored.append((z1, u1, h1, vec1, mixed, z2, u2, h2, vec2, gram, vec3))

    def voxel_form(value):
        return value.reshape(clips, rows, columns, frames, wide).transpose(0, 3, 1, 2, 4)

    def sum_cores(*pieces):
        if inner == 1:
            return jnp.concatenate([mine for mine, _ in pieces], axis=1)
        return jnp.concatenate([mine + swap(sent) for mine, sent in pieces], axis=1)

    results = [None, None]
    for layer in (1, 0):
        z1, u1, h1, vec1, mixed, z2, u2, h2, vec2, gram, vec3 = stored[layer]
        if layer == 0:
            sums = after(sums, first)
        got = share(sums)
        if layer == 0:
            got, reduce_mine, reduce_sent = lax.optimization_barrier(
                (got, reduce_mine, reduce_sent)
            )
            reduce_sum = sum_cores((reduce_mine, reduce_sent))
        per, field, tall_field, edge_one, edge_two = by_clip("expand")
        go2, up, dn, sums, tot3 = call(
            functools.partial(expand_back_kernel, dims, per), clips // per,
            [smem(), smem(), field, field, field, field, full(many), full(vec_wide),
             full((width, wide))],
            [field, edge_two, edge_two, full(two), full((1, 2 * wide))],
            [narrow(BF16), pair, pair, flat(*two), flat(1, 2 * wide)],
            [pltpu.VMEM((width, width), BF16), pltpu.VMEM(vec, F32),
             pltpu.VMEM((per * per_clip, width), F32), pltpu.VMEM((16, width), F32)], 6,
        )(scal, nf, low, h2, z2, u2, got, vec3, w3[layer])
        expand_mine, expand_sent = call(
            expand_grad_kernel, 1,
            [smem(), smem(), full((1, 2 * wide)), full(vec_wide), full((width, wide)),
             full((width + 8, width)), full((width, wide))],
            [full(owned.shape), full(owned.shape)], [owned, owned], [], 3,
        )(scal, nf, tot3, vec3, t, gram, w3[layer])
        if layer == 0:
            sums, reduce_sum = lax.optimization_barrier((sums, reduce_sum))
        above, below = neighbours(up, dn)
        got = share(sums)
        got, expand_mine, expand_sent = lax.optimization_barrier((got, expand_mine, expand_sent))
        expands = (expand_mine, expand_sent)
        if layer == 0:
            second = jnp.concatenate([reduce_sum, sum_cores(expands)], axis=1)
            second = lax.all_to_all(after(second, (got, above, below)), CHIPS, 0, 0)
        per, field, tall_field, edge_one, edge_two = by_clip("depth")
        go1, sums, gm, gp, tot2 = call(
            functools.partial(depth_back_kernel, dims, layer, per), clips // per,
            [smem(), smem(), field, edge_two, edge_two, field, full(two), full(vec), field,
             field, full((64, width)), full((width, width))],
            [field, full(two), field, field, full((1, 2 * width))],
            [narrow(BF16), flat(*two), narrow(BF16), narrow(BF16), flat(1, 2 * width)],
            [*depth_scratch, pltpu.VMEM((per_clip, width), F32), pltpu.VMEM(vec, F32),
             pltpu.VMEM((16, width), F32)], 12,
        )(scal, nf, go2, above, below, z2, got, vec2, z1, u1, par, w2[layer])
        if layer == 0:
            sums = after(sums, second)
        got = share(sums)
        per, field, tall_field, edge_one, edge_two = by_clip("grads")
        taps_mine, taps_sent = call(
            functools.partial(kernel_grads, dims, per), clips // per,
            [smem(), tall_field, field, field, field],
            [full(owned_taps.shape), full(owned_taps.shape)],
            [owned_taps, owned_taps],
            [pltpu.VMEM((width, width), F32), pltpu.VMEM((LANE, width), F32),
             pltpu.VMEM((3, tall, width), BF16),
             pltpu.VMEM((width // LANE, per_clip, 2 * LANE), BF16),
             pltpu.VMEM((width // LANE, 2 * LANE, 9 * LANE), F32),
             pltpu.VMEM((9, 8, width), F32)], 12,
        )(scal, mixed, gp, gm, h1)
        got, taps_mine, taps_sent = lax.optimization_barrier((got, taps_mine, taps_sent))
        if layer == 1:
            first = lax.all_to_all(sum_cores((taps_mine, taps_sent), expands), CHIPS, 0, 0)
        if layer == 1:
            h2_0, vec3_0 = stored[0][7], stored[0][10]
            gs, low, t, sums, tot1 = call(
                functools.partial(cross_kernel, dims, lines), steps,
                [smem(), smem(), thin, thin, full(two), full(vec), broad, broad, thin,
                 full(vec_wide), full((wide, width)), full((width, wide))],
                [broad, thin, full((width, wide)), full(many), full((1, 2 * width))],
                [wide_shape, narrow(BF16), flat(width, wide), struct(many, BF16),
                 flat(1, 2 * width)],
                [pltpu.VMEM((lines * line, width), BF16), pltpu.VMEM((2, lines * line, 256), F32), pltpu.VMEM((wide, width), BF16),
                 pltpu.VMEM((width, wide), BF16), pltpu.VMEM(vec, F32),
                 pltpu.VMEM((8, wide), F32)], 15,
            )(scal, nf, go1, z1, got, vec1, gs, slope, h2_0, vec3_0, w1[1], w3[0])
            reduce_mine, reduce_sent = call(
                functools.partial(reduce_grad_kernel, dims, many_lines, 2.0), few,
                [smem(), smem(), big_thin, big_thin, full((1, 2 * width)), full(vec), big_broad], [full(owned.shape), full(owned.shape)], [owned, owned],
                [pltpu.VMEM((many_lines * line, width), BF16), pltpu.VMEM(vec, F32),
                 pltpu.VMEM((width, wide), F32)], 5,
            )(scal, nf, go1, z1, tot1, vec1, carried)
        else:
            gr, mine, sent, tot1 = call(
                functools.partial(last_grad_kernel, dims, many_lines), few,
                [smem(), smem(), big_thin, big_thin, full(two), full(vec), big_native],
                [big_thin, full(owned.shape), full(owned.shape), full((1, 2 * width))],
                [narrow(BF16), owned, owned, flat(1, 2 * width)],
                [pltpu.VMEM(vec, F32), pltpu.VMEM((width, wide), F32)], 6,
            )(scal, nf, go1, z1, got, vec1, x)
            input_grad = call(
                input_kernel, few, [big_thin, big_broad, full((peers, r1, width))], big_native,
                native_shape, [], 6,
            )(gr, gs, early)
        results[layer] = (tot1, tot2, tot3)

    last = sum_cores((mine, sent), (taps_mine, taps_sent))
    last = jnp.sum(lax.all_to_all(last, CHIPS, 0, 0).astype(F32), axis=0)
    first = jnp.sum(first.astype(F32), axis=0)
    second = jnp.sum(second.astype(F32), axis=0)
    to_wide = lambda one: one.reshape(blocks, r2, width).transpose(1, 0, 2).reshape(r2, wide)
    grad_reduce = jnp.stack([last[0:r1], second[0:r1]])
    grad_mix = jnp.stack([last[r1 : r1 + r2], first[0:r2]])
    depths = (last[r1 + r2 : r1 + r2 + r4], first[r2 : r2 + r4])
    grad_depth = jnp.stack([one[:, 0:27].T for one in depths])
    grad_expand = jnp.stack([to_wide(second[r1:]), to_wide(first[r2 + r4 :])])

    mid_sums = jnp.concatenate(
        [
            jnp.concatenate([results[layer][0], results[layer][1]], axis=0).reshape(2, 2, width)
            for layer in range(2)
        ],
        axis=0,
    )
    mid = lax.dynamic_slice_in_dim(mid_sums, place * r4, r4, axis=2)
    out_sums = jnp.concatenate([results[layer][2].reshape(1, 2, wide) for layer in range(2)])
    r6 = gains_out.shape[1]
    outs = lax.dynamic_slice_in_dim(out_sums, place * r6, r6, axis=2)

    return (
        voxel_form(output),
        voxel_form(input_grad),
        grad_reduce,
        grad_mix,
        grad_expand,
        grad_depth,
        mid[:, 1].reshape(2, 2, r4),
        mid[:, 0].reshape(2, 2, r4),
        outs[:, 1],
        outs[:, 0],
    )


def solution(mesh):
    clip_size, sp_size = mesh.shape["clip"], mesh.shape["sp"]
    inner = 2 if sp_size % 2 == 0 else 1
    divided = Mesh(mesh.devices.reshape(clip_size, sp_size // inner, inner), ALL)
    activations = P("clip", None, SP, None, None)
    middle, last, vectors = P(None, ALL, None), P(None, None, ALL), P(None, ALL)
    return jax.shard_map(
        on_device,
        mesh=divided,
        in_specs=(
            activations, P(), activations, middle, middle, middle, last, last, last, vectors,
            vectors,
        ),
        out_specs=(
            activations, activations, middle, middle, middle, last, last, last, vectors, vectors,
        ),
        check_vma=False,
    )
```
